32 devices in a mesh: groups: 2 (over x), ctx: 16 (over z, y, core).
Axes of the slice: x: 2, y: 2, z: 4, core: 2. Of those that a mesh axis runs over, the one named last changes fastest.
Arguments:
- queries: bfloat16 [4096, 8192], P(('groups', 'ctx')), parts along dimension 0, may hold values from -8 to 8
- new_keys: bfloat16 [4096, 1024], P(('groups', 'ctx')), parts along dimension 0, may hold values from -12 to 12
- new_values: bfloat16 [4096, 1024], P(('groups', 'ctx')), parts along dimension 0, may hold values from -6 to 6
- prefix_keys: bfloat16 [256, 1024], P(('groups', 'ctx')), parts along dimension 0, may hold values from -16 to 16
- prefix_values: bfloat16 [256, 1024], P(('groups', 'ctx')), parts along dimension 0, may hold values from -6 to 6
- pool_keys: bfloat16 [32, 2, 256, 1024], P(('groups', 'ctx')), parts along dimension 0, may hold values from -12 to 12
- pool_values: bfloat16 [32, 2, 256, 1024], P(('groups', 'ctx')), parts along dimension 0, may hold values from -6 to 6
- owners: int32 [4], P('groups'), parts along dimension 0, may hold values from 0 to 15
- lengths: int32 [32], P(('groups', 'ctx')), parts along dimension 0, may hold values from 1 to 128, as said below
Outputs:
- attended: bfloat16 [4096, 8192], P(('groups', 'ctx')), parts along dimension 0
The draws below stay inside these ranges and needn't reach their ends.
There are 2 independent parts, one for each index of `groups`. The reference program is written for one: setup_inputs(seed, part) draws one part's arguments, and reference() takes and returns one part's arrays. A program takes and returns all parts, laid end to end along the dimension named above; each array names one. Nothing has to cross between parts.
Inputs may be any that keep to these rules, and one draw needn't show every extreme that they name: `lengths`: some device's prompt fills all 128 slots.
All inputs are finite; a program needn't handle non-finite values.
Results may differ from the reference program's by a relative error of at most 0.0035.
Values may be sent and summed in bfloat16 or wider, within the bound.
No kernel may reach another device: no remote copies, remote signals or barrier semaphores. Data moves between devices by JAX's collectives and lax.ppermute only.
A program may use at most 128 MiB of HBM per device.

```python
import jax
import jax.numpy as jnp
from jax import lax

H = 64
KVH = 8
HD = 128
Q_DEV = 128
SB = 2
BLK = 256
PREFIX = 128
TOKENS = 2048
N_CTX = 16


def draw_queries(key, part):
    noise_key = jax.random.fold_in(key, 11)
    values_drawn = jnp.clip(1.5 * jax.random.normal(noise_key, (TOKENS, H * HD), jnp.float32), -8.0, 8.0)
    return values_drawn.astype(jnp.bfloat16)


def draw_prefix_keys(key, part):
    noise_key = jax.random.fold_in(key, 13)
    values_drawn = jnp.clip(2.0 * jax.random.normal(noise_key, (PREFIX, KVH * HD), jnp.float32), -16.0, 16.0)
    return values_drawn.astype(jnp.bfloat16)


def draw_lengths(key, part):
    key_values, key_full = jax.random.split(jax.random.fold_in(key, 23))
    count = TOKENS // Q_DEV
    drawn = jax.random.randint(key_values, (count,), 1, Q_DEV + 1)
    full_index = jax.random.randint(key_full, (), 0, count)
    return drawn.at[full_index].set(Q_DEV).astype(jnp.int32)


def levels(rng, dims, shards, smallest, top_value):
    def one(dim, parts):
        steps = jax.random.uniform(jax.random.fold_in(jax.random.fold_in(rng, 6), dim), (parts,), jnp.float32, smallest / len(shards), top_value / len(shards))
        return jnp.repeat(jnp.exp(steps), dims[dim] // parts).reshape((-1,) + (1,) * (len(dims) - dim - 1))

    gain = one(*shards[0])
    for cut in shards[1:]:
        gain = gain * one(*cut)
    return gain


def centred(own_key, shape, spread, most, cuts=(), kind=jnp.bfloat16):
    entries = spread * jax.random.normal(own_key, shape, jnp.float32)
    if cuts:
        entries = entries * levels(own_key, shape, cuts, -0.22, 0.18)
    return jnp.clip(entries, -most, most).astype(kind)


def setup_inputs(seed: int = 0, part: int = 0) -> dict:
    seeds = jax.random.split(jax.random.key(seed), 10)
    part_splits = jax.random.split(jax.random.fold_in(seeds[9], part), 10)
    return {
        "queries": draw_queries(jax.random.fold_in(jax.random.fold_in(seeds[9], part), 71), part),
        "new_keys": centred(part_splits[1], (TOKENS, KVH * HD), 2.0, 12.0, ((0, 16),)),
        "new_values": centred(part_splits[2], (TOKENS, KVH * HD), 1.0, 6.0, ((0, 16),)),
        "prefix_keys": draw_prefix_keys(jax.random.fold_in(jax.random.fold_in(seeds[9], part), 71), part),
        "prefix_values": centred(part_splits[4], (PREFIX, KVH * HD), 1.0, 6.0, ((0, 16),)),
        "pool_keys": centred(part_splits[5], (N_CTX, SB, BLK, KVH * HD), 2.0, 12.0, ((0, 16),)),
        "pool_values": centred(part_splits[6], (N_CTX, SB, BLK, KVH * HD), 1.0, 6.0, ((0, 16),)),
        "owners": jax.random.randint(part_splits[7], (SB,), 0, N_CTX).astype(jnp.int32),
        "lengths": draw_lengths(jax.random.fold_in(jax.random.fold_in(seeds[9], part), 71), part),
    }


def reference(queries, new_keys, new_values, prefix_keys, prefix_values, pool_keys, pool_values, owners, lengths):
    group_size = H // KVH
    score_scale = 1.0 / (HD ** 0.5)
    block_ids = jnp.arange(SB).astype(jnp.int32)
    shared_keys = pool_keys[owners.astype(jnp.int32), block_ids].reshape(SB * BLK, KVH * HD)
    shared_values = pool_values[owners.astype(jnp.int32), block_ids].reshape(SB * BLK, KVH * HD)

    def one_block(device):
        start = (device * Q_DEV).astype(jnp.int32)
        query_rows = lax.dynamic_slice_in_dim(queries, start, Q_DEV, 0)
        own_keys = lax.dynamic_slice_in_dim(new_keys, start, Q_DEV, 0)
        own_values = lax.dynamic_slice_in_dim(new_values, start, Q_DEV, 0)
        length = lengths[device]
        key_rows = jnp.concatenate([shared_keys, prefix_keys, own_keys], axis=0)
        value_rows = jnp.concatenate([shared_values, prefix_values, own_values], axis=0)
        positions = jnp.arange(Q_DEV).astype(jnp.int32)
        own_visible = (positions[None, :] <= positions[:, None]) & (positions[None, :] < length)
        visible = jnp.concatenate([jnp.ones((Q_DEV, SB * BLK + PREFIX), dtype=bool), own_visible], axis=1)
        visible = jnp.repeat(visible, group_size, axis=0)
        pieces = []
        for kv_head in range(KVH):
            head_queries = query_rows[:, kv_head * group_size * HD:(kv_head + 1) * group_size * HD].reshape(Q_DEV * group_size, HD)
            head_keys = key_rows[:, kv_head * HD:(kv_head + 1) * HD]
            head_values = value_rows[:, kv_head * HD:(kv_head + 1) * HD]
            scores = lax.dot_general(head_queries, head_keys, (((1,), (1,)), ((), ())), preferred_element_type=jnp.float32) * score_scale
            scores = jnp.where(visible, scores, -1e30)
            row_max = jnp.max(scores, axis=1, keepdims=True)
            weights = jnp.where(visible, jnp.exp(scores - row_max), 0.0)
            totals = jnp.sum(weights, axis=1, keepdims=True)
            summed = jnp.dot(weights.astype(jnp.bfloat16), head_values, preferred_element_type=jnp.float32)
            pieces.append((summed / totals).reshape(Q_DEV, group_size * HD))
        joined = jnp.concatenate(pieces, axis=1)
        live = positions < length
        return jnp.where(live[:, None], joined, 0.0).astype(jnp.bfloat16)

    blocks = lax.map(one_block, jnp.arange(TOKENS // Q_DEV).astype(jnp.int32))
    return blocks.reshape(TOKENS, H * HD)
```

```python
import functools

import jax
import jax.numpy as jnp
from jax import lax
from jax.experimental import pallas as pl
from jax.experimental.pallas import tpu as pltpu
from jax.sharding import PartitionSpec as P

HD = 128
CORES = 2
COLUMNS = 2
LOG2_E = 1.4426950408889634
NT = (((1,), (1,)), ((), ()))
TN = (((0,), (0,)), ((), ()))
VMEM_LIMIT = 48 * 1024 * 1024


def stacked_heads(queries_ref):
    group = queries_ref.shape[1] // HD
    return jnp.concatenate([queries_ref[:, g * HD : (g + 1) * HD] for g in range(group)], axis=0)


def first_kernel(scale, length_ref, queries_ref, own_k_ref, own_v_ref, pre_k_ref, pre_v_ref, acc_ref, max_ref, sum_ref):
    rows = queries_ref.shape[0]
    group = queries_ref.shape[1] // HD
    heads = stacked_heads(queries_ref)
    own = lax.dot_general(own_k_ref[...], heads, NT, preferred_element_type=jnp.float32)
    pre = lax.dot_general(pre_k_ref[...], heads, NT, preferred_element_type=jnp.float32)
    key_at = lax.broadcasted_iota(jnp.int32, (rows, rows), 0)
    query_at = lax.broadcasted_iota(jnp.int32, (rows, rows), 1)
    seen = (key_at <= query_at) & (key_at < length_ref[0])
    own = jnp.where(jnp.concatenate([seen] * group, axis=1), own, -1e30)
    top = jnp.maximum(jnp.max(own, axis=0, keepdims=True), jnp.max(pre, axis=0, keepdims=True))
    own = jnp.exp2((own - top) * scale)
    pre = jnp.exp2((pre - top) * scale)
    max_ref[0] = top
    sum_ref[0] = jnp.sum(own, axis=0, keepdims=True) + jnp.sum(pre, axis=0, keepdims=True)
    acc_ref[0] = lax.dot_general(
        own_v_ref[...], own.astype(jnp.bfloat16), TN, preferred_element_type=jnp.float32
    ) + lax.dot_general(pre_v_ref[...], pre.astype(jnp.bfloat16), TN, preferred_element_type=jnp.float32)


def second_kernel(scale, pieces, length_ref, queries_ref, acc_ref, max_ref, sum_ref, *rest):
    piece_refs, out_ref = rest[:pieces], rest[pieces]
    rows = queries_ref.shape[0]
    group = queries_ref.shape[1] // HD
    half = piece_refs[0].shape[0] // 2
    heads = stacked_heads(queries_ref)
    keys = jnp.concatenate([ref[:half] for ref in piece_refs], axis=0)
    values = jnp.concatenate([ref[half:] for ref in piece_refs], axis=0)
    scores = lax.dot_general(keys, heads, NT, preferred_element_type=jnp.float32)
    top = jnp.maximum(max_ref[0], jnp.max(scores, axis=0, keepdims=True))
    weights = jnp.exp2((scores - top) * scale)
    shrink = jnp.exp2((max_ref[0] - top) * scale)
    total = sum_ref[0] * shrink + jnp.sum(weights, axis=0, keepdims=True)
    summed = acc_ref[0] * shrink + lax.dot_general(
        values, weights.astype(jnp.bfloat16), TN, preferred_element_type=jnp.float32
    )
    live = lax.broadcasted_iota(jnp.int32, (rows, HD), 0) < length_ref[0]
    summed = summed / total
    for g in range(group):
        turned = summed[:, g * rows : (g + 1) * rows].T
        out_ref[:, g * HD : (g + 1) * HD] = jnp.where(live, turned, 0.0).astype(jnp.bfloat16)


def attend_first(queries, own_k, own_v, pre_k, pre_v, lengths, kv_heads):
    rows = queries.shape[0]
    width = queries.shape[1] // kv_heads
    packed = rows * width // HD
    keys = own_k.shape[0] + pre_k.shape[0]
    column = lambda h: (0, h)
    state = lambda h: (h, 0, 0)
    return pl.pallas_call(
        functools.partial(first_kernel, LOG2_E / HD**0.5),
        grid=(kv_heads,),
        in_specs=[
            pl.BlockSpec(memory_space=pltpu.SMEM),
            pl.BlockSpec((rows, width), column),
            pl.BlockSpec((own_k.shape[0], HD), column),
            pl.BlockSpec((own_k.shape[0], HD), column),
            pl.BlockSpec((pre_k.shape[0], HD), column),
            pl.BlockSpec((pre_k.shape[0], HD), column),
        ],
        out_specs=[
            pl.BlockSpec((1, HD, packed), state),
            pl.BlockSpec((1, 1, packed), state),
            pl.BlockSpec((1, 1, packed), state),
        ],
        out_shape=[
            jax.ShapeDtypeStruct((kv_heads, HD, packed), jnp.float32),
            jax.ShapeDtypeStruct((kv_heads, 1, packed), jnp.float32),
            jax.ShapeDtypeStruct((kv_heads, 1, packed), jnp.float32),
        ],
        compiler_params=pltpu.CompilerParams(vmem_limit_bytes=VMEM_LIMIT),
        cost_estimate=pl.CostEstimate(
            flops=4 * keys * packed * HD * kv_heads,
            bytes_accessed=queries.size * 6,
            transcendentals=keys * packed * kv_heads,
        ),
        name="own_and_prefix",
    )(lengths, queries, own_k, own_v, pre_k, pre_v)


def attend_second(queries, state, pieces, lengths, kv_heads):
    rows = queries.shape[0]
    width = queries.shape[1] // kv_heads
    packed = rows * width // HD
    keys = sum(piece.shape[0] for piece in pieces) // 2
    column = lambda h: (0, h)
    stacked = lambda h: (h, 0, 0)
    return pl.pallas_call(
        functools.partial(second_kernel, LOG2_E / HD**0.5, len(pieces)),
        grid=(kv_heads,),
        in_specs=[
            pl.BlockSpec(memory_space=pltpu.SMEM),
            pl.BlockSpec((rows, width), column),
            pl.BlockSpec((1, HD, packed), stacked),
            pl.BlockSpec((1, 1, packed), stacked),
            pl.BlockSpec((1, 1, packed), stacked),
        ]
        + [pl.BlockSpec((piece.shape[0], HD), column) for piece in pieces],
        out_specs=pl.BlockSpec((rows, width), column),
        out_shape=jax.ShapeDtypeStruct(queries.shape, queries.dtype),
        compiler_params=pltpu.CompilerParams(vmem_limit_bytes=VMEM_LIMIT),
        cost_estimate=pl.CostEstimate(
            flops=4 * keys * packed * HD * kv_heads,
            bytes_accessed=queries.size * 8,
            transcendentals=keys * packed * kv_heads,
        ),
        name="shared_and_merge",
    )(lengths, queries, *state, *pieces)


class Places:
    def __init__(self, devices):
        self.devices = devices
        self.levels = devices // (CORES * COLUMNS)

    def split(self, index):
        return index // (CORES * COLUMNS), index // CORES % COLUMNS, index % CORES

    def moved(self, array, level=0, column=0, core=0):
        pairs = []
        for index in range(self.devices):
            z, y, c = self.split(index)
            z, y, c = (z + level) % self.levels, (y + column) % COLUMNS, (c + core) % CORES
            pairs.append((index, (z * COLUMNS + y) * CORES + c))
        return lax.ppermute(array, "ctx", pairs)


def gathered(places, piece):
    levels = [piece] + [places.moved(piece, level=s) for s in range(1, places.levels)]
    chips = levels + [places.moved(one, column=1) for one in levels]
    return chips + [places.moved(one, core=1) for one in chips]


def spread(places, pool_keys, pool_values, owners):
    me = lax.axis_index("ctx")
    z, y, c = places.split(me)
    owner_z, owner_y, owner_c = places.split(owners[c])
    pages = [lax.dynamic_index_in_dim(pool[0], c, 0, False) for pool in (pool_keys, pool_values)]
    others = [lax.dynamic_index_in_dim(pool[0], 1 - c, 0, False) for pool in (pool_keys, pool_values)]
    swapped = [places.moved(other, core=1) for other in others]
    pages = [jnp.where(owner_c == c, page, got) for page, got in zip(pages, swapped)]
    part = pages[0].shape[0] // COLUMNS
    cut = lambda at: jnp.concatenate([lax.dynamic_slice_in_dim(page, at * part, part, 0) for page in pages])
    got = places.moved(cut(1 - y), column=1)
    halves = jnp.where(owner_y == y, cut(y), got).reshape(2, part, -1)
    rows = part // places.levels
    cut = lambda at: lax.dynamic_slice_in_dim(halves, at * rows, rows, 1).reshape(2 * rows, -1)
    piece = cut(z)
    steps = (z - owner_z) % places.levels
    for s in range(1, places.levels):
        got = places.moved(cut((z + s) % places.levels), level=s)
        piece = jnp.where(steps == s, got, piece)
    return piece


def owned_rows(pool, owners):
    owned = (owners == lax.axis_index("ctx"))[:, None, None]
    return lax.psum(jnp.where(owned, pool[0], 0), "ctx").reshape(-1, pool.shape[-1])


def body(queries, new_keys, new_values, prefix_keys, prefix_values, pool_keys, pool_values, owners, lengths, devices):
    kv_heads = new_keys.shape[1] // HD
    blocks, block_rows = pool_keys.shape[1:3]
    chips = devices // CORES
    by_permutes = blocks == CORES and devices % (CORES * COLUMNS) == 0 and block_rows % (16 * chips) == 0
    if by_permutes:
        places = Places(devices)
        prefix = jnp.stack(gathered(places, jnp.concatenate([prefix_keys, prefix_values])))
        prefix = prefix.reshape(devices, 2, -1, prefix.shape[-1])
        pre_k, pre_v = (prefix[:, i].reshape(-1, prefix.shape[-1]) for i in range(2))
        pieces = gathered(places, spread(places, pool_keys, pool_values, owners))
    else:
        pre_k, pre_v = (lax.all_gather(rows, "ctx", axis=0, tiled=True) for rows in (prefix_keys, prefix_values))
        pieces = [jnp.concatenate([owned_rows(pool_keys, owners), owned_rows(pool_values, owners)])]
    state = attend_first(queries, new_keys, new_values, pre_k, pre_v, lengths, kv_heads)
    return attend_second(queries, state, pieces, lengths, kv_heads)


def solution(mesh):
    both = ("groups", "ctx")
    placed = (P(both, None),) * 5 + (P(both, None, None, None),) * 2 + (P("groups"), P(both))
    return jax.shard_map(
        functools.partial(body, devices=mesh.shape["ctx"]),
        mesh=mesh,
        in_specs=placed,
        out_specs=P(both, None),
        check_vma=False,
    )
```

```python
import functools

import jax
import jax.numpy as jnp
from jax import lax
from jax.experimental import pallas as pl
from jax.experimental.pallas import tpu as pltpu
from jax.sharding import PartitionSpec as P

HD = 128
CORES = 2
COLUMNS = 2
TOGETHER = 2
LOG2_E = 1.4426950408889634
NT = (((1,), (1,)), ((), ()))
TN = (((0,), (0,)), ((), ()))
VMEM_LIMIT = 40 * 1024 * 1024


def attend_kernel(scale, halves, length_ref, queries_ref, own_k_ref, own_v_ref, pre_k_ref, pre_v_ref, *rest):
    piece_refs, out_ref = rest[: len(halves)], rest[-1]
    rows = queries_ref.shape[0]
    group = queries_ref.shape[1] // HD
    shared = [ref[...].reshape(-1, 2, half, HD) for ref, half in zip(piece_refs, halves)]
    keys = jnp.concatenate([own_k_ref[...], pre_k_ref[...]] + [one[:, 0].reshape(-1, HD) for one in shared], axis=0)
    values = jnp.concatenate([own_v_ref[...], pre_v_ref[...]] + [one[:, 1].reshape(-1, HD) for one in shared], axis=0)
    length = length_ref[0]
    key_at = lax.broadcasted_iota(jnp.int32, (rows, rows), 0)
    query_at = lax.broadcasted_iota(jnp.int32, (rows, rows), 1)
    seen = (key_at <= query_at) & (key_at < length)
    seen = jnp.concatenate([seen] * TOGETHER, axis=1)
    live = lax.broadcasted_iota(jnp.int32, (rows, HD), 0) < length
    for first in range(0, group, TOGETHER):
        heads = range(first, first + TOGETHER)
        asked = jnp.concatenate([queries_ref[:, g * HD : (g + 1) * HD] for g in heads], axis=0)
        scores = lax.dot_general(keys, asked, NT, preferred_element_type=jnp.float32)
        scores = jnp.concatenate([jnp.where(seen, scores[:rows], -1e30), scores[rows:]], axis=0)
        top = jnp.max(scores, axis=0, keepdims=True)
        weights = jnp.exp2((scores - top) * scale)
        total = jnp.sum(weights, axis=0, keepdims=True)
        summed = lax.dot_general(values, weights.astype(jnp.bfloat16), TN, preferred_element_type=jnp.float32)
        summed = summed / total
        for at, g in enumerate(heads):
            turned = summed[:, at * rows : (at + 1) * rows].T
            out_ref[:, g * HD : (g + 1) * HD] = jnp.where(live, turned, 0.0).astype(jnp.bfloat16)


def attend(queries, own_k, own_v, pre_k, pre_v, pieces, lengths, heads, kv_heads, begun):
    rows = queries.shape[0]
    width = queries.shape[1] // kv_heads
    first, count = heads
    halves = [half for _, half in pieces]
    arrays = [array for array, _ in pieces]
    keys = own_k.shape[0] + pre_k.shape[0] + sum(array.shape[0] for array in arrays) // 2
    column = lambda h: (0, h + first)
    local = lambda h: (0, h)
    in_specs = (
        [pl.BlockSpec(memory_space=pltpu.SMEM), pl.BlockSpec((rows, width), column)]
        + [pl.BlockSpec((array.shape[0], HD), column) for array in (own_k, own_v, pre_k, pre_v)]
        + [pl.BlockSpec((array.shape[0], HD), local) for array in arrays]
    )
    operands = [lengths, queries, own_k, own_v, pre_k, pre_v] + arrays
    aliases = {}
    if begun is not None:
        aliases = {len(operands): 0}
        operands.append(begun)
        in_specs.append(pl.BlockSpec(memory_space=pl.ANY))
    return pl.pallas_call(
        functools.partial(attend_kernel, LOG2_E / HD**0.5, halves),
        grid=(count,),
        in_specs=in_specs,
        out_specs=pl.BlockSpec((rows, width), column),
        out_shape=jax.ShapeDtypeStruct(queries.shape, queries.dtype),
        input_output_aliases=aliases,
        compiler_params=pltpu.CompilerParams(vmem_limit_bytes=VMEM_LIMIT),
        cost_estimate=pl.CostEstimate(
            flops=4 * keys * rows * width * count,
            bytes_accessed=4 * rows * width * count,
            transcendentals=keys * rows * width // HD * count,
        ),
        name="attend_heads",
    )(*operands)


class Places:
    def __init__(self, devices):
        self.devices = devices
        self.levels = devices // (CORES * COLUMNS)

    def split(self, index):
        return index // (CORES * COLUMNS), index // CORES % COLUMNS, index % CORES

    def swapped(self, array, level=0, column=0, core=0):
        pairs = []
        for index in range(self.devices):
            z, y, c = self.split(index)
            z, y, c = z ^ level, y ^ column, c ^ core
            pairs.append((index, (z * COLUMNS + y) * CORES + c))
        return lax.ppermute(array, "ctx", pairs)

    def over_levels(self, array):
        return [array] + [self.swapped(array, level=s) for s in range(1, self.levels)]


def gathered(places, piece):
    rows = jnp.concatenate(places.over_levels(piece))
    chips = [rows, places.swapped(rows, column=1)]
    return chips + [places.swapped(one, core=1) for one in chips]


def cut_rows(array, start, size):
    return lax.dynamic_slice_in_dim(array, start, size, 0)


def spread(places, pages, owner):
    z, y, _ = places.split(lax.axis_index("ctx"))
    owner_z, owner_y, _ = places.split(owner)
    part = pages[0].shape[0] // COLUMNS
    cut = lambda at: jnp.concatenate([cut_rows(page, at * part, part) for page in pages])
    got = places.swapped(cut(1 - y), column=1)
    halves = jnp.where(owner_y == y, cut(y), got).reshape(2, part, -1)
    rows = part // places.levels
    cut = lambda at: lax.dynamic_slice_in_dim(halves, at * rows, rows, 1).reshape(2 * rows, -1)
    piece = cut(z)
    for s in range(1, places.levels):
        piece = jnp.where(z ^ owner_z == s, places.swapped(cut(z ^ s), level=s), piece)
    return piece


def owned_rows(pool, owners):
    owned = (owners == lax.axis_index("ctx"))[:, None, None]
    return lax.psum(jnp.where(owned, pool[0], 0), "ctx").reshape(-1, pool.shape[-1])


def body(queries, new_keys, new_values, prefix_keys, prefix_values, pool_keys, pool_values, owners, lengths, devices):
    kv_heads = new_keys.shape[1] // HD
    blocks, block_rows = pool_keys.shape[1:3]
    chips = devices // CORES
    levels = chips // COLUMNS
    by_permutes = (
        blocks == CORES
        and chips % COLUMNS == 0
        and levels & (levels - 1) == 0
        and block_rows % (16 * chips) == 0
        and kv_heads % 2 == 0
    )
    if not by_permutes:
        pre_k, pre_v = (lax.all_gather(rows, "ctx", axis=0, tiled=True) for rows in (prefix_keys, prefix_values))
        shared = jnp.concatenate([owned_rows(pool_keys, owners), owned_rows(pool_values, owners)])
        pieces = [(shared, shared.shape[0] // 2)]
        return attend(queries, new_keys, new_values, pre_k, pre_v, pieces, lengths, (0, kv_heads), kv_heads, None)
    places = Places(devices)
    c = lax.axis_index("ctx") % CORES
    owner = owners[c]
    pages = []
    for pool in (pool_keys[0], pool_values[0]):
        page, got = (lax.dynamic_index_in_dim(at, c, 0, False) for at in (pool, places.swapped(pool, core=1)))
        pages.append(jnp.where(owner % CORES == c, page, got))
    prefix = jnp.concatenate(gathered(places, jnp.concatenate([prefix_keys, prefix_values])))
    prefix = prefix.reshape(devices, 2, -1, prefix.shape[-1])
    pre_k, pre_v = (prefix[:, i].reshape(-1, prefix.shape[-1]) for i in range(2))
    out = None
    count = kv_heads // 2
    for first in range(0, kv_heads, count):
        columns = slice(first * HD, (first + count) * HD)
        piece = spread(places, [page[:, columns] for page in pages], owner)
        pieces = [(array, piece.shape[0] // 2) for array in gathered(places, piece)]
        out = attend(
            queries, new_keys, new_values, pre_k, pre_v, pieces, lengths, (first, count), kv_heads, out
        )
    return out


def solution(mesh):
    both = ("groups", "ctx")
    placed = (P(both, None),) * 5 + (P(both, None, None, None),) * 2 + (P("groups"), P(both))
    return jax.shard_map(
        functools.partial(body, devices=mesh.shape["ctx"]),
        mesh=mesh,
        in_specs=placed,
        out_specs=P(both, None),
        check_vma=False,
    )
```

```python
import functools

import jax
import jax.numpy as jnp
from jax import lax
from jax.experimental import pallas as pl
from jax.experimental.pallas import tpu as pltpu
from jax.sharding import PartitionSpec as P

HD = 128
CORES = 2
COLUMNS = 2
TOGETHER = 2
LOG2_E = 1.4426950408889634
NT = (((1,), (1,)), ((), ()))
VMEM_LIMIT = 40 * 1024 * 1024


def attend_kernel(scale, halves, length_ref, queries_ref, own_k_ref, own_v_ref, pre_k_ref, pre_v_ref, *rest):
    piece_refs, out_ref = rest[: len(halves)], rest[-1]
    rows = queries_ref.shape[0]
    group = queries_ref.shape[1] // HD
    shared = [ref[...].reshape(-1, 2, half, HD) for ref, half in zip(piece_refs, halves)]
    keys = jnp.concatenate([own_k_ref[...], pre_k_ref[...]] + [one[:, 0].reshape(-1, HD) for one in shared], axis=0)
    values = jnp.concatenate([own_v_ref[...], pre_v_ref[...]] + [one[:, 1].reshape(-1, HD) for one in shared], axis=0)
    values = jnp.concatenate([values, jnp.ones_like(values)], axis=1)
    length = length_ref[...]
    query_at = lax.broadcasted_iota(jnp.int32, (rows, rows), 0)
    key_at = lax.broadcasted_iota(jnp.int32, (rows, rows), 1)
    seen = (key_at <= query_at) & (key_at < length)
    seen = jnp.concatenate([seen] * TOGETHER, axis=0)
    live = lax.broadcasted_iota(jnp.int32, (rows, HD), 0) < length
    for first in range(0, group, TOGETHER):
        heads = range(first, first + TOGETHER)
        asked = jnp.concatenate([queries_ref[:, g * HD : (g + 1) * HD] for g in heads], axis=0)
        scores = lax.dot_general(asked, keys, NT, preferred_element_type=jnp.float32)
        scores = jnp.concatenate([jnp.where(seen, scores[:, :rows], -1e30), scores[:, rows:]], axis=1)
        top = jnp.max(scores, axis=1, keepdims=True)
        weights = jnp.exp2((scores - top) * scale)
        summed = jnp.dot(weights.astype(jnp.bfloat16), values, preferred_element_type=jnp.float32)
        summed = summed[:, :HD] / summed[:, HD:]
        for at, g in enumerate(heads):
            kept = jnp.where(live, summed[at * rows : (at + 1) * rows], 0.0)
            out_ref[:, g * HD : (g + 1) * HD] = kept.astype(jnp.bfloat16)


def attend(queries, own_k, own_v, pre_k, pre_v, pieces, lengths, heads, kv_heads, begun):
    rows = queries.shape[0]
    width = queries.shape[1] // kv_heads
    first, count = heads
    halves = [half for _, half in pieces]
    arrays = [array for array, _ in pieces]
    keys = own_k.shape[0] + pre_k.shape[0] + sum(array.shape[0] for array in arrays) // 2
    column = lambda h: (0, h + first)
    local = lambda h: (0, h)
    in_specs = (
        [pl.BlockSpec((1, HD), lambda h: (0, 0)), pl.BlockSpec((rows, width), column)]
        + [pl.BlockSpec((array.shape[0], HD), column) for array in (own_k, own_v, pre_k, pre_v)]
        + [pl.BlockSpec((array.shape[0], HD), local) for array in arrays]
    )
    length = jnp.broadcast_to(lengths[:, None], (1, HD))
    operands = [length, queries, own_k, own_v, pre_k, pre_v] + arrays
    aliases = {}
    if begun is not None:
        aliases = {len(operands): 0}
        operands.append(begun)
        in_specs.append(pl.BlockSpec(memory_space=pl.ANY))
    return pl.pallas_call(
        functools.partial(attend_kernel, LOG2_E / HD**0.5, halves),
        grid=(count,),
        in_specs=in_specs,
        out_specs=pl.BlockSpec((rows, width), column),
        out_shape=jax.ShapeDtypeStruct(queries.shape, queries.dtype),
        input_output_aliases=aliases,
        compiler_params=pltpu.CompilerParams(vmem_limit_bytes=VMEM_LIMIT),
        cost_estimate=pl.CostEstimate(
            flops=4 * keys * rows * width * count,
            bytes_accessed=4 * rows * width * count,
            transcendentals=keys * rows * width // HD * count,
        ),
        name="attend_heads",
    )(*operands)


class Places:
    def __init__(self, devices):
        self.devices = devices
        self.levels = devices // (CORES * COLUMNS)

    def split(self, index):
        return index // (CORES * COLUMNS), index // CORES % COLUMNS, index % CORES

    def swapped(self, array, level=0, column=0, core=0):
        pairs = []
        for index in range(self.devices):
            z, y, c = self.split(index)
            z, y, c = z ^ level, y ^ column, c ^ core
            pairs.append((index, (z * COLUMNS + y) * CORES + c))
        return lax.ppermute(array, "ctx", pairs)

    def over_levels(self, array):
        return [array] + [self.swapped(array, level=s) for s in range(1, self.levels)]


def over_chips(places, rows):
    chips = [rows, places.swapped(rows, column=1)]
    return chips + [places.swapped(one, core=1) for one in chips]


def cut_rows(array, start, size):
    return lax.dynamic_slice_in_dim(array, start, size, 0)


def over_columns(places, pages, owner):
    _, y, _ = places.split(lax.axis_index("ctx"))
    _, owner_y, _ = places.split(owner)
    part = pages[0].shape[0] // COLUMNS
    cut = lambda at: jnp.concatenate([cut_rows(page, at * part, part) for page in pages])
    got = places.swapped(cut(1 - y), column=1)
    return jnp.where(owner_y == y, cut(y), got).reshape(2, part, -1)


def scattered(places, part, owner):
    z, _, _ = places.split(lax.axis_index("ctx"))
    owner_z, _, _ = places.split(owner)
    rows = part.shape[1] // places.levels
    cut = lambda at: lax.dynamic_slice_in_dim(part, at * rows, rows, 1).reshape(2 * rows, -1)
    piece = cut(z)
    for s in range(1, places.levels):
        piece = jnp.where(z ^ owner_z == s, places.swapped(cut(z ^ s), level=s), piece)
    return piece


def owned_rows(pool, owners):
    owned = (owners == lax.axis_index("ctx"))[:, None, None]
    return lax.psum(jnp.where(owned, pool[0], 0), "ctx").reshape(-1, pool.shape[-1])


def body(queries, new_keys, new_values, prefix_keys, prefix_values, pool_keys, pool_values, owners, lengths, devices):
    kv_heads = new_keys.shape[1] // HD
    blocks, block_rows = pool_keys.shape[1:3]
    chips = devices // CORES
    levels = chips // COLUMNS
    by_permutes = (
        blocks == CORES
        and chips % COLUMNS == 0
        and levels & (levels - 1) == 0
        and block_rows % (16 * chips) == 0
        and kv_heads % 2 == 0
    )
    if not by_permutes:
        pre_k, pre_v = (lax.all_gather(rows, "ctx", axis=0, tiled=True) for rows in (prefix_keys, prefix_values))
        shared = jnp.concatenate([owned_rows(pool_keys, owners), owned_rows(pool_values, owners)])
        pieces = [(shared, shared.shape[0] // 2)]
        return attend(queries, new_keys, new_values, pre_k, pre_v, pieces, lengths, (0, kv_heads), kv_heads, None)
    places = Places(devices)
    c = lax.axis_index("ctx") % CORES
    owner = owners[c]
    pages = []
    for pool in (pool_keys[0], pool_values[0]):
        page, got = (lax.dynamic_index_in_dim(at, c, 0, False) for at in (pool, places.swapped(pool, core=1)))
        pages.append(jnp.where(owner % CORES == c, page, got))
    prefix = jnp.concatenate(places.over_levels(jnp.concatenate([prefix_keys, prefix_values])))
    count = kv_heads // 2
    starts = range(0, kv_heads, count)
    columns = [slice(first * HD, (first + count) * HD) for first in starts]
    parts = [over_columns(places, [page[:, at] for page in pages], owner) for at in columns]
    prefix, parts[0] = lax.optimization_barrier((prefix, parts[0]))
    prefix = jnp.concatenate(over_chips(places, prefix))
    prefix = prefix.reshape(devices, 2, -1, prefix.shape[-1])
    pre_k, pre_v = (prefix[:, i].reshape(-1, prefix.shape[-1]) for i in range(2))
    out = None
    for first, part in zip(starts, parts):
        piece = scattered(places, part, owner)
        joined = jnp.concatenate(places.over_levels(piece))
        pieces = [(array, piece.shape[0] // 2) for array in over_chips(places, joined)]
        heads = (first, count)
        out = attend(queries, new_keys, new_values, pre_k, pre_v, pieces, lengths, heads, kv_heads, out)
    return out


def solution(mesh):
    both = ("groups", "ctx")
    placed = (P(both, None),) * 5 + (P(both, None, None, None),) * 2 + (P("groups"), P(both))
    return jax.shard_map(
        functools.partial(body, devices=mesh.shape["ctx"]),
        mesh=mesh,
        in_specs=placed,
        out_specs=P(both, None),
        check_vma=False,
    )
```

```python
import functools

import jax
import jax.numpy as jnp
from jax import lax
from jax.experimental import pallas as pl
from jax.experimental.pallas import tpu as pltpu
from jax.sharding import PartitionSpec as P

HD = 128
CORES = 2
COLUMNS = 2
TOGETHER = 2
LOG2_E = 1.4426950408889634
NT = (((1,), (1,)), ((), ()))
VMEM_LIMIT = 40 * 1024 * 1024


def attend_kernel(scale, halves, length_ref, queries_ref, own_k_ref, own_v_ref, pre_k_ref, pre_v_ref, *rest):
    piece_refs, out_ref = rest[: len(halves)], rest[-1]
    rows = queries_ref.shape[0]
    group = queries_ref.shape[1] // HD
    shared = [ref[...].reshape(-1, 2, half, HD) for ref, half in zip(piece_refs, halves)]
    keys = jnp.concatenate([own_k_ref[...], pre_k_ref[...]] + [one[:, 0].reshape(-1, HD) for one in shared], axis=0)
    values = jnp.concatenate([own_v_ref[...], pre_v_ref[...]] + [one[:, 1].reshape(-1, HD) for one in shared], axis=0)
    values = jnp.concatenate([values, jnp.ones_like(values)], axis=1)
    length = length_ref[...]
    query_at = lax.broadcasted_iota(jnp.int32, (rows, rows), 0)
    key_at = lax.broadcasted_iota(jnp.int32, (rows, rows), 1)
    seen = (key_at <= query_at) & (key_at < length)
    seen = jnp.concatenate([seen] * TOGETHER, axis=0)
    live = lax.broadcasted_iota(jnp.int32, (rows, HD), 0) < length
    blocks = range(0, group, TOGETHER)

    def scored(first):
        asked = [queries_ref[:, g * HD : (g + 1) * HD] for g in range(first, first + TOGETHER)]
        return lax.dot_general(jnp.concatenate(asked, axis=0), keys, NT, preferred_element_type=jnp.float32)

    def weighed(scores):
        scores = jnp.concatenate([jnp.where(seen, scores[:, :rows], -1e30), scores[:, rows:]], axis=1)
        top = jnp.max(scores, axis=1, keepdims=True)
        return jnp.exp2((scores - top) * scale).astype(jnp.bfloat16)

    def stored(first, weights):
        summed = jnp.dot(weights, values, preferred_element_type=jnp.float32)
        summed = summed[:, :HD] / summed[:, HD:]
        for at in range(TOGETHER):
            kept = jnp.where(live, summed[at * rows : (at + 1) * rows], 0.0)
            out_ref[:, (first + at) * HD : (first + at + 1) * HD] = kept.astype(jnp.bfloat16)

    scores, weights = scored(0), None
    for first in blocks:
        ahead = scored(first + TOGETHER) if first + TOGETHER < group else None
        if weights is not None:
            stored(first - TOGETHER, weights)
        weights = weighed(scores)
        scores = ahead
    stored(blocks[-1], weights)


def attend(queries, own_k, own_v, pre_k, pre_v, pieces, lengths, heads, kv_heads, begun):
    rows = queries.shape[0]
    width = queries.shape[1] // kv_heads
    first, at, count = heads
    halves = [half for _, half in pieces]
    arrays = [array for array, _ in pieces]
    keys = own_k.shape[0] + pre_k.shape[0] + sum(array.shape[0] for array in arrays) // 2
    column = lambda h: (0, h + first + at)
    local = lambda h: (0, h + at)
    in_specs = (
        [pl.BlockSpec((1, HD), lambda h: (0, 0)), pl.BlockSpec((rows, width), column)]
        + [pl.BlockSpec((array.shape[0], HD), column) for array in (own_k, own_v, pre_k, pre_v)]
        + [pl.BlockSpec((array.shape[0], HD), local) for array in arrays]
    )
    length = jnp.broadcast_to(lengths[:, None], (1, HD))
    operands = [length, queries, own_k, own_v, pre_k, pre_v] + arrays
    aliases = {}
    if begun is not None:
        aliases = {len(operands): 0}
        operands.append(begun)
        in_specs.append(pl.BlockSpec(memory_space=pl.ANY))
    return pl.pallas_call(
        functools.partial(attend_kernel, LOG2_E / HD**0.5, halves),
        grid=(count,),
        in_specs=in_specs,
        out_specs=pl.BlockSpec((rows, width), column),
        out_shape=jax.ShapeDtypeStruct(queries.shape, queries.dtype),
        input_output_aliases=aliases,
        compiler_params=pltpu.CompilerParams(vmem_limit_bytes=VMEM_LIMIT),
        cost_estimate=pl.CostEstimate(
            flops=4 * keys * rows * width * count,
            bytes_accessed=4 * rows * width * count,
            transcendentals=keys * rows * width // HD * count,
        ),
        name="attend_heads",
    )(*operands)


class Places:
    def __init__(self, devices):
        self.devices = devices
        self.levels = devices // (CORES * COLUMNS)

    def split(self, index):
        if isinstance(index, int):
            return index // (CORES * COLUMNS), index // CORES % COLUMNS, index % CORES
        chip = lax.div(index, CORES)
        return lax.div(chip, COLUMNS), lax.rem(chip, COLUMNS), lax.rem(index, CORES)

    def swapped(self, array, level=0, column=0, core=0):
        pairs = []
        for index in range(self.devices):
            z, y, c = self.split(index)
            z, y, c = z ^ level, y ^ column, c ^ core
            pairs.append((index, (z * COLUMNS + y) * CORES + c))
        return lax.ppermute(array, "ctx", pairs)

    def over_levels(self, array):
        return [array] + [self.swapped(array, level=s) for s in range(1, self.levels)]


def over_chips(places, rows):
    chips = [rows, places.swapped(rows, column=1)]
    return chips + [places.swapped(one, core=1) for one in chips]


def cut_rows(array, start, size):
    return lax.dynamic_slice_in_dim(array, start, size, 0)


def over_columns(places, pages, owner):
    _, y, _ = places.split(lax.axis_index("ctx"))
    _, owner_y, _ = places.split(owner)
    part = pages[0].shape[0] // COLUMNS
    cut = lambda at: jnp.concatenate([cut_rows(page, at * part, part) for page in pages])
    got = places.swapped(cut(1 - y), column=1)
    return jnp.where(owner_y == y, cut(y), got).reshape(2, part, -1)


def scattered(places, part, owner):
    z, _, _ = places.split(lax.axis_index("ctx"))
    owner_z, _, _ = places.split(owner)
    rows = part.shape[1] // places.levels
    cut = lambda at: lax.dynamic_slice_in_dim(part, at * rows, rows, 1).reshape(2 * rows, -1)
    piece = cut(z)
    for s in range(1, places.levels):
        piece = jnp.where(z ^ owner_z == s, places.swapped(cut(z ^ s), level=s), piece)
    return piece


def owned_rows(pool, owners):
    owned = (owners == lax.axis_index("ctx"))[:, None, None]
    return lax.psum(jnp.where(owned, pool[0], 0), "ctx").reshape(-1, pool.shape[-1])


def body(queries, new_keys, new_values, prefix_keys, prefix_values, pool_keys, pool_values, owners, lengths, devices):
    kv_heads = new_keys.shape[1] // HD
    blocks, block_rows = pool_keys.shape[1:3]
    chips = devices // CORES
    levels = chips // COLUMNS
    by_permutes = (
        blocks == CORES
        and chips % COLUMNS == 0
        and levels & (levels - 1) == 0
        and block_rows % (16 * chips) == 0
        and kv_heads % 2 == 0
    )
    if not by_permutes:
        pre_k, pre_v = (lax.all_gather(rows, "ctx", axis=0, tiled=True) for rows in (prefix_keys, prefix_values))
        shared = jnp.concatenate([owned_rows(pool_keys, owners), owned_rows(pool_values, owners)])
        pieces = [(shared, shared.shape[0] // 2)]
        return attend(queries, new_keys, new_values, pre_k, pre_v, pieces, lengths, (0, 0, kv_heads), kv_heads, None)
    places = Places(devices)
    c = lax.rem(lax.axis_index("ctx"), CORES)
    owner = jnp.where(c == 0, owners[0], owners[1])
    pages = []
    for pool in (pool_keys[0], pool_values[0]):
        page, got = (lax.dynamic_index_in_dim(at, c, 0, False) for at in (pool, places.swapped(pool, core=1)))
        pages.append(jnp.where(lax.rem(owner, CORES) == c, page, got))
    prefix = jnp.concatenate(places.over_levels(jnp.concatenate([prefix_keys, prefix_values])))
    count = kv_heads // 2
    columns = [slice(0, count * HD), slice(count * HD, kv_heads * HD)]
    parts = [over_columns(places, [page[:, at] for page in pages], owner) for at in columns]
    first_part, last_part = parts
    prefix, first_part = lax.optimization_barrier((prefix, first_part))
    piece = scattered(places, first_part, owner)
    across, piece = lax.optimization_barrier((places.swapped(prefix, column=1), piece))
    prefix = [prefix, across]
    joined = jnp.concatenate(places.over_levels(piece))
    prefix += [places.swapped(one, core=1) for one in prefix]
    prefix, joined = lax.optimization_barrier((prefix, joined))
    prefix = jnp.concatenate(prefix).reshape(devices, 2, -1, new_keys.shape[1])
    half = piece.shape[0] // 2
    rows = (queries, new_keys, new_values) + tuple(prefix[:, i].reshape(-1, prefix.shape[-1]) for i in range(2))
    first_pieces = [(array, half) for array in over_chips(places, joined)]

    joined = jnp.concatenate(places.over_levels(scattered(places, last_part, owner)))
    across = places.swapped(joined, column=1)
    out = attend(*rows, first_pieces, lengths, (0, 0, count // 2), kv_heads, None)
    across, out = lax.optimization_barrier((across, out))
    last_pieces = [(array, half) for array in (joined, across)]
    last_pieces += [(places.swapped(array, core=1), half) for array, _ in last_pieces]
    out = attend(*rows, first_pieces, lengths, (0, count // 2, count - count // 2), kv_heads, out)
    return attend(*rows, last_pieces, lengths, (count, 0, kv_heads - count), kv_heads, out)


def solution(mesh):
    both = ("groups", "ctx")
    placed = (P(both, None),) * 5 + (P(both, None, None, None),) * 2 + (P("groups"), P(both))
    return jax.shard_map(
        functools.partial(body, devices=mesh.shape["ctx"]),
        mesh=mesh,
        in_specs=placed,
        out_specs=P(both, None),
        check_vma=False,
    )
```

```python
import functools

import jax
import jax.numpy as jnp
from jax import lax
from jax.experimental import pallas as pl
from jax.experimental.pallas import tpu as pltpu
from jax.sharding import PartitionSpec as P

HD = 128
CORES = 2
COLUMNS = 2
TOGETHER = 8
LOG2_E = 1.4426950408889634
NT = (((1,), (1,)), ((), ()))
VMEM_LIMIT = 40 * 1024 * 1024


def attend_kernel(scale, halves, length_ref, queries_ref, own_k_ref, own_v_ref, pre_k_ref, pre_v_ref, *rest):
    piece_refs, out_ref = rest[: len(halves)], rest[-1]
    rows = queries_ref.shape[0]
    group = queries_ref.shape[1] // HD
    shared = [ref[...].reshape(-1, 2, half, HD) for ref, half in zip(piece_refs, halves)]
    keys = jnp.concatenate([own_k_ref[...], pre_k_ref[...]] + [one[:, 0].reshape(-1, HD) for one in shared], axis=0)
    values = jnp.concatenate([own_v_ref[...], pre_v_ref[...]] + [one[:, 1].reshape(-1, HD) for one in shared], axis=0)
    values = jnp.concatenate([values, jnp.ones_like(values)], axis=1)
    length = length_ref[...]
    query_at = lax.broadcasted_iota(jnp.int32, (rows, rows), 0)
    key_at = lax.broadcasted_iota(jnp.int32, (rows, rows), 1)
    seen = (key_at <= query_at) & (key_at < length)
    seen = jnp.concatenate([seen] * TOGETHER, axis=0)
    live = lax.broadcasted_iota(jnp.int32, (rows, HD), 0) < length
    blocks = range(0, group, TOGETHER)

    def scored(first):
        asked = [queries_ref[:, g * HD : (g + 1) * HD] for g in range(first, first + TOGETHER)]
        return lax.dot_general(jnp.concatenate(asked, axis=0), keys, NT, preferred_element_type=jnp.float32)

    def weighed(scores):
        scores = jnp.concatenate([jnp.where(seen, scores[:, :rows], -1e30), scores[:, rows:]], axis=1)
        top = jnp.max(scores, axis=1, keepdims=True)
        return jnp.exp2((scores - top) * scale).astype(jnp.bfloat16)

    def stored(first, weights):
        summed = jnp.dot(weights, values, preferred_element_type=jnp.float32)
        summed = summed[:, :HD] / summed[:, HD:]
        for at in range(TOGETHER):
            kept = jnp.where(live, summed[at * rows : (at + 1) * rows], 0.0)
            out_ref[:, (first + at) * HD : (first + at + 1) * HD] = kept.astype(jnp.bfloat16)

    scores, weights = scored(0), None
    for first in blocks:
        ahead = scored(first + TOGETHER) if first + TOGETHER < group else None
        if weights is not None:
            stored(first - TOGETHER, weights)
        weights = weighed(scores)
        scores = ahead
    stored(blocks[-1], weights)


def attend(queries, own_k, own_v, pre_k, pre_v, pieces, lengths, heads, kv_heads, begun):
    rows = queries.shape[0]
    width = queries.shape[1] // kv_heads
    first, count = heads
    halves = [half for _, half in pieces]
    arrays = [array for array, _ in pieces]
    keys = own_k.shape[0] + pre_k.shape[0] + sum(array.shape[0] for array in arrays) // 2
    column = lambda h: (0, h + first)
    local = lambda h: (0, h)
    in_specs = (
        [pl.BlockSpec((1, HD), lambda h: (0, 0)), pl.BlockSpec((rows, width), column)]
        + [pl.BlockSpec((array.shape[0], HD), column) for array in (own_k, own_v, pre_k, pre_v)]
        + [pl.BlockSpec((array.shape[0], HD), local) for array in arrays]
    )
    length = jnp.broadcast_to(lengths[:, None], (1, HD))
    operands = [length, queries, own_k, own_v, pre_k, pre_v] + arrays
    aliases = {}
    if begun is not None:
        aliases = {len(operands): 0}
        operands.append(begun)
        in_specs.append(pl.BlockSpec(memory_space=pl.ANY))
    return pl.pallas_call(
        functools.partial(attend_kernel, LOG2_E / HD**0.5, halves),
        grid=(count,),
        in_specs=in_specs,
        out_specs=pl.BlockSpec((rows, width), column),
        out_shape=jax.ShapeDtypeStruct(queries.shape, queries.dtype),
        input_output_aliases=aliases,
        compiler_params=pltpu.CompilerParams(vmem_limit_bytes=VMEM_LIMIT),
        cost_estimate=pl.CostEstimate(
            flops=4 * keys * rows * width * count,
            bytes_accessed=4 * rows * width * count,
            transcendentals=keys * rows * width // HD * count,
        ),
        name="attend_heads",
    )(*operands)


class Places:
    def __init__(self, devices):
        self.devices = devices
        self.levels = devices // (CORES * COLUMNS)

    def split(self, index):
        if isinstance(index, int):
            return index // (CORES * COLUMNS), index // CORES % COLUMNS, index % CORES
        chip = lax.div(index, CORES)
        return lax.div(chip, COLUMNS), lax.rem(chip, COLUMNS), lax.rem(index, CORES)

    def swapped(self, array, level=0, column=0, core=0):
        pairs = []
        for index in range(self.devices):
            z, y, c = self.split(index)
            z, y, c = z ^ level, y ^ column, c ^ core
            pairs.append((index, (z * COLUMNS + y) * CORES + c))
        return lax.ppermute(array, "ctx", pairs)

    def over_levels(self, array):
        return [array] + [self.swapped(array, level=s) for s in range(1, self.levels)]


def over_chips(places, rows):
    chips = [rows, places.swapped(rows, column=1)]
    return chips + [places.swapped(one, core=1) for one in chips]


def cut_rows(array, start, size):
    return lax.dynamic_slice_in_dim(array, start, size, 0)


def over_columns(places, pages, owner):
    _, y, _ = places.split(lax.axis_index("ctx"))
    _, owner_y, _ = places.split(owner)
    part = pages[0].shape[0] // COLUMNS
    cut = lambda at: jnp.concatenate([cut_rows(page, at * part, part) for page in pages])
    got = places.swapped(cut(1 - y), column=1)
    return jnp.where(owner_y == y, cut(y), got).reshape(2, part, -1)


def scattered(places, part, owner):
    z, _, _ = places.split(lax.axis_index("ctx"))
    owner_z, _, _ = places.split(owner)
    rows = part.shape[1] // places.levels
    cut = lambda at: lax.dynamic_slice_in_dim(part, at * rows, rows, 1).reshape(2 * rows, -1)
    piece = cut(z)
    for s in range(1, places.levels):
        piece = jnp.where(z ^ owner_z == s, places.swapped(cut(z ^ s), level=s), piece)
    return piece


def owned_rows(pool, owners):
    owned = (owners == lax.axis_index("ctx"))[:, None, None]
    return lax.psum(jnp.where(owned, pool[0], 0), "ctx").reshape(-1, pool.shape[-1])


def body(queries, new_keys, new_values, prefix_keys, prefix_values, pool_keys, pool_values, owners, lengths, devices):
    kv_heads = new_keys.shape[1] // HD
    blocks, block_rows = pool_keys.shape[1:3]
    chips = devices // CORES
    levels = chips // COLUMNS
    by_permutes = (
        blocks == CORES
        and chips % COLUMNS == 0
        and levels & (levels - 1) == 0
        and block_rows % (16 * chips) == 0
        and kv_heads % 2 == 0
    )
    if not by_permutes:
        pre_k, pre_v = (lax.all_gather(rows, "ctx", axis=0, tiled=True) for rows in (prefix_keys, prefix_values))
        shared = jnp.concatenate([owned_rows(pool_keys, owners), owned_rows(pool_values, owners)])
        pieces = [(shared, shared.shape[0] // 2)]
        return attend(queries, new_keys, new_values, pre_k, pre_v, pieces, lengths, (0, kv_heads), kv_heads, None)
    places = Places(devices)
    c = lax.rem(lax.axis_index("ctx"), CORES)
    owner = jnp.where(c == 0, owners[0], owners[1])
    pages = []
    for pool in (pool_keys[0], pool_values[0]):
        page, got = (lax.dynamic_index_in_dim(at, c, 0, False) for at in (pool, places.swapped(pool, core=1)))
        pages.append(jnp.where(lax.rem(owner, CORES) == c, page, got))
    prefix = jnp.concatenate(places.over_levels(jnp.concatenate([prefix_keys, prefix_values])))
    count = kv_heads // 2
    columns = [slice(0, count * HD), slice(count * HD, kv_heads * HD)]
    parts = [over_columns(places, [page[:, at] for page in pages], owner) for at in columns]
    pieces = [scattered(places, part, owner) for part in parts]
    prefix, pieces[0] = lax.optimization_barrier((prefix, pieces[0]))
    joined = [jnp.concatenate(places.over_levels(pieces[0]))]
    prefix = [prefix, places.swapped(prefix, column=1)]
    prefix, joined[0], pieces[1] = lax.optimization_barrier((prefix, joined[0], pieces[1]))
    joined.append(jnp.concatenate(places.over_levels(pieces[1])))
    prefix = jnp.concatenate(prefix + [places.swapped(one, core=1) for one in prefix])
    prefix = prefix.reshape(devices, 2, -1, prefix.shape[-1])
    rows = (queries, new_keys, new_values) + tuple(prefix[:, i].reshape(-1, prefix.shape[-1]) for i in range(2))
    half = pieces[0].shape[0] // 2
    across = places.swapped(joined[1], column=1)
    out = attend(*rows, [(at, half) for at in over_chips(places, joined[0])], lengths, (0, count), kv_heads, None)
    across, out = lax.optimization_barrier((across, out))
    shared = [joined[1], across]
    shared += [places.swapped(at, core=1) for at in shared]
    return attend(*rows, [(at, half) for at in shared], lengths, (count, kv_heads - count), kv_heads, out)


def solution(mesh):
    both = ("groups", "ctx")
    placed = (P(both, None),) * 5 + (P(both, None, None, None),) * 2 + (P("groups"), P(both))
    return jax.shard_map(
        functools.partial(body, devices=mesh.shape["ctx"]),
        mesh=mesh,
        in_specs=placed,
        out_specs=P(both, None),
        check_vma=False,
    )
```

```python
import functools

import jax
import jax.numpy as jnp
from jax import lax
from jax.experimental import pallas as pl
from jax.experimental.pallas import tpu as pltpu
from jax.sharding import PartitionSpec as P

HD = 128
CORES = 2
COLUMNS = 2
TOGETHER = 1
LOG2_E = 1.4426950408889634
NT = (((1,), (1,)), ((), ()))
VMEM_LIMIT = 40 * 1024 * 1024


def attend_kernel(scale, halves, length_ref, queries_ref, own_k_ref, own_v_ref, pre_k_ref, pre_v_ref, *rest):
    piece_refs, out_ref = rest[: len(halves)], rest[-1]
    rows = queries_ref.shape[0]
    group = queries_ref.shape[1] // HD
    shared = [ref[...].reshape(-1, 2, half, HD) for ref, half in zip(piece_refs, halves)]
    keys = jnp.concatenate([own_k_ref[...], pre_k_ref[...]] + [one[:, 0].reshape(-1, HD) for one in shared], axis=0)
    values = jnp.concatenate([own_v_ref[...], pre_v_ref[...]] + [one[:, 1].reshape(-1, HD) for one in shared], axis=0)
    values = jnp.concatenate([values, jnp.ones_like(values)], axis=1)
    length = length_ref[...]
    query_at = lax.broadcasted_iota(jnp.int32, (rows, rows), 0)
    key_at = lax.broadcasted_iota(jnp.int32, (rows, rows), 1)
    seen = (key_at <= query_at) & (key_at < length)
    seen = jnp.concatenate([seen] * TOGETHER, axis=0)
    live = lax.broadcasted_iota(jnp.int32, (rows, HD), 0) < length
    blocks = range(0, group, TOGETHER)

    def scored(first):
        asked = [queries_ref[:, g * HD : (g + 1) * HD] for g in range(first, first + TOGETHER)]
        return lax.dot_general(jnp.concatenate(asked, axis=0), keys, NT, preferred_element_type=jnp.float32)

    def weighed(scores):
        scores = jnp.concatenate([jnp.where(seen, scores[:, :rows], -1e30), scores[:, rows:]], axis=1)
        top = jnp.max(scores, axis=1, keepdims=True)
        return jnp.exp2((scores - top) * scale).astype(jnp.bfloat16)

    def stored(first, weights):
        summed = jnp.dot(weights, values, preferred_element_type=jnp.float32)
        summed = summed[:, :HD] / summed[:, HD:]
        for at in range(TOGETHER):
            kept = jnp.where(live, summed[at * rows : (at + 1) * rows], 0.0)
            out_ref[:, (first + at) * HD : (first + at + 1) * HD] = kept.astype(jnp.bfloat16)

    scores, weights = scored(0), None
    for first in blocks:
        ahead = scored(first + TOGETHER) if first + TOGETHER < group else None
        if weights is not None:
            stored(first - TOGETHER, weights)
        weights = weighed(scores)
        scores = ahead
    stored(blocks[-1], weights)


def attend(queries, own_k, own_v, pre_k, pre_v, pieces, lengths, heads, kv_heads, begun):
    rows = queries.shape[0]
    width = queries.shape[1] // kv_heads
    first, count = heads
    halves = [half for _, half in pieces]
    arrays = [array for array, _ in pieces]
    keys = own_k.shape[0] + pre_k.shape[0] + sum(array.shape[0] for array in arrays) // 2
    column = lambda h: (0, h + first)
    local = lambda h: (0, h)
    in_specs = (
        [pl.BlockSpec((1, HD), lambda h: (0, 0)), pl.BlockSpec((rows, width), column)]
        + [pl.BlockSpec((array.shape[0], HD), column) for array in (own_k, own_v, pre_k, pre_v)]
        + [pl.BlockSpec((array.shape[0], HD), local) for array in arrays]
    )
    length = jnp.broadcast_to(lengths[:, None], (1, HD))
    operands = [length, queries, own_k, own_v, pre_k, pre_v] + arrays
    aliases = {}
    if begun is not None:
        aliases = {len(operands): 0}
        operands.append(begun)
        in_specs.append(pl.BlockSpec(memory_space=pl.ANY))
    return pl.pallas_call(
        functools.partial(attend_kernel, LOG2_E / HD**0.5, halves),
        grid=(count,),
        in_specs=in_specs,
        out_specs=pl.BlockSpec((rows, width), column),
        out_shape=jax.ShapeDtypeStruct(queries.shape, queries.dtype),
        input_output_aliases=aliases,
        compiler_params=pltpu.CompilerParams(vmem_limit_bytes=VMEM_LIMIT),
        cost_estimate=pl.CostEstimate(
            flops=4 * keys * rows * width * count,
            bytes_accessed=4 * rows * width * count,
            transcendentals=keys * rows * width // HD * count,
        ),
        name="attend_heads",
    )(*operands)


class Places:
    def __init__(self, devices):
        self.devices = devices
        self.levels = devices // (CORES * COLUMNS)

    def split(self, index):
        if isinstance(index, int):
            return index // (CORES * COLUMNS), index // CORES % COLUMNS, index % CORES
        chip = lax.div(index, CORES)
        return lax.div(chip, COLUMNS), lax.rem(chip, COLUMNS), lax.rem(index, CORES)

    def swapped(self, array, level=0, column=0, core=0):
        pairs = []
        for index in range(self.devices):
            z, y, c = self.split(index)
            z, y, c = z ^ level, y ^ column, c ^ core
            pairs.append((index, (z * COLUMNS + y) * CORES + c))
        return lax.ppermute(array, "ctx", pairs)

    def over_levels(self, array):
        return [array] + [self.swapped(array, level=s) for s in range(1, self.levels)]


def over_chips(places, rows):
    chips = [rows, places.swapped(rows, column=1)]
    return chips + [places.swapped(one, core=1) for one in chips]


def chosen(flag, mine, got, starts, sizes):
    return jnp.where(flag, lax.dynamic_slice(mine, starts, sizes), lax.dynamic_slice(got, starts, sizes))


def for_levels(places, part):
    z, _, _ = places.split(lax.axis_index("ctx"))
    rows = part.shape[1] // places.levels
    return [
        lax.dynamic_slice_in_dim(part, (z ^ s) * rows, rows, 1).reshape(2 * rows, -1) for s in range(places.levels)
    ]


def from_owner(distance, mine, got):
    piece = mine
    for s, one in enumerate(got, 1):
        piece = jnp.where(distance == s, one, piece)
    return piece


def owned_rows(pool, owners):
    owned = (owners == lax.axis_index("ctx"))[:, None, None]
    return lax.psum(jnp.where(owned, pool[0], 0), "ctx").reshape(-1, pool.shape[-1])


def body(queries, new_keys, new_values, prefix_keys, prefix_values, pool_keys, pool_values, owners, lengths, devices):
    kv_heads = new_keys.shape[1] // HD
    blocks, block_rows = pool_keys.shape[1:3]
    chips = devices // CORES
    levels = chips // COLUMNS
    by_permutes = (
        blocks == CORES
        and chips % COLUMNS == 0
        and levels & (levels - 1) == 0
        and block_rows % (16 * chips) == 0
        and kv_heads % 2 == 0
    )
    if not by_permutes:
        pre_k, pre_v = (lax.all_gather(rows, "ctx", axis=0, tiled=True) for rows in (prefix_keys, prefix_values))
        shared = jnp.concatenate([owned_rows(pool_keys, owners), owned_rows(pool_values, owners)])
        pieces = [(shared, shared.shape[0] // 2)]
        return attend(queries, new_keys, new_values, pre_k, pre_v, pieces, lengths, (0, kv_heads), kv_heads, None)
    places = Places(devices)
    z, y, c = places.split(lax.axis_index("ctx"))
    owner = jnp.where(c == 0, owners[0], owners[1])
    owner_z, owner_y, owner_c = places.split(owner)
    pools = [(pool[0], places.swapped(pool[0], core=1)) for pool in (pool_keys, pool_values)]
    count = kv_heads // 2
    part = block_rows // COLUMNS
    tied = lax.optimization_barrier

    def cut(pools, column, first):
        sizes = (1, part, count * HD)
        rows = [chosen(owner_c == c, *pool, (c, column * part, first * HD), sizes) for pool in pools]
        return jnp.concatenate(rows)

    sent = [cut(pools, 1 - y, 0)]
    sent[0], pools = tied((sent[0], pools))
    sent.append(cut(pools, 1 - y, count))
    prefix, sent[1] = tied((jnp.concatenate([prefix_keys, prefix_values]), sent[1]))
    got = [places.swapped(one, column=1) for one in sent]
    prefix = jnp.concatenate(places.over_levels(prefix))

    def over_z(cuts):
        return [places.swapped(one, level=s) for s, one in enumerate(cuts) if s]

    first_cuts = for_levels(places, jnp.where(owner_y == y, cut(pools, y, 0), got[0]))
    first_got = over_z(first_cuts)
    last_cuts = for_levels(places, jnp.where(owner_y == y, cut(pools, y, count), got[1]))
    last_got = over_z(last_cuts)
    piece = from_owner(z ^ owner_z, first_cuts[0], first_got)
    pieces = [piece, from_owner(z ^ owner_z, last_cuts[0], last_got)]
    prefix, pieces[1] = tied((prefix, pieces[1]))
    joined = [jnp.concatenate(places.over_levels(one)) for one in pieces]
    prefix, joined[1] = tied(([prefix, places.swapped(prefix, column=1)], joined[1]))
    prefix = jnp.concatenate(prefix + [places.swapped(one, core=1) for one in prefix])
    prefix = prefix.reshape(devices, 2, -1, prefix.shape[-1])
    rows = (queries, new_keys, new_values) + tuple(prefix[:, i].reshape(-1, prefix.shape[-1]) for i in range(2))
    half = pieces[0].shape[0] // 2
    across = places.swapped(joined[1], column=1)
    out = attend(*rows, [(at, half) for at in over_chips(places, joined[0])], lengths, (0, count), kv_heads, None)
    across, out = tied((across, out))
    shared = [joined[1], across]
    shared += [places.swapped(at, core=1) for at in shared]
    return attend(*rows, [(at, half) for at in shared], lengths, (count, kv_heads - count), kv_heads, out)


def solution(mesh):
    both = ("groups", "ctx")
    placed = (P(both, None),) * 5 + (P(both, None, None, None),) * 2 + (P("groups"), P(both))
    return jax.shard_map(
        functools.partial(body, devices=mesh.shape["ctx"]),
        mesh=mesh,
        in_specs=placed,
        out_specs=P(both, None),
        check_vma=False,
    )
```

```python
import functools

import jax
import jax.numpy as jnp
from jax import lax
from jax.experimental import pallas as pl
from jax.experimental.pallas import tpu as pltpu
from jax.sharding import PartitionSpec as P

HD = 128
CORES = 2
COLUMNS = 2
LOG2_E = 1.4426950408889634
VMEM_LIMIT = 24 * 1024 * 1024


def attend_kernel(scale, halves, has_own, goes_on, ends, length_ref, queries_ref, *rest):
    rest = list(rest)
    own_refs = [rest.pop(0) for _ in range(4 if has_own else 0)]
    piece_refs = [rest.pop(0) for _ in halves]
    state_refs = [rest.pop(0) for _ in range(2 if goes_on else 0)]
    out_refs = rest[-1:] if ends else rest[-2:]
    rows = queries_ref.shape[0]
    group = queries_ref.shape[1] // HD
    shared = [ref[...].reshape(-1, 2, half, HD) for ref, half in zip(piece_refs, halves)]
    keys = jnp.concatenate([ref[...] for ref in own_refs[::2]] + [one[:, 0].reshape(-1, HD) for one in shared])
    values = jnp.concatenate([ref[...] for ref in own_refs[1::2]] + [one[:, 1].reshape(-1, HD) for one in shared])
    values = jnp.concatenate([values, jnp.ones_like(values)], axis=1)
    turned = keys.T
    length = length_ref[...]
    query_at = lax.broadcasted_iota(jnp.int32, (rows, rows), 0)
    key_at = lax.broadcasted_iota(jnp.int32, (rows, rows), 1)
    seen = (key_at <= query_at) & (key_at < length)
    live = lax.broadcasted_iota(jnp.int32, (rows, HD), 0) < length

    def scored(g):
        asked = queries_ref[:, g * HD : (g + 1) * HD]
        return jnp.dot(asked, turned, preferred_element_type=jnp.float32)

    def weighed(g, scores):
        if has_own:
            scores = jnp.concatenate([jnp.where(seen, scores[:, :rows], -1e30), scores[:, rows:]], axis=1)
        top = jnp.max(scores, axis=1, keepdims=True)
        if goes_on:
            top = jnp.maximum(state_refs[1][0, g * rows : (g + 1) * rows].astype(jnp.float32), top)
            wide = jnp.concatenate([top] * (scores.shape[1] // HD), axis=1)
        else:
            wide = top
        if not ends:
            top = jnp.broadcast_to(top, (rows, HD)).astype(jnp.bfloat16)
            out_refs[1][0, g * rows : (g + 1) * rows] = top
            wide = top.astype(jnp.float32)[:, :1]
        return top, jnp.exp2((scores - wide) * scale).astype(jnp.bfloat16)

    def stored(g, top, weights):
        at = slice(g * rows, (g + 1) * rows)
        summed = jnp.dot(weights, values, preferred_element_type=jnp.float32)
        if goes_on:
            shrink = jnp.exp2((state_refs[1][0, at].astype(jnp.float32) - top) * scale)
            summed += state_refs[0][0, at] * jnp.concatenate([shrink, shrink], axis=1)
        if ends:
            total = summed[:, HD:]
            inverse = pl.reciprocal(total, approx=True)
            inverse *= 2.0 - total * inverse
            kept = jnp.where(live, summed[:, :HD] * inverse, 0.0)
            out_refs[0][:, g * HD : (g + 1) * HD] = kept.astype(jnp.bfloat16)
        else:
            out_refs[0][0, at] = summed

    scores, weights = scored(0), None
    for g in range(group):
        ahead = scored(g + 1) if g + 1 < group else None
        if weights is not None:
            stored(g - 1, *weights)
        weights = weighed(g, scores)
        scores = ahead
    stored(group - 1, *weights)


def attend(queries, own, pieces, length, heads, first_column, kv_heads, state=None, begun=None, ends=True):
    rows = queries.shape[0]
    width = queries.shape[1] // kv_heads
    packed = rows * width // HD
    first, count = heads
    halves = [half for _, half in pieces]
    arrays = [array for array, _ in pieces]
    keys = sum(array.shape[0] for array in own[::2]) + sum(array.shape[0] for array in arrays) // 2
    column = lambda h: (0, h + first)
    local = lambda h: (0, h + first - first_column)
    stacked = lambda h: (h, 0, 0)
    state_specs = [pl.BlockSpec((1, packed, 2 * HD), stacked), pl.BlockSpec((1, packed, HD), stacked)]
    in_specs = (
        [pl.BlockSpec((1, HD), lambda h: (0, 0)), pl.BlockSpec((rows, width), column)]
        + [pl.BlockSpec((array.shape[0], HD), column) for array in own]
        + [pl.BlockSpec((array.shape[0], HD), local) for array in arrays]
    )
    operands = [length, queries, *own, *arrays]
    if state is not None:
        operands += state
        in_specs += state_specs
    aliases = {}
    if begun is not None:
        aliases = {len(operands): 0}
        operands.append(begun)
        in_specs.append(pl.BlockSpec(memory_space=pl.ANY))
    if ends:
        out_specs = pl.BlockSpec((rows, width), column)
        out_shape = jax.ShapeDtypeStruct(queries.shape, queries.dtype)
    else:
        out_specs = state_specs
        out_shape = [
            jax.ShapeDtypeStruct((count, packed, 2 * HD), jnp.float32),
            jax.ShapeDtypeStruct((count, packed, HD), jnp.bfloat16),
        ]
    return pl.pallas_call(
        functools.partial(attend_kernel, LOG2_E / HD**0.5, halves, bool(own), state is not None, ends),
        grid=(count,),
        in_specs=in_specs,
        out_specs=out_specs,
        out_shape=out_shape,
        input_output_aliases=aliases,
        compiler_params=pltpu.CompilerParams(vmem_limit_bytes=VMEM_LIMIT),
        cost_estimate=pl.CostEstimate(
            flops=4 * keys * packed * HD * count,
            bytes_accessed=4 * rows * width * count,
            transcendentals=keys * packed * count,
        ),
        name="attend_heads",
    )(*operands)


class Places:
    def __init__(self, devices):
        self.devices = devices
        self.levels = devices // (CORES * COLUMNS)

    def split(self, index):
        if isinstance(index, int):
            return index // (CORES * COLUMNS), index // CORES % COLUMNS, index % CORES
        chip = lax.div(index, CORES)
        return lax.div(chip, COLUMNS), lax.rem(chip, COLUMNS), lax.rem(index, CORES)

    def swapped(self, array, level=0, column=0, core=0):
        pairs = []
        for index in range(self.devices):
            z, y, c = self.split(index)
            z, y, c = z ^ level, y ^ column, c ^ core
            pairs.append((index, (z * COLUMNS + y) * CORES + c))
        return lax.ppermute(array, "ctx", pairs)

    def over_levels(self, array):
        return [array] + [self.swapped(array, level=s) for s in range(1, self.levels)]


def over_chips(places, rows):
    chips = [rows, places.swapped(rows, column=1)]
    return chips + [places.swapped(one, core=1) for one in chips]


def chosen(flag, mine, got, starts, sizes):
    return jnp.where(flag, lax.dynamic_slice(mine, starts, sizes), lax.dynamic_slice(got, starts, sizes))


def for_levels(places, part):
    z, _, _ = places.split(lax.axis_index("ctx"))
    rows = part.shape[1] // places.levels
    return [
        lax.dynamic_slice_in_dim(part, (z ^ s) * rows, rows, 1).reshape(2 * rows, -1) for s in range(places.levels)
    ]


def from_owner(distance, mine, got):
    piece = mine
    for s, one in enumerate(got, 1):
        piece = jnp.where(distance == s, one, piece)
    return piece


def owned_rows(pool, owners):
    owned = (owners == lax.axis_index("ctx"))[:, None, None]
    return lax.psum(jnp.where(owned, pool[0], 0), "ctx").reshape(-1, pool.shape[-1])


def body(queries, new_keys, new_values, prefix_keys, prefix_values, pool_keys, pool_values, owners, lengths, devices):
    kv_heads = new_keys.shape[1] // HD
    blocks, block_rows = pool_keys.shape[1:3]
    length = jnp.broadcast_to(lengths[:, None], (1, HD))
    chips = devices // CORES
    levels = chips // COLUMNS
    by_permutes = (
        blocks == CORES
        and chips % COLUMNS == 0
        and levels & (levels - 1) == 0
        and block_rows % (16 * chips) == 0
        and kv_heads % 2 == 0
    )
    if not by_permutes:
        pre_k, pre_v = (lax.all_gather(rows, "ctx", axis=0, tiled=True) for rows in (prefix_keys, prefix_values))
        shared = jnp.concatenate([owned_rows(pool_keys, owners), owned_rows(pool_values, owners)])
        pieces = [(shared, shared.shape[0] // 2)]
        own = (new_keys, new_values, pre_k, pre_v)
        return attend(queries, own, pieces, length, (0, kv_heads), 0, kv_heads)
    places = Places(devices)
    z, y, c = places.split(lax.axis_index("ctx"))
    owner = jnp.where(c == 0, owners[0], owners[1])
    owner_z, owner_y, owner_c = places.split(owner)
    pools = [(pool[0], places.swapped(pool[0], core=1)) for pool in (pool_keys, pool_values)]
    count = kv_heads // 2
    part = block_rows // COLUMNS
    tied = lax.optimization_barrier

    def cut(pools, column, first):
        sizes = (1, part, count * HD)
        rows = [chosen(owner_c == c, *pool, (c, column * part, first * HD), sizes) for pool in pools]
        return jnp.concatenate(rows)

    sent = [cut(pools, 1 - y, 0)]
    sent[0], pools = tied((sent[0], pools))
    sent.append(cut(pools, 1 - y, count))
    prefix, sent[1] = tied((jnp.concatenate([prefix_keys, prefix_values]), sent[1]))
    got = [places.swapped(one, column=1) for one in sent]
    prefix = jnp.concatenate(places.over_levels(prefix))

    def over_z(cuts):
        return [places.swapped(one, level=s) for s, one in enumerate(cuts) if s]

    first_cuts = for_levels(places, jnp.where(owner_y == y, cut(pools, y, 0), got[0]))
    first_got = over_z(first_cuts)
    last_cuts = for_levels(places, jnp.where(owner_y == y, cut(pools, y, count), got[1]))
    last_got = over_z(last_cuts)
    prefix, last_cuts[0] = tied((prefix, last_cuts[0]))
    prefix = [prefix, places.swapped(prefix, column=1)]
    pieces = [from_owner(z ^ owner_z, *one) for one in ((first_cuts[0], first_got), (last_cuts[0], last_got))]
    prefix, pieces[1] = tied((prefix, pieces[1]))
    joined = [jnp.concatenate(places.over_levels(one)) for one in pieces]
    prefix = jnp.concatenate(prefix + [places.swapped(one, core=1) for one in prefix])
    prefix = prefix.reshape(devices, 2, -1, prefix.shape[-1])
    own = (new_keys, new_values) + tuple(prefix[:, i].reshape(-1, prefix.shape[-1]) for i in range(2))
    half = pieces[0].shape[0] // 2
    across = [places.swapped(one, column=1) for one in joined]
    other = [places.swapped(one, core=1) for one in joined]
    first = [(at, half) for at in (joined[0], other[0], across[0], places.swapped(across[0], core=1))]
    out = attend(queries, own, first, length, (0, count - 1), 0, kv_heads)
    across[1], out = tied((across[1], out))
    last = [(at, half) for at in (joined[1], other[1], across[1], places.swapped(across[1], core=1))]
    out = attend(queries, own, first, length, (count - 1, 1), 0, kv_heads, begun=out)
    return attend(queries, own, last, length, (count, kv_heads - count), count, kv_heads, begun=out)


def solution(mesh):
    both = ("groups", "ctx")
    placed = (P(both, None),) * 5 + (P(both, None, None, None),) * 2 + (P("groups"), P(both))
    return jax.shard_map(
        functools.partial(body, devices=mesh.shape["ctx"]),
        mesh=mesh,
        in_specs=placed,
        out_specs=P(both, None),
        check_vma=False,
    )
```

```python
import functools

import jax
import jax.numpy as jnp
from jax import lax
from jax.experimental import pallas as pl
from jax.experimental.pallas import tpu as pltpu
from jax.sharding import PartitionSpec as P

HD = 128
CORES = 2
COLUMNS = 2
LOG2_E = 1.4426950408889634
VMEM_LIMIT = 24 * 1024 * 1024


def attend_kernel(scale, halves, heads, first_column, length_ref, queries_ref, *rest):
    own_refs, piece_refs = rest[:4], rest[4 : 4 + len(halves)]
    out_ref, blocks_ref, sent_sems = rest[-3:]
    first, count = heads
    rows = queries_ref.shape[0]
    width = blocks_ref.shape[2]
    group = width // HD
    length = length_ref[...]
    query_at = lax.broadcasted_iota(jnp.int32, (rows, rows), 0)
    key_at = lax.broadcasted_iota(jnp.int32, (rows, rows), 1)
    seen = (key_at <= query_at) & (key_at < length)
    live = lax.broadcasted_iota(jnp.int32, (rows, HD), 0) < length

    def copied(h):
        target = out_ref.at[:, pl.ds(pl.multiple_of((first + h) * width, width), width)]
        return pltpu.make_async_copy(blocks_ref.at[h], target, sent_sems.at[h])

    def one_head(h, _):
        column = pl.ds(pl.multiple_of((first + h) * HD, HD), HD)
        local = pl.ds(pl.multiple_of((first + h) * HD - first_column, HD), HD)
        shared = [ref[:, local].reshape(-1, 2, half, HD) for ref, half in zip(piece_refs, halves)]
        keys = jnp.concatenate([ref[:, column] for ref in own_refs[::2]] + [one[:, 0].reshape(-1, HD) for one in shared])
        values = [ref[:, column] for ref in own_refs[1::2]] + [one[:, 1].reshape(-1, HD) for one in shared]
        values = jnp.concatenate(values)
        values = jnp.concatenate([values, jnp.ones_like(values)], axis=1)
        turned = keys.T

        def scored(g):
            asked = queries_ref[:, pl.ds(pl.multiple_of((first + h) * width + g * HD, HD), HD)]
            return jnp.dot(asked, turned, preferred_element_type=jnp.float32)

        def weighed(scores):
            scores = jnp.concatenate([jnp.where(seen, scores[:, :rows], -1e30), scores[:, rows:]], axis=1)
            top = jnp.max(scores, axis=1, keepdims=True)
            return jnp.exp2((scores - top) * scale).astype(jnp.bfloat16)

        def stored(g, weights):
            summed = jnp.dot(weights, values, preferred_element_type=jnp.float32)
            total = summed[:, HD:]
            inverse = pl.reciprocal(total, approx=True)
            inverse *= 2.0 - total * inverse
            kept = jnp.where(live, summed[:, :HD] * inverse, 0.0)
            blocks_ref[h, :, g * HD : (g + 1) * HD] = kept.astype(jnp.bfloat16)

        scores, weights = scored(0), None
        for g in range(group):
            ahead = scored(g + 1) if g + 1 < group else None
            if weights is not None:
                stored(g - 1, weights)
            weights = weighed(scores)
            scores = ahead
        stored(group - 1, weights)
        copied(h).start()
        return _

    lax.fori_loop(0, count, one_head, 0)
    for h in range(count):
        copied(h).wait()


def attend(queries, own, pieces, length, heads, first_column, kv_heads, begun=None):
    rows = queries.shape[0]
    width = queries.shape[1] // kv_heads
    count = heads[1]
    halves = [half for _, half in pieces]
    arrays = [array for array, _ in pieces]
    keys = sum(array.shape[0] for array in own[::2]) + sum(array.shape[0] for array in arrays) // 2
    operands = [length, queries, *own, *arrays]
    in_specs = [pl.BlockSpec(memory_space=pltpu.VMEM) for _ in operands]
    aliases = {}
    if begun is not None:
        aliases = {len(operands): 0}
        operands.append(begun)
        in_specs.append(pl.BlockSpec(memory_space=pl.ANY))
    return pl.pallas_call(
        functools.partial(attend_kernel, LOG2_E / HD**0.5, halves, heads, first_column * HD),
        in_specs=in_specs,
        out_specs=pl.BlockSpec(memory_space=pl.ANY),
        out_shape=jax.ShapeDtypeStruct(queries.shape, queries.dtype),
        scratch_shapes=[pltpu.VMEM((count, rows, width), queries.dtype), pltpu.SemaphoreType.DMA((count,))],
        input_output_aliases=aliases,
        compiler_params=pltpu.CompilerParams(vmem_limit_bytes=VMEM_LIMIT),
        cost_estimate=pl.CostEstimate(
            flops=4 * keys * rows * width * count,
            bytes_accessed=4 * rows * width * count,
            transcendentals=keys * rows * width // HD * count,
        ),
        name="attend_heads",
    )(*operands)


class Places:
    def __init__(self, devices):
        self.devices = devices
        self.levels = devices // (CORES * COLUMNS)

    def split(self, index):
        if isinstance(index, int):
            return index // (CORES * COLUMNS), index // CORES % COLUMNS, index % CORES
        chip = lax.div(index, CORES)
        return lax.div(chip, COLUMNS), lax.rem(chip, COLUMNS), lax.rem(index, CORES)

    def swapped(self, array, level=0, column=0, core=0):
        pairs = []
        for index in range(self.devices):
            z, y, c = self.split(index)
            z, y, c = z ^ level, y ^ column, c ^ core
            pairs.append((index, (z * COLUMNS + y) * CORES + c))
        return lax.ppermute(array, "ctx", pairs)

    def over_levels(self, array):
        return [array] + [self.swapped(array, level=s) for s in range(1, self.levels)]


def over_chips(places, rows):
    chips = [rows, places.swapped(rows, column=1)]
    return chips + [places.swapped(one, core=1) for one in chips]


def chosen(flag, mine, got, starts, sizes):
    return jnp.where(flag, lax.dynamic_slice(mine, starts, sizes), lax.dynamic_slice(got, starts, sizes))


def for_levels(places, part):
    z, _, _ = places.split(lax.axis_index("ctx"))
    rows = part.shape[1] // places.levels
    return [
        lax.dynamic_slice_in_dim(part, (z ^ s) * rows, rows, 1).reshape(2 * rows, -1) for s in range(places.levels)
    ]


def from_owner(distance, mine, got):
    piece = mine
    for s, one in enumerate(got, 1):
        piece = jnp.where(distance == s, one, piece)
    return piece


def owned_rows(pool, owners):
    owned = (owners == lax.axis_index("ctx"))[:, None, None]
    return lax.psum(jnp.where(owned, pool[0], 0), "ctx").reshape(-1, pool.shape[-1])


def body(queries, new_keys, new_values, prefix_keys, prefix_values, pool_keys, pool_values, owners, lengths, devices):
    kv_heads = new_keys.shape[1] // HD
    blocks, block_rows = pool_keys.shape[1:3]
    length = jnp.broadcast_to(lengths[:, None], (1, HD))
    chips = devices // CORES
    levels = chips // COLUMNS
    by_permutes = (
        blocks == CORES
        and chips % COLUMNS == 0
        and levels & (levels - 1) == 0
        and block_rows % (16 * chips) == 0
        and kv_heads % 2 == 0
    )
    if not by_permutes:
        pre_k, pre_v = (lax.all_gather(rows, "ctx", axis=0, tiled=True) for rows in (prefix_keys, prefix_values))
        shared = jnp.concatenate([owned_rows(pool_keys, owners), owned_rows(pool_values, owners)])
        pieces = [(shared, shared.shape[0] // 2)]
        own = (new_keys, new_values, pre_k, pre_v)
        return attend(queries, own, pieces, length, (0, kv_heads), 0, kv_heads)
    places = Places(devices)
    z, y, c = places.split(lax.axis_index("ctx"))
    owner = jnp.where(c == 0, owners[0], owners[1])
    owner_z, owner_y, owner_c = places.split(owner)
    pools = [(pool[0], places.swapped(pool[0], core=1)) for pool in (pool_keys, pool_values)]
    count = kv_heads // 2
    part = block_rows // COLUMNS
    tied = lax.optimization_barrier

    def cut(pools, column, first):
        sizes = (1, part, count * HD)
        rows = [chosen(owner_c == c, *pool, (c, column * part, first * HD), sizes) for pool in pools]
        return jnp.concatenate(rows)

    sent = [cut(pools, 1 - y, 0)]
    sent[0], pools = tied((sent[0], pools))
    sent.append(cut(pools, 1 - y, count))
    prefix, sent[1] = tied((jnp.concatenate([prefix_keys, prefix_values]), sent[1]))
    got = [places.swapped(one, column=1) for one in sent]
    prefix = jnp.concatenate(places.over_levels(prefix))

    def over_z(cuts):
        return [places.swapped(one, level=s) for s, one in enumerate(cuts) if s]

    first_cuts = for_levels(places, jnp.where(owner_y == y, cut(pools, y, 0), got[0]))
    first_got = over_z(first_cuts)
    last_cuts = for_levels(places, jnp.where(owner_y == y, cut(pools, y, count), got[1]))
    last_got = over_z(last_cuts)
    prefix, last_cuts[0] = tied((prefix, last_cuts[0]))
    prefix = [prefix, places.swapped(prefix, column=1)]
    pieces = [from_owner(z ^ owner_z, *one) for one in ((first_cuts[0], first_got), (last_cuts[0], last_got))]
    prefix, pieces[1] = tied((prefix, pieces[1]))
    joined = [jnp.concatenate(places.over_levels(one)) for one in pieces]
    prefix = jnp.concatenate(prefix + [places.swapped(one, core=1) for one in prefix])
    prefix = prefix.reshape(devices, 2, -1, prefix.shape[-1])
    own = (new_keys, new_values) + tuple(prefix[:, i].reshape(-1, prefix.shape[-1]) for i in range(2))
    half = pieces[0].shape[0] // 2
    across = [places.swapped(one, column=1) for one in joined]
    other = [places.swapped(one, core=1) for one in joined]
    first = [(at, half) for at in (joined[0], other[0], across[0], places.swapped(across[0], core=1))]
    out = attend(queries, own, first, length, (0, count - 1), 0, kv_heads)
    across[1], out = tied((across[1], out))
    last = [(at, half) for at in (joined[1], other[1], across[1], places.swapped(across[1], core=1))]
    out = attend(queries, own, first, length, (count - 1, 1), 0, kv_heads, begun=out)
    return attend(queries, own, last, length, (count, kv_heads - count), count, kv_heads, begun=out)


def solution(mesh):
    both = ("groups", "ctx")
    placed = (P(both, None),) * 5 + (P(both, None, None, None),) * 2 + (P("groups"), P(both))
    return jax.shard_map(
        functools.partial(body, devices=mesh.shape["ctx"]),
        mesh=mesh,
        in_specs=placed,
        out_specs=P(both, None),
        check_vma=False,
    )
```

```python
import functools

import jax
import jax.numpy as jnp
from jax import lax
from jax.experimental import pallas as pl
from jax.experimental.pallas import tpu as pltpu
from jax.sharding import PartitionSpec as P

HD = 128
CORES = 2
COLUMNS = 2
LOG2_E = 1.4426950408889634
VMEM_LIMIT = 24 * 1024 * 1024


def attend_kernel(scale, halves, heads, first_column, length_ref, queries_ref, *rest):
    own_refs, piece_refs = rest[:4], rest[4 : 4 + len(halves)]
    out_ref, blocks_ref, sent_sems = rest[-3:]
    first, count = heads
    rows = queries_ref.shape[0]
    width = blocks_ref.shape[2]
    group = width // HD
    length = length_ref[...]
    query_at = lax.broadcasted_iota(jnp.int32, (rows, rows), 0)
    key_at = lax.broadcasted_iota(jnp.int32, (rows, rows), 1)
    seen = (key_at <= query_at) & (key_at < length)
    live = lax.broadcasted_iota(jnp.int32, (rows, HD), 0) < length

    def copied(h):
        target = out_ref.at[:, pl.ds(pl.multiple_of((first + h) * width, width), width)]
        return pltpu.make_async_copy(blocks_ref.at[h], target, sent_sems.at[h])

    def one_head(h, _):
        column = pl.ds(pl.multiple_of((first + h) * HD, HD), HD)
        local = pl.ds(pl.multiple_of((first + h) * HD - first_column, HD), HD)
        shared = [ref[:, local].reshape(-1, 2, half, HD) for ref, half in zip(piece_refs, halves)]
        keys = jnp.concatenate([ref[:, column] for ref in own_refs[::2]] + [one[:, 0].reshape(-1, HD) for one in shared])
        values = [ref[:, column] for ref in own_refs[1::2]] + [one[:, 1].reshape(-1, HD) for one in shared]
        values = jnp.concatenate(values)
        turned = keys.T

        def scored(g):
            asked = queries_ref[:, pl.ds(pl.multiple_of((first + h) * width + g * HD, HD), HD)]
            return jnp.dot(asked, turned, preferred_element_type=jnp.float32)

        def weighed(scores):
            scores = jnp.concatenate([jnp.where(seen, scores[:, :rows], -1e30), scores[:, rows:]], axis=1)
            top = jnp.max(scores, axis=1, keepdims=True)
            weights = jnp.exp2((scores - top) * scale)
            return weights.astype(jnp.bfloat16), jnp.sum(weights, axis=1, keepdims=True)

        def stored(g, weights, total):
            summed = jnp.dot(weights, values, preferred_element_type=jnp.float32)
            inverse = pl.reciprocal(total, approx=True)
            inverse *= 2.0 - total * inverse
            kept = jnp.where(live, summed * inverse, 0.0)
            blocks_ref[h, :, g * HD : (g + 1) * HD] = kept.astype(jnp.bfloat16)

        scores, weights = scored(0), None
        for g in range(group):
            ahead = scored(g + 1) if g + 1 < group else None
            if weights is not None:
                stored(g - 1, *weights)
            weights = weighed(scores)
            scores = ahead
        stored(group - 1, *weights)
        copied(h).start()
        return _

    lax.fori_loop(0, count, one_head, 0)
    for h in range(count):
        copied(h).wait()


def attend(queries, own, pieces, length, heads, first_column, kv_heads, begun=None):
    rows = queries.shape[0]
    width = queries.shape[1] // kv_heads
    count = heads[1]
    halves = [half for _, half in pieces]
    arrays = [array for array, _ in pieces]
    keys = sum(array.shape[0] for array in own[::2]) + sum(array.shape[0] for array in arrays) // 2
    operands = [length, queries, *own, *arrays]
    in_specs = [pl.BlockSpec(memory_space=pltpu.VMEM) for _ in operands]
    aliases = {}
    if begun is not None:
        aliases = {len(operands): 0}
        operands.append(begun)
        in_specs.append(pl.BlockSpec(memory_space=pl.ANY))
    return pl.pallas_call(
        functools.partial(attend_kernel, LOG2_E / HD**0.5, halves, heads, first_column * HD),
        in_specs=in_specs,
        out_specs=pl.BlockSpec(memory_space=pl.ANY),
        out_shape=jax.ShapeDtypeStruct(queries.shape, queries.dtype),
        scratch_shapes=[pltpu.VMEM((count, rows, width), queries.dtype), pltpu.SemaphoreType.DMA((count,))],
        input_output_aliases=aliases,
        compiler_params=pltpu.CompilerParams(vmem_limit_bytes=VMEM_LIMIT),
        cost_estimate=pl.CostEstimate(
            flops=4 * keys * rows * width * count,
            bytes_accessed=4 * rows * width * count,
            transcendentals=keys * rows * width // HD * count,
        ),
        name="attend_heads",
    )(*operands)


class Places:
    def __init__(self, devices):
        self.devices = devices
        self.levels = devices // (CORES * COLUMNS)

    def split(self, index):
        if isinstance(index, int):
            return index // (CORES * COLUMNS), index // CORES % COLUMNS, index % CORES
        chip = lax.div(index, CORES)
        return lax.div(chip, COLUMNS), lax.rem(chip, COLUMNS), lax.rem(index, CORES)

    def swapped(self, array, level=0, column=0, core=0):
        pairs = []
        for index in range(self.devices):
            z, y, c = self.split(index)
            z, y, c = z ^ level, y ^ column, c ^ core
            pairs.append((index, (z * COLUMNS + y) * CORES + c))
        return lax.ppermute(array, "ctx", pairs)

    def over_levels(self, array):
        return [array] + [self.swapped(array, level=s) for s in range(1, self.levels)]


def over_chips(places, rows):
    chips = [rows, places.swapped(rows, column=1)]
    return chips + [places.swapped(one, core=1) for one in chips]


def chosen(flag, mine, got, starts, sizes):
    return jnp.where(flag, lax.dynamic_slice(mine, starts, sizes), lax.dynamic_slice(got, starts, sizes))


def for_levels(places, part):
    z, _, _ = places.split(lax.axis_index("ctx"))
    rows = part.shape[1] // places.levels
    return [
        lax.dynamic_slice_in_dim(part, (z ^ s) * rows, rows, 1).reshape(2 * rows, -1) for s in range(places.levels)
    ]


def from_owner(distance, mine, got):
    piece = mine
    for s, one in enumerate(got, 1):
        piece = jnp.where(distance == s, one, piece)
    return piece


def owned_rows(pool, owners):
    owned = (owners == lax.axis_index("ctx"))[:, None, None]
    return lax.psum(jnp.where(owned, pool[0], 0), "ctx").reshape(-1, pool.shape[-1])


def body(queries, new_keys, new_values, prefix_keys, prefix_values, pool_keys, pool_values, owners, lengths, devices):
    kv_heads = new_keys.shape[1] // HD
    blocks, block_rows = pool_keys.shape[1:3]
    length = jnp.broadcast_to(lengths[:, None], (1, HD))
    chips = devices // CORES
    levels = chips // COLUMNS
    by_permutes = (
        blocks == CORES
        and chips % COLUMNS == 0
        and levels > 1
        and levels & (levels - 1) == 0
        and block_rows % (16 * chips) == 0
        and kv_heads % 2 == 0
    )
    if not by_permutes:
        pre_k, pre_v = (lax.all_gather(rows, "ctx", axis=0, tiled=True) for rows in (prefix_keys, prefix_values))
        shared = jnp.concatenate([owned_rows(pool_keys, owners), owned_rows(pool_values, owners)])
        pieces = [(shared, shared.shape[0] // 2)]
        own = (new_keys, new_values, pre_k, pre_v)
        return attend(queries, own, pieces, length, (0, kv_heads), 0, kv_heads)
    places = Places(devices)
    z, y, c = places.split(lax.axis_index("ctx"))
    owner = jnp.where(c == 0, owners[0], owners[1])
    owner_z, owner_y, owner_c = places.split(owner)
    pools = [(pool[0], places.swapped(pool[0], core=1)) for pool in (pool_keys, pool_values)]
    count = kv_heads // 2
    part = block_rows // COLUMNS
    tied = lax.optimization_barrier

    def cut(pools, column, first):
        sizes = (1, part, count * HD)
        rows = [chosen(owner_c == c, *pool, (c, column * part, first * HD), sizes) for pool in pools]
        return jnp.concatenate(rows)

    sent = [cut(pools, 1 - y, 0)]
    sent[0], pools = tied((sent[0], pools))
    sent.append(cut(pools, 1 - y, count))
    prefix, sent[1] = tied((jnp.concatenate([prefix_keys, prefix_values]), sent[1]))
    got = [places.swapped(one, column=1) for one in sent]
    step = 1
    while step < levels:
        prefix = [prefix, places.swapped(prefix, level=step)]
        step *= 2
        prefix = jnp.concatenate(prefix) if step < levels else prefix

    def over_z(cuts):
        return [places.swapped(one, level=s) for s, one in enumerate(cuts) if s]

    first_cuts = for_levels(places, jnp.where(owner_y == y, cut(pools, y, 0), got[0]))
    first_got = over_z(first_cuts)
    last_cuts = for_levels(places, jnp.where(owner_y == y, cut(pools, y, count), got[1]))
    last_got = over_z(last_cuts)
    prefix, last_cuts[0] = tied((prefix, last_cuts[0]))
    prefix = jnp.concatenate(prefix)
    prefix = [prefix, places.swapped(prefix, column=1)]
    pieces = [from_owner(z ^ owner_z, *one) for one in ((first_cuts[0], first_got), (last_cuts[0], last_got))]
    prefix, pieces[1] = tied((prefix, pieces[1]))
    joined = [jnp.concatenate(places.over_levels(one)) for one in pieces]
    prefix = jnp.concatenate(prefix + [places.swapped(one, core=1) for one in prefix])
    prefix = prefix.reshape(devices, 2, -1, prefix.shape[-1])
    own = (new_keys, new_values) + tuple(prefix[:, i].reshape(-1, prefix.shape[-1]) for i in range(2))
    half = pieces[0].shape[0] // 2
    across = [places.swapped(one, column=1) for one in joined]
    other = [places.swapped(one, core=1) for one in joined]
    first = [(at, half) for at in (joined[0], other[0], across[0], places.swapped(across[0], core=1))]
    out = attend(queries, own, first, length, (0, count - 1), 0, kv_heads)
    across[1], out = tied((across[1], out))
    last = [(at, half) for at in (joined[1], other[1], across[1], places.swapped(across[1], core=1))]
    out = attend(queries, own, first, length, (count - 1, 1), 0, kv_heads, begun=out)
    return attend(queries, own, last, length, (count, kv_heads - count), count, kv_heads, begun=out)


def solution(mesh):
    both = ("groups", "ctx")
    placed = (P(both, None),) * 5 + (P(both, None, None, None),) * 2 + (P("groups"), P(both))
    return jax.shard_map(
        functools.partial(body, devices=mesh.shape["ctx"]),
        mesh=mesh,
        in_specs=placed,
        out_specs=P(both, None),
        check_vma=False,
    )
```

```python
import functools

import jax
import jax.numpy as jnp
from jax import lax
from jax.experimental import pallas as pl
from jax.experimental.pallas import tpu as pltpu
from jax.sharding import PartitionSpec as P

HD = 128
CORES = 2
COLUMNS = 2
LOG2_E = 1.4426950408889634
VMEM_LIMIT = 24 * 1024 * 1024


def attend_kernel(scale, groups, has_own, goes_on, ends, width, length_ref, queries_ref, *rest):
    rest = list(rest)
    own_refs = [rest.pop(0) for _ in range(4 if has_own else 0)]
    piece_refs = [[rest.pop(0) for _ in halves] for _, _, halves in groups]
    state_refs = [rest.pop(0) for _ in range(2 if goes_on else 0)]
    if ends:
        out_ref, blocks_ref, sent_sems = rest[-3:]
    else:
        products_ref, statistics_ref = rest[-2:]
    rows = queries_ref.shape[0]
    heads_each = width // HD
    length = length_ref[...]
    query_at = lax.broadcasted_iota(jnp.int32, (rows, rows), 0)
    key_at = lax.broadcasted_iota(jnp.int32, (rows, rows), 1)
    seen = (key_at <= query_at) & (key_at < length)
    live = lax.broadcasted_iota(jnp.int32, (rows, HD), 0) < length
    lane = lax.broadcasted_iota(jnp.int32, (rows, HD), 1)

    def at_lanes(start, size):
        return pl.ds(pl.multiple_of(start, HD), size)

    def copied(slot, h):
        target = out_ref.at[:, at_lanes(h * width, width)]
        return pltpu.make_async_copy(blocks_ref.at[slot], target, sent_sems.at[slot])

    def one_head(h, first, slot, refs, halves):
        column, local = at_lanes(h * HD, HD), at_lanes((h - first) * HD, HD)
        shared = [ref[:, local].reshape(-1, 2, half, HD) for ref, half in zip(refs, halves)]
        keys = [ref[:, column] for ref in own_refs[::2]] + [one[:, 0].reshape(-1, HD) for one in shared]
        values = [ref[:, column] for ref in own_refs[1::2]] + [one[:, 1].reshape(-1, HD) for one in shared]
        turned, values = jnp.concatenate(keys).T, jnp.concatenate(values)
        before = state_refs[1][h] if goes_on else None
        statistics = jnp.zeros((rows, HD), jnp.float32)

        def at_query(g):
            return at_lanes(h * width + g * HD, HD)

        def scored(g):
            return jnp.dot(queries_ref[:, at_query(g)], turned, preferred_element_type=jnp.float32)

        def weighed(g, scores):
            if has_own:
                scores = jnp.concatenate([jnp.where(seen, scores[:, :rows], -1e30), scores[:, rows:]], axis=1)
            top = jnp.max(scores, axis=1, keepdims=True)
            if goes_on:
                top = jnp.maximum(before[:, g : g + 1], top)
            weights = jnp.exp2((scores - top) * scale)
            return weights.astype(jnp.bfloat16), jnp.sum(weights, axis=1, keepdims=True), top

        def stored(g, weights, total, top):
            summed = jnp.dot(weights, values, preferred_element_type=jnp.float32)
            if goes_on:
                shrink = jnp.exp2((before[:, g : g + 1] - top) * scale)
                total += before[:, HD // 2 + g : HD // 2 + g + 1] * shrink
                summed += state_refs[0][:, at_query(g)] * shrink
            if ends:
                inverse = pl.reciprocal(total, approx=True)
                inverse *= 2.0 - total * inverse
                kept = jnp.where(live, summed * inverse, 0.0)
                blocks_ref[slot, :, g * HD : (g + 1) * HD] = kept.astype(jnp.bfloat16)
            else:
                products_ref[:, at_query(g)] = summed

        scores, weights = scored(0), None
        for g in range(heads_each):
            ahead = scored(g + 1) if g + 1 < heads_each else None
            if weights is not None:
                stored(g - 1, *weights)
            weights = weighed(g, scores)
            if not ends:
                statistics = jnp.where(lane == g, weights[2], statistics)
                statistics = jnp.where(lane == HD // 2 + g, weights[1], statistics)
            scores = ahead
        stored(heads_each - 1, *weights)
        if ends:
            copied(slot, h).start()
        else:
            statistics_ref[h] = statistics

    done = 0
    for (first, count, halves), refs in zip(groups, piece_refs):

        def step(i, carry, first=first, done=done, refs=refs, halves=halves):
            one_head(first + i, first, done + i, refs, halves)
            return carry

        lax.fori_loop(0, count, step, 0)
        done += count
    if ends:
        done = 0
        for first, count, _ in groups:
            for i in range(count):
                copied(done + i, first + i).wait()
            done += count


def attend(queries, own, groups, length, kv_heads, state=(), begun=None, ends=True):
    rows = queries.shape[0]
    width = queries.shape[1] // kv_heads
    heads = sum(count for _, count, _ in groups)
    shapes = [(first, count, [half for _, half in pieces]) for first, count, pieces in groups]
    operands = [length, queries, *own] + [array for _, _, pieces in groups for array, _ in pieces] + list(state)
    in_specs = [pl.BlockSpec(memory_space=pltpu.VMEM) for _ in operands]
    keys = sum(array.shape[0] for array in own[::2]) + sum(array.shape[0] for array, _ in groups[0][2]) // 2
    aliases = {}
    if begun is not None:
        aliases = {len(operands): 0}
        operands.append(begun)
        in_specs.append(pl.BlockSpec(memory_space=pl.ANY))
    if ends:
        out_specs = pl.BlockSpec(memory_space=pl.ANY)
        out_shape = jax.ShapeDtypeStruct(queries.shape, queries.dtype)
        scratch = [pltpu.VMEM((heads, rows, width), queries.dtype), pltpu.SemaphoreType.DMA((heads,))]
    else:
        out_specs = [pl.BlockSpec(memory_space=pltpu.VMEM)] * 2
        out_shape = [
            jax.ShapeDtypeStruct(queries.shape, jnp.float32),
            jax.ShapeDtypeStruct((kv_heads, rows, HD), jnp.float32),
        ]
        scratch = []
    return pl.pallas_call(
        functools.partial(
            attend_kernel, LOG2_E / HD**0.5, shapes, bool(own), bool(state), ends, width
        ),
        in_specs=in_specs,
        out_specs=out_specs,
        out_shape=out_shape,
        scratch_shapes=scratch,
        input_output_aliases=aliases,
        compiler_params=pltpu.CompilerParams(vmem_limit_bytes=VMEM_LIMIT),
        cost_estimate=pl.CostEstimate(
            flops=4 * keys * rows * width * heads,
            bytes_accessed=4 * rows * width * heads,
            transcendentals=keys * rows * width // HD * heads,
        ),
        name="attend_heads",
    )(*operands)


class Places:
    def __init__(self, devices):
        self.devices = devices
        self.levels = devices // (CORES * COLUMNS)

    def split(self, index):
        if isinstance(index, int):
            return index // (CORES * COLUMNS), index // CORES % COLUMNS, index % CORES
        chip = lax.div(index, CORES)
        return lax.div(chip, COLUMNS), lax.rem(chip, COLUMNS), lax.rem(index, CORES)

    def swapped(self, array, level=0, column=0, core=0):
        pairs = []
        for index in range(self.devices):
            z, y, c = self.split(index)
            z, y, c = z ^ level, y ^ column, c ^ core
            pairs.append((index, (z * COLUMNS + y) * CORES + c))
        return lax.ppermute(array, "ctx", pairs)

    def over_levels(self, array):
        return [array] + [self.swapped(array, level=s) for s in range(1, self.levels)]


def over_chips(places, rows):
    chips = [rows, places.swapped(rows, column=1)]
    return chips + [places.swapped(one, core=1) for one in chips]


def chosen(flag, mine, got, starts, sizes):
    return jnp.where(flag, lax.dynamic_slice(mine, starts, sizes), lax.dynamic_slice(got, starts, sizes))


def for_levels(places, part):
    z, _, _ = places.split(lax.axis_index("ctx"))
    rows = part.shape[1] // places.levels
    return [
        lax.dynamic_slice_in_dim(part, (z ^ s) * rows, rows, 1).reshape(2 * rows, -1) for s in range(places.levels)
    ]


def from_owner(distance, mine, got):
    piece = mine
    for s, one in enumerate(got, 1):
        piece = jnp.where(distance == s, one, piece)
    return piece


def owned_rows(pool, owners):
    owned = (owners == lax.axis_index("ctx"))[:, None, None]
    return lax.psum(jnp.where(owned, pool[0], 0), "ctx").reshape(-1, pool.shape[-1])


def body(queries, new_keys, new_values, prefix_keys, prefix_values, pool_keys, pool_values, owners, lengths, devices):
    kv_heads = new_keys.shape[1] // HD
    blocks, block_rows = pool_keys.shape[1:3]
    length = jnp.broadcast_to(lengths[:, None], (1, HD))
    chips = devices // CORES
    levels = chips // COLUMNS
    by_permutes = (
        blocks == CORES
        and chips % COLUMNS == 0
        and levels > 1
        and levels & (levels - 1) == 0
        and block_rows % (16 * chips) == 0
        and kv_heads % 2 == 0
    )
    if not by_permutes:
        pre_k, pre_v = (lax.all_gather(rows, "ctx", axis=0, tiled=True) for rows in (prefix_keys, prefix_values))
        shared = jnp.concatenate([owned_rows(pool_keys, owners), owned_rows(pool_values, owners)])
        pieces = [(shared, shared.shape[0] // 2)]
        own = (new_keys, new_values, pre_k, pre_v)
        return attend(queries, own, [(0, kv_heads, pieces)], length, kv_heads)
    places = Places(devices)
    z, y, c = places.split(lax.axis_index("ctx"))
    owner = jnp.where(c == 0, owners[0], owners[1])
    owner_z, owner_y, owner_c = places.split(owner)
    pools = [(pool[0], places.swapped(pool[0], core=1)) for pool in (pool_keys, pool_values)]
    count = kv_heads // 2
    part = block_rows // COLUMNS
    tied = lax.optimization_barrier

    def cut(pools, column, first):
        sizes = (1, part, count * HD)
        rows = [chosen(owner_c == c, *pool, (c, column * part, first * HD), sizes) for pool in pools]
        return jnp.concatenate(rows)

    sent = [cut(pools, 1 - y, 0)]
    sent[0], pools = tied((sent[0], pools))
    sent.append(cut(pools, 1 - y, count))
    prefix, sent[1] = tied((jnp.concatenate([prefix_keys, prefix_values]), sent[1]))
    got = [places.swapped(one, column=1) for one in sent]
    step = 1
    while step < levels:
        prefix = [prefix, places.swapped(prefix, level=step)]
        step *= 2
        prefix = jnp.concatenate(prefix) if step < levels else prefix

    def over_z(cuts):
        return [places.swapped(one, level=s) for s, one in enumerate(cuts) if s]

    first_cuts = for_levels(places, jnp.where(owner_y == y, cut(pools, y, 0), got[0]))
    first_got = over_z(first_cuts)
    last_cuts = for_levels(places, jnp.where(owner_y == y, cut(pools, y, count), got[1]))
    last_got = over_z(last_cuts)
    prefix, last_cuts[0] = tied((prefix, last_cuts[0]))
    prefix = jnp.concatenate(prefix)
    prefix = [prefix, places.swapped(prefix, column=1)]
    pieces = [from_owner(z ^ owner_z, *one) for one in ((first_cuts[0], first_got), (last_cuts[0], last_got))]
    prefix, pieces[1] = tied((prefix, pieces[1]))
    rows = [places.over_levels(one) for one in pieces]
    prefix = jnp.concatenate(prefix + [places.swapped(one, core=1) for one in prefix])
    prefix = prefix.reshape(devices, 2, -1, prefix.shape[-1])
    own = (new_keys, new_values) + tuple(prefix[:, i].reshape(-1, prefix.shape[-1]) for i in range(2))
    half = pieces[0].shape[0] // 2
    firsts, counts = (0, count), (count, kv_heads - count)

    def grouped(at, mine):
        return firsts[at], counts[at], [(mine, half), (places.swapped(mine, core=1), half)]

    def begin(at, joined):
        return attend(queries, own, [grouped(at, joined)], length, kv_heads, ends=False)

    def end(at, across, state, out):
        return attend(queries, (), [grouped(at, across)], length, kv_heads, state, out)

    joined = jnp.concatenate(rows[0])
    across = places.swapped(joined, column=1)
    state = begin(0, joined)
    rows[1], state = tied((rows[1], state))
    joined = jnp.concatenate(rows[1])
    last_across = places.swapped(joined, column=1)
    last_state = begin(1, joined)
    last_across, last_state = tied((last_across, last_state))
    out = end(0, across, state, None)

    return end(1, last_across, last_state, out)


def solution(mesh):
    both = ("groups", "ctx")
    placed = (P(both, None),) * 5 + (P(both, None, None, None),) * 2 + (P("groups"), P(both))
    return jax.shard_map(
        functools.partial(body, devices=mesh.shape["ctx"]),
        mesh=mesh,
        in_specs=placed,
        out_specs=P(both, None),
        check_vma=False,
    )
```

```python
import functools

import jax
import jax.numpy as jnp
from jax import lax
from jax.experimental import pallas as pl
from jax.experimental.pallas import tpu as pltpu
from jax.sharding import PartitionSpec as P

HD = 128
CORES = 2
COLUMNS = 2
LOG2_E = 1.4426950408889634
VMEM_LIMIT = 24 * 1024 * 1024


def attend_kernel(scale, halves, heads, first_column, length_ref, queries_ref, *rest):
    own_refs, piece_refs = rest[:4], rest[4 : 4 + len(halves)]
    out_ref, blocks_ref, sent_sems = rest[-3:]
    first, count = heads
    rows = queries_ref.shape[0]
    width = blocks_ref.shape[2]
    group = width // HD
    length = length_ref[...]
    query_at = lax.broadcasted_iota(jnp.int32, (rows, rows), 0)
    key_at = lax.broadcasted_iota(jnp.int32, (rows, rows), 1)
    seen = (key_at <= query_at) & (key_at < length)
    live = lax.broadcasted_iota(jnp.int32, (rows, HD), 0) < length

    def copied(h):
        target = out_ref.at[:, pl.ds(pl.multiple_of((first + h) * width, width), width)]
        return pltpu.make_async_copy(blocks_ref.at[h], target, sent_sems.at[h])

    def one_head(h, _):
        column = pl.ds(pl.multiple_of((first + h) * HD, HD), HD)
        local = pl.ds(pl.multiple_of((first + h) * HD - first_column, HD), HD)
        shared = [ref[:, local].reshape(-1, 2, half, HD) for ref, half in zip(piece_refs, halves)]
        keys = jnp.concatenate([ref[:, column] for ref in own_refs[::2]] + [one[:, 0].reshape(-1, HD) for one in shared])
        values = [ref[:, column] for ref in own_refs[1::2]] + [one[:, 1].reshape(-1, HD) for one in shared]
        values = jnp.concatenate(values)
        turned = keys.T

        def scored(g):
            asked = queries_ref[:, pl.ds(pl.multiple_of((first + h) * width + g * HD, HD), HD)]
            return jnp.dot(asked, turned, preferred_element_type=jnp.float32)

        def weighed(scores):
            scores = jnp.concatenate([jnp.where(seen, scores[:, :rows], -1e30), scores[:, rows:]], axis=1)
            top = jnp.max(scores, axis=1, keepdims=True)
            weights = jnp.exp2((scores - top) * scale)
            return weights.astype(jnp.bfloat16), jnp.sum(weights, axis=1, keepdims=True)

        def stored(g, weights, total):
            summed = jnp.dot(weights, values, preferred_element_type=jnp.float32)
            inverse = pl.reciprocal(total, approx=True)
            inverse *= 2.0 - total * inverse
            kept = jnp.where(live, summed * inverse, 0.0)
            blocks_ref[h, :, g * HD : (g + 1) * HD] = kept.astype(jnp.bfloat16)

        scores, weights = scored(0), None
        for g in range(group):
            ahead = scored(g + 1) if g + 1 < group else None
            if weights is not None:
                stored(g - 1, *weights)
            weights = weighed(scores)
            scores = ahead
        stored(group - 1, *weights)
        copied(h).start()
        return _

    lax.fori_loop(0, count, one_head, 0)
    for h in range(count):
        copied(h).wait()


def attend(queries, own, pieces, length, heads, first_column, kv_heads, begun=None):
    rows = queries.shape[0]
    width = queries.shape[1] // kv_heads
    count = heads[1]
    halves = [half for _, half in pieces]
    arrays = [array for array, _ in pieces]
    keys = sum(array.shape[0] for array in own[::2]) + sum(array.shape[0] for array in arrays) // 2
    operands = [length, queries, *own, *arrays]
    in_specs = [pl.BlockSpec(memory_space=pltpu.VMEM) for _ in operands]
    aliases = {}
    if begun is not None:
        aliases = {len(operands): 0}
        operands.append(begun)
        in_specs.append(pl.BlockSpec(memory_space=pl.ANY))
    return pl.pallas_call(
        functools.partial(attend_kernel, LOG2_E / HD**0.5, halves, heads, first_column * HD),
        in_specs=in_specs,
        out_specs=pl.BlockSpec(memory_space=pl.ANY),
        out_shape=jax.ShapeDtypeStruct(queries.shape, queries.dtype),
        scratch_shapes=[pltpu.VMEM((count, rows, width), queries.dtype), pltpu.SemaphoreType.DMA((count,))],
        input_output_aliases=aliases,
        compiler_params=pltpu.CompilerParams(vmem_limit_bytes=VMEM_LIMIT),
        cost_estimate=pl.CostEstimate(
            flops=4 * keys * rows * width * count,
            bytes_accessed=4 * rows * width * count,
            transcendentals=keys * rows * width // HD * count,
        ),
        name="attend_heads",
    )(*operands)


class Places:
    def __init__(self, devices):
        self.devices = devices
        self.levels = devices // (CORES * COLUMNS)

    def split(self, index):
        if isinstance(index, int):
            return index // (CORES * COLUMNS), index // CORES % COLUMNS, index % CORES
        chip = lax.div(index, CORES)
        return lax.div(chip, COLUMNS), lax.rem(chip, COLUMNS), lax.rem(index, CORES)

    def swapped(self, array, level=0, column=0, core=0):
        pairs = []
        for index in range(self.devices):
            z, y, c = self.split(index)
            z, y, c = z ^ level, y ^ column, c ^ core
            pairs.append((index, (z * COLUMNS + y) * CORES + c))
        return lax.ppermute(array, "ctx", pairs)

    def over_levels(self, array):
        return [array] + [self.swapped(array, level=s) for s in range(1, self.levels)]


def over_chips(places, rows):
    chips = [rows, places.swapped(rows, column=1)]
    return chips + [places.swapped(one, core=1) for one in chips]


def chosen(flag, mine, got, starts, sizes):
    return jnp.where(flag, lax.dynamic_slice(mine, starts, sizes), lax.dynamic_slice(got, starts, sizes))


def for_levels(places, part):
    z, _, _ = places.split(lax.axis_index("ctx"))
    rows = part.shape[1] // places.levels
    return [
        lax.dynamic_slice_in_dim(part, (z ^ s) * rows, rows, 1).reshape(2 * rows, -1) for s in range(places.levels)
    ]


def from_owner(distance, mine, got):
    piece = mine
    for s, one in enumerate(got, 1):
        piece = jnp.where(distance == s, one, piece)
    return piece


def owned_rows(pool, owners):
    owned = (owners == lax.axis_index("ctx"))[:, None, None]
    return lax.psum(jnp.where(owned, pool[0], 0), "ctx").reshape(-1, pool.shape[-1])


def body(queries, new_keys, new_values, prefix_keys, prefix_values, pool_keys, pool_values, owners, lengths, devices):
    kv_heads = new_keys.shape[1] // HD
    blocks, block_rows = pool_keys.shape[1:3]
    length = jnp.broadcast_to(lengths[:, None], (1, HD))
    chips = devices // CORES
    levels = chips // COLUMNS
    by_permutes = (
        blocks == CORES
        and chips % COLUMNS == 0
        and levels > 1
        and levels & (levels - 1) == 0
        and block_rows % (16 * chips) == 0
        and kv_heads % 2 == 0
    )
    if not by_permutes:
        pre_k, pre_v = (lax.all_gather(rows, "ctx", axis=0, tiled=True) for rows in (prefix_keys, prefix_values))
        shared = jnp.concatenate([owned_rows(pool_keys, owners), owned_rows(pool_values, owners)])
        pieces = [(shared, shared.shape[0] // 2)]
        own = (new_keys, new_values, pre_k, pre_v)
        return attend(queries, own, pieces, length, (0, kv_heads), 0, kv_heads)
    places = Places(devices)
    z, y, c = places.split(lax.axis_index("ctx"))
    owner = jnp.where(c == 0, owners[0], owners[1])
    owner_z, owner_y, owner_c = places.split(owner)
    pools = [(pool[0], places.swapped(pool[0], core=1)) for pool in (pool_keys, pool_values)]
    count = kv_heads // 2
    part = block_rows // COLUMNS
    tied = lax.optimization_barrier

    def cut(pools, column, first):
        sizes = (1, part, count * HD)
        rows = [chosen(owner_c == c, *pool, (c, column * part, first * HD), sizes) for pool in pools]
        return jnp.concatenate(rows)

    sent = [cut(pools, 1 - y, 0)]
    sent[0], pools = tied((sent[0], pools))
    sent.append(cut(pools, 1 - y, count))
    prefix, sent[1] = tied((jnp.concatenate([prefix_keys, prefix_values]), sent[1]))
    got = [places.swapped(one, column=1) for one in sent]
    step = 1
    while step < levels:
        prefix = [prefix, places.swapped(prefix, level=step)]
        step *= 2
        prefix = jnp.concatenate(prefix) if step < levels else prefix

    def over_z(cuts):
        return [places.swapped(one, level=s) for s, one in enumerate(cuts) if s]

    first_cuts = for_levels(places, jnp.where(owner_y == y, cut(pools, y, 0), got[0]))
    first_got = over_z(first_cuts)
    last_cuts = for_levels(places, jnp.where(owner_y == y, cut(pools, y, count), got[1]))
    last_got = over_z(last_cuts)
    prefix, last_cuts[0] = tied((prefix, last_cuts[0]))
    prefix = jnp.concatenate(prefix)
    prefix = [prefix, places.swapped(prefix, column=1)]
    pieces = [from_owner(z ^ owner_z, *one) for one in ((first_cuts[0], first_got), (last_cuts[0], last_got))]
    prefix, pieces[1] = tied((prefix, pieces[1]))
    early = places.swapped(pieces[0], column=1)
    early, pieces[1] = tied((early, pieces[1]))
    early = [early, places.swapped(pieces[1], column=1)]
    gathered = [places.over_levels(one) for one in pieces]
    early[1], gathered[0] = tied((early[1], gathered[0]))
    across = [places.swapped(jnp.concatenate(gathered[0][1:]), column=1)]
    prefix, early, gathered[1] = tied((prefix, early, gathered[1]))
    across.append(places.swapped(jnp.concatenate(gathered[1][1:]), column=1))
    mine = [jnp.concatenate(rows + [one]) for rows, one in zip(gathered, early)]
    other = [places.swapped(one, core=1) for one in mine]
    prefix = jnp.concatenate(prefix)
    prefix = jnp.concatenate([prefix, places.swapped(prefix, core=1)])
    prefix = prefix.reshape(devices, 2, -1, prefix.shape[-1])
    own = (new_keys, new_values) + tuple(prefix[:, i].reshape(-1, prefix.shape[-1]) for i in range(2))
    half = pieces[0].shape[0] // 2

    def arrived(at):
        rows = (mine[at], other[at], across[at], places.swapped(across[at], core=1))
        return [(one, half) for one in rows]

    first = arrived(0)
    out = attend(queries, own, first, length, (0, count - 1), 0, kv_heads)
    across[1], out = tied((across[1], out))
    last = arrived(1)
    out = attend(queries, own, first, length, (count - 1, 1), 0, kv_heads, begun=out)
    return attend(queries, own, last, length, (count, kv_heads - count), count, kv_heads, begun=out)


def solution(mesh):
    both = ("groups", "ctx")
    placed = (P(both, None),) * 5 + (P(both, None, None, None),) * 2 + (P("groups"), P(both))
    return jax.shard_map(
        functools.partial(body, devices=mesh.shape["ctx"]),
        mesh=mesh,
        in_specs=placed,
        out_specs=P(both, None),
        check_vma=False,
    )
```

```python
import functools

import jax
import jax.numpy as jnp
from jax import lax
from jax.experimental import pallas as pl
from jax.experimental.pallas import tpu as pltpu
from jax.sharding import PartitionSpec as P

HD = 128
CORES = 2
COLUMNS = 2
LOG2_E = 1.4426950408889634
VMEM_LIMIT = 24 * 1024 * 1024


def attend_kernel(scale, groups, has_own, goes_on, ends, width, length_ref, queries_ref, *rest):
    rest = list(rest)
    own_refs = [rest.pop(0) for _ in range(4 if has_own else 0)]
    piece_refs = [[rest.pop(0) for _ in halves] for *_, halves in groups]
    state_refs = [rest.pop(0) for _ in range(3 if goes_on else 0)]
    if ends:
        out_ref, blocks_ref, sent_sems = rest[-3:]
    else:
        products_ref, maxima_ref, sums_ref = rest[-3:]
    rows = queries_ref.shape[0]
    heads_each = width // HD
    length = length_ref[...]
    query_at = lax.broadcasted_iota(jnp.int32, (rows, rows), 0)
    key_at = lax.broadcasted_iota(jnp.int32, (rows, rows), 1)
    seen = (key_at <= query_at) & (key_at < length)
    live = lax.broadcasted_iota(jnp.int32, (rows, HD), 0) < length

    def at_lanes(start, size):
        return pl.ds(pl.multiple_of(start, HD), size)

    def copied(slot, h):
        target = out_ref.at[:, at_lanes(h * width, width)]
        return pltpu.make_async_copy(blocks_ref.at[slot], target, sent_sems.at[slot])

    def one_head(h, base, slot, refs, halves):
        column, local = at_lanes(h * HD, HD), at_lanes((h - base) * HD, HD)
        shared = [ref[:, local].reshape(-1, 2, half, HD) for ref, half in zip(refs, halves)]
        keys = [ref[:, column] for ref in own_refs[::2]] + [one[:, 0].reshape(-1, HD) for one in shared]
        values = [ref[:, column] for ref in own_refs[1::2]] + [one[:, 1].reshape(-1, HD) for one in shared]
        turned, values = jnp.concatenate(keys).T, jnp.concatenate(values)

        def at_query(g):
            return at_lanes(h * width + g * HD, HD)

        def scored(g):
            return jnp.dot(queries_ref[:, at_query(g)], turned, preferred_element_type=jnp.float32)

        def weighed(g, scores):
            if has_own:
                scores = jnp.concatenate([jnp.where(seen, scores[:, :rows], -1e30), scores[:, rows:]], axis=1)
            top = jnp.broadcast_to(jnp.max(scores, axis=1, keepdims=True), (rows, HD))
            if goes_on:
                top = jnp.maximum(state_refs[1][:, at_query(g)], top)
            wide = jnp.concatenate([top] * (scores.shape[1] // HD), axis=1)
            weights = jnp.exp2((scores - wide) * scale)
            total = jnp.broadcast_to(jnp.sum(weights, axis=1, keepdims=True), (rows, HD))
            return weights.astype(jnp.bfloat16), total, top

        def stored(g, weights, total, top):
            summed = jnp.dot(weights, values, preferred_element_type=jnp.float32)
            if goes_on:
                shrink = jnp.exp2((state_refs[1][:, at_query(g)] - top) * scale)
                total += state_refs[2][:, at_query(g)] * shrink
                summed += state_refs[0][:, at_query(g)] * shrink
            if ends:
                inverse = pl.reciprocal(total, approx=True)
                inverse *= 2.0 - total * inverse
                kept = jnp.where(live, summed * inverse, 0.0)
                blocks_ref[slot, :, g * HD : (g + 1) * HD] = kept.astype(jnp.bfloat16)
            else:
                products_ref[:, at_query(g)] = summed
                maxima_ref[:, at_query(g)] = top
                sums_ref[:, at_query(g)] = total

        scores, weights = scored(0), None
        for g in range(heads_each):
            ahead = scored(g + 1) if g + 1 < heads_each else None
            if weights is not None:
                stored(g - 1, *weights)
            weights = weighed(g, scores)
            scores = ahead
        stored(heads_each - 1, *weights)
        if ends:
            copied(slot, h).start()

    done = 0
    for (first, count, base, halves), refs in zip(groups, piece_refs):

        def step(i, carry, first=first, base=base, done=done, refs=refs, halves=halves):
            one_head(first + i, base, done + i, refs, halves)
            return carry

        lax.fori_loop(0, count, step, 0)
        done += count
    if ends:
        done = 0
        for first, count, *_ in groups:
            for i in range(count):
                copied(done + i, first + i).wait()
            done += count


def attend(queries, own, groups, length, kv_heads, state=(), begun=None, ends=True):
    rows = queries.shape[0]
    width = queries.shape[1] // kv_heads
    heads = sum(group[1] for group in groups)
    shapes = [(*group[:3], [half for _, half in group[3]]) for group in groups]
    operands = [length, queries, *own] + [array for group in groups for array, _ in group[3]] + list(state)
    in_specs = [pl.BlockSpec(memory_space=pltpu.VMEM) for _ in operands]
    keys = sum(array.shape[0] for array in own[::2]) + sum(array.shape[0] for array, _ in groups[0][3]) // 2
    aliases = {}
    if begun is not None:
        aliases = {len(operands): 0}
        operands.append(begun)
        in_specs.append(pl.BlockSpec(memory_space=pl.ANY))
    if ends:
        out_specs = pl.BlockSpec(memory_space=pl.ANY)
        out_shape = jax.ShapeDtypeStruct(queries.shape, queries.dtype)
        scratch = [pltpu.VMEM((heads, rows, width), queries.dtype), pltpu.SemaphoreType.DMA((heads,))]
    else:
        out_specs = [pl.BlockSpec(memory_space=pltpu.VMEM)] * 3
        out_shape = [jax.ShapeDtypeStruct(queries.shape, jnp.float32)] * 3
        scratch = []
    return pl.pallas_call(
        functools.partial(
            attend_kernel, LOG2_E / HD**0.5, shapes, bool(own), bool(state), ends, width
        ),
        in_specs=in_specs,
        out_specs=out_specs,
        out_shape=out_shape,
        scratch_shapes=scratch,
        input_output_aliases=aliases,
        compiler_params=pltpu.CompilerParams(vmem_limit_bytes=VMEM_LIMIT),
        cost_estimate=pl.CostEstimate(
            flops=4 * keys * rows * width * heads,
            bytes_accessed=4 * rows * width * heads,
            transcendentals=keys * rows * width // HD * heads,
        ),
        name="attend_heads",
    )(*operands)


class Places:
    def __init__(self, devices):
        self.devices = devices
        self.levels = devices // (CORES * COLUMNS)

    def split(self, index):
        if isinstance(index, int):
            return index // (CORES * COLUMNS), index // CORES % COLUMNS, index % CORES
        chip = lax.div(index, CORES)
        return lax.div(chip, COLUMNS), lax.rem(chip, COLUMNS), lax.rem(index, CORES)

    def swapped(self, array, level=0, column=0, core=0):
        pairs = []
        for index in range(self.devices):
            z, y, c = self.split(index)
            z, y, c = z ^ level, y ^ column, c ^ core
            pairs.append((index, (z * COLUMNS + y) * CORES + c))
        return lax.ppermute(array, "ctx", pairs)

    def over_levels(self, array):
        return [array] + [self.swapped(array, level=s) for s in range(1, self.levels)]


def over_chips(places, rows):
    chips = [rows, places.swapped(rows, column=1)]
    return chips + [places.swapped(one, core=1) for one in chips]


def chosen(flag, mine, got, starts, sizes):
    return jnp.where(flag, lax.dynamic_slice(mine, starts, sizes), lax.dynamic_slice(got, starts, sizes))


def for_levels(places, part):
    z, _, _ = places.split(lax.axis_index("ctx"))
    rows = part.shape[1] // places.levels
    return [
        lax.dynamic_slice_in_dim(part, (z ^ s) * rows, rows, 1).reshape(2 * rows, -1) for s in range(places.levels)
    ]


def from_owner(distance, mine, got):
    piece = mine
    for s, one in enumerate(got, 1):
        piece = jnp.where(distance == s, one, piece)
    return piece


def owned_rows(pool, owners):
    owned = (owners == lax.axis_index("ctx"))[:, None, None]
    return lax.psum(jnp.where(owned, pool[0], 0), "ctx").reshape(-1, pool.shape[-1])


def body(queries, new_keys, new_values, prefix_keys, prefix_values, pool_keys, pool_values, owners, lengths, devices):
    kv_heads = new_keys.shape[1] // HD
    blocks, block_rows = pool_keys.shape[1:3]
    length = jnp.broadcast_to(lengths[:, None], (1, HD))
    chips = devices // CORES
    levels = chips // COLUMNS
    by_permutes = (
        blocks == CORES
        and chips % COLUMNS == 0
        and levels > 1
        and levels & (levels - 1) == 0
        and block_rows % (16 * chips) == 0
        and kv_heads % 2 == 0
    )
    if not by_permutes:
        pre_k, pre_v = (lax.all_gather(rows, "ctx", axis=0, tiled=True) for rows in (prefix_keys, prefix_values))
        shared = jnp.concatenate([owned_rows(pool_keys, owners), owned_rows(pool_values, owners)])
        pieces = [(shared, shared.shape[0] // 2)]
        own = (new_keys, new_values, pre_k, pre_v)
        return attend(queries, own, [(0, kv_heads, 0, pieces)], length, kv_heads)
    places = Places(devices)
    z, y, c = places.split(lax.axis_index("ctx"))
    owner = jnp.where(c == 0, owners[0], owners[1])
    owner_z, owner_y, owner_c = places.split(owner)
    pools = [(pool[0], places.swapped(pool[0], core=1)) for pool in (pool_keys, pool_values)]
    count = kv_heads // 2
    part = block_rows // COLUMNS
    tied = lax.optimization_barrier

    def cut(pools, column, first):
        sizes = (1, part, count * HD)
        rows = [chosen(owner_c == c, *pool, (c, column * part, first * HD), sizes) for pool in pools]
        return jnp.concatenate(rows)

    sent = [cut(pools, 1 - y, 0)]
    prefix = jnp.concatenate([prefix_keys, prefix_values])
    sent[0], pools = tied((sent[0], pools))
    sent.append(cut(pools, 1 - y, count))
    prefix, sent[1] = tied((prefix, sent[1]))
    step = 1
    while step < levels:
        prefix = [prefix, places.swapped(prefix, level=step)]
        if step == 1:
            prefix, sent[1] = tied((prefix, sent[1]))
        step *= 2
        prefix = jnp.concatenate(prefix) if step < levels else prefix
    got = [places.swapped(one, column=1) for one in sent]

    def over_z(cuts):
        return [places.swapped(one, level=s) for s, one in enumerate(cuts) if s]

    first_cuts = for_levels(places, jnp.where(owner_y == y, cut(pools, y, 0), got[0]))
    first_got = over_z(first_cuts)
    last_cuts = for_levels(places, jnp.where(owner_y == y, cut(pools, y, count), got[1]))
    last_got = over_z(last_cuts)
    prefix, last_cuts[0] = tied((prefix, last_cuts[0]))
    prefix = jnp.concatenate(prefix)
    prefix = [prefix, places.swapped(prefix, column=1)]
    pieces = [from_owner(z ^ owner_z, *one) for one in ((first_cuts[0], first_got), (last_cuts[0], last_got))]
    prefix, pieces[1] = tied((prefix, pieces[1]))
    early = places.swapped(pieces[0], column=1)
    early, pieces[1] = tied((early, pieces[1]))
    early = [early, places.swapped(pieces[1], column=1)]
    prefix = jnp.concatenate(prefix)
    prefix = jnp.concatenate([prefix, places.swapped(prefix, core=1)])
    gathered = [places.over_levels(one) for one in pieces]
    early[1], gathered[0] = tied((early[1], gathered[0]))
    across = [places.swapped(jnp.concatenate(gathered[0][1:]), column=1)]
    prefix = prefix.reshape(devices, 2, -1, prefix.shape[-1])
    own = (new_keys, new_values) + tuple(prefix[:, i].reshape(-1, prefix.shape[-1]) for i in range(2))
    state = attend(queries, own, [(0, kv_heads, 0, [])], length, kv_heads, ends=False)
    early, state, gathered[1] = tied((early, state, gathered[1]))
    across.append(places.swapped(jnp.concatenate(gathered[1][1:]), column=1))
    mine = [jnp.concatenate(rows + [one]) for rows, one in zip(gathered, early)]
    other = [places.swapped(one, core=1) for one in mine]
    half = pieces[0].shape[0] // 2

    def arrived(at):
        rows = (mine[at], other[at], across[at], places.swapped(across[at], core=1))
        return [(one, half) for one in rows]

    first = arrived(0)
    out = attend(queries, (), [(0, count - 1, 0, first)], length, kv_heads, state)
    across[1], out = tied((across[1], out))
    last = arrived(1)
    out = attend(queries, (), [(count - 1, 1, 0, first)], length, kv_heads, state, out)
    return attend(queries, (), [(count, kv_heads - count, count, last)], length, kv_heads, state, out)


def solution(mesh):
    both = ("groups", "ctx")
    placed = (P(both, None),) * 5 + (P(both, None, None, None),) * 2 + (P("groups"), P(both))
    return jax.shard_map(
        functools.partial(body, devices=mesh.shape["ctx"]),
        mesh=mesh,
        in_specs=placed,
        out_specs=P(both, None),
        check_vma=False,
    )
```

```python
import functools

import jax
import jax.numpy as jnp
from jax import lax
from jax.experimental import pallas as pl
from jax.experimental.pallas import tpu as pltpu
from jax.sharding import PartitionSpec as P

HD = 128
CORES = 2
COLUMNS = 2
TILE = 256
LOG2_E = 1.4426950408889634
VMEM_LIMIT = 24 * 1024 * 1024


def attend_kernel(scale, halves, heads, first_column, length_ref, queries_ref, *rest):
    own_refs, piece_refs = rest[:4], rest[4 : 4 + len(halves)]
    out_ref, blocks_ref, sent_sems = rest[-3:]
    first, count = heads
    rows = queries_ref.shape[0]
    width = blocks_ref.shape[2]
    group = width // HD
    length = length_ref[...]
    query_at = lax.broadcasted_iota(jnp.int32, (rows, rows), 0)
    key_at = lax.broadcasted_iota(jnp.int32, (rows, rows), 1)
    seen = (key_at <= query_at) & (key_at < length)
    live = lax.broadcasted_iota(jnp.int32, (rows, HD), 0) < length

    def copied(h):
        target = out_ref.at[:, pl.ds(pl.multiple_of((first + h) * width, width), width)]
        return pltpu.make_async_copy(blocks_ref.at[h], target, sent_sems.at[h])

    def one_head(h, _):
        column = pl.ds(pl.multiple_of((first + h) * HD, HD), HD)
        local = pl.ds(pl.multiple_of((first + h) * HD - first_column, HD), HD)
        shared = [ref[:, local].reshape(-1, 2, half, HD) for ref, half in zip(piece_refs, halves)]
        keys = jnp.concatenate([ref[:, column] for ref in own_refs[::2]] + [one[:, 0].reshape(-1, HD) for one in shared])
        values = [ref[:, column] for ref in own_refs[1::2]] + [one[:, 1].reshape(-1, HD) for one in shared]
        values = jnp.concatenate(values)
        tiles = [slice(at, at + TILE) for at in range(0, keys.shape[0], TILE)]
        turned = [keys[tile].T for tile in tiles]

        def scored(g, t):
            asked = queries_ref[:, pl.ds(pl.multiple_of((first + h) * width + g * HD, HD), HD)]
            scores = jnp.dot(asked, turned[t], preferred_element_type=jnp.float32)
            if t:
                return scores
            return jnp.concatenate([jnp.where(seen, scores[:, :rows], -1e30), scores[:, rows:]], axis=1)

        def largest(scores):
            return functools.reduce(jnp.maximum, [jnp.max(one, axis=1, keepdims=True) for one in scores])

        def stored(g, products, total):
            inverse = pl.reciprocal(total, approx=True)
            inverse *= 2.0 - total * inverse
            kept = jnp.where(live, products * inverse, 0.0)
            blocks_ref[h, :, g * HD : (g + 1) * HD] = kept.astype(jnp.bfloat16)

        scores = [scored(0, t) for t in range(len(tiles))]
        top = largest(scores)
        done = None
        for g in range(group + 1):
            ahead, weights, products, total = [], [], 0.0, 0.0
            for t, tile in enumerate(tiles):
                if g + 1 < group:
                    ahead.append(scored(g + 1, t))
                if g < group:
                    one = jnp.exp2((scores[t] - top) * scale)
                    total += jnp.sum(one, axis=1, keepdims=True)
                    weights.append(one.astype(jnp.bfloat16))
                if done is not None:
                    products += jnp.dot(done[0][t], values[tile], preferred_element_type=jnp.float32)
            if done is not None:
                stored(g - 1, products, done[1])
            done = weights, total
            if ahead:
                scores, top = ahead, largest(ahead)
        copied(h).start()
        return _

    lax.fori_loop(0, count, one_head, 0)
    for h in range(count):
        copied(h).wait()


def attend(queries, own, pieces, length, heads, first_column, kv_heads, begun=None):
    rows = queries.shape[0]
    width = queries.shape[1] // kv_heads
    count = heads[1]
    halves = [half for _, half in pieces]
    arrays = [array for array, _ in pieces]
    keys = sum(array.shape[0] for array in own[::2]) + sum(array.shape[0] for array in arrays) // 2
    operands = [length, queries, *own, *arrays]
    in_specs = [pl.BlockSpec(memory_space=pltpu.VMEM) for _ in operands]
    aliases = {}
    if begun is not None:
        aliases = {len(operands): 0}
        operands.append(begun)
        in_specs.append(pl.BlockSpec(memory_space=pl.ANY))
    return pl.pallas_call(
        functools.partial(attend_kernel, LOG2_E / HD**0.5, halves, heads, first_column * HD),
        in_specs=in_specs,
        out_specs=pl.BlockSpec(memory_space=pl.ANY),
        out_shape=jax.ShapeDtypeStruct(queries.shape, queries.dtype),
        scratch_shapes=[pltpu.VMEM((count, rows, width), queries.dtype), pltpu.SemaphoreType.DMA((count,))],
        input_output_aliases=aliases,
        compiler_params=pltpu.CompilerParams(vmem_limit_bytes=VMEM_LIMIT),
        cost_estimate=pl.CostEstimate(
            flops=4 * keys * rows * width * count,
            bytes_accessed=4 * rows * width * count,
            transcendentals=keys * rows * width // HD * count,
        ),
        name="attend_heads",
    )(*operands)


class Places:
    def __init__(self, devices):
        self.devices = devices
        self.levels = devices // (CORES * COLUMNS)

    def split(self, index):
        if isinstance(index, int):
            return index // (CORES * COLUMNS), index // CORES % COLUMNS, index % CORES
        chip = lax.div(index, CORES)
        return lax.div(chip, COLUMNS), lax.rem(chip, COLUMNS), lax.rem(index, CORES)

    def swapped(self, array, level=0, column=0, core=0):
        pairs = []
        for index in range(self.devices):
            z, y, c = self.split(index)
            z, y, c = z ^ level, y ^ column, c ^ core
            pairs.append((index, (z * COLUMNS + y) * CORES + c))
        return lax.ppermute(array, "ctx", pairs)

    def over_levels(self, array):
        return [array] + [self.swapped(array, level=s) for s in range(1, self.levels)]


def over_chips(places, rows):
    chips = [rows, places.swapped(rows, column=1)]
    return chips + [places.swapped(one, core=1) for one in chips]


def chosen(flag, mine, got, starts, sizes):
    return jnp.where(flag, lax.dynamic_slice(mine, starts, sizes), lax.dynamic_slice(got, starts, sizes))


def for_levels(places, part):
    z, _, _ = places.split(lax.axis_index("ctx"))
    rows = part.shape[1] // places.levels
    return [
        lax.dynamic_slice_in_dim(part, (z ^ s) * rows, rows, 1).reshape(2 * rows, -1) for s in range(places.levels)
    ]


def from_owner(distance, mine, got):
    piece = mine
    for s, one in enumerate(got, 1):
        piece = jnp.where(distance == s, one, piece)
    return piece


def owned_rows(pool, owners):
    owned = (owners == lax.axis_index("ctx"))[:, None, None]
    return lax.psum(jnp.where(owned, pool[0], 0), "ctx").reshape(-1, pool.shape[-1])


def body(queries, new_keys, new_values, prefix_keys, prefix_values, pool_keys, pool_values, owners, lengths, devices):
    kv_heads = new_keys.shape[1] // HD
    blocks, block_rows = pool_keys.shape[1:3]
    length = jnp.broadcast_to(lengths[:, None], (1, HD))
    chips = devices // CORES
    levels = chips // COLUMNS
    by_permutes = (
        blocks == CORES
        and chips % COLUMNS == 0
        and levels > 1
        and levels & (levels - 1) == 0
        and block_rows % (16 * chips) == 0
        and kv_heads % 2 == 0
    )
    if not by_permutes:
        pre_k, pre_v = (lax.all_gather(rows, "ctx", axis=0, tiled=True) for rows in (prefix_keys, prefix_values))
        shared = jnp.concatenate([owned_rows(pool_keys, owners), owned_rows(pool_values, owners)])
        pieces = [(shared, shared.shape[0] // 2)]
        own = (new_keys, new_values, pre_k, pre_v)
        return attend(queries, own, pieces, length, (0, kv_heads), 0, kv_heads)
    places = Places(devices)
    z, y, c = places.split(lax.axis_index("ctx"))
    owner = jnp.where(c == 0, owners[0], owners[1])
    owner_z, owner_y, owner_c = places.split(owner)
    pools = [(pool[0], places.swapped(pool[0], core=1)) for pool in (pool_keys, pool_values)]
    count = kv_heads // 2
    part = block_rows // COLUMNS
    tied = lax.optimization_barrier

    def cut(pools, column, first):
        sizes = (1, part, count * HD)
        rows = [chosen(owner_c == c, *pool, (c, column * part, first * HD), sizes) for pool in pools]
        return jnp.concatenate(rows)

    sent = [cut(pools, 1 - y, 0)]
    sent[0], pools = tied((sent[0], pools))
    sent.append(cut(pools, 1 - y, count))
    prefix, sent[1] = tied((jnp.concatenate([prefix_keys, prefix_values]), sent[1]))
    got = [places.swapped(one, column=1) for one in sent]
    step = 1
    while step < levels:
        prefix = [prefix, places.swapped(prefix, level=step)]
        step *= 2
        prefix = jnp.concatenate(prefix) if step < levels else prefix

    def over_z(cuts):
        return [places.swapped(one, level=s) for s, one in enumerate(cuts) if s]

    first_cuts = for_levels(places, jnp.where(owner_y == y, cut(pools, y, 0), got[0]))
    first_got = over_z(first_cuts)
    last_cuts = for_levels(places, jnp.where(owner_y == y, cut(pools, y, count), got[1]))
    last_got = over_z(last_cuts)
    prefix, last_cuts[0] = tied((prefix, last_cuts[0]))
    prefix = jnp.concatenate(prefix)
    prefix = [prefix, places.swapped(prefix, column=1)]
    pieces = [from_owner(z ^ owner_z, *one) for one in ((first_cuts[0], first_got), (last_cuts[0], last_got))]
    prefix, pieces[1] = tied((prefix, pieces[1]))
    early = places.swapped(pieces[0], column=1)
    early, pieces[1] = tied((early, pieces[1]))
    early = [early, places.swapped(pieces[1], column=1)]
    gathered = [places.over_levels(one) for one in pieces]
    early[1], gathered[0] = tied((early[1], gathered[0]))
    across = [places.swapped(jnp.concatenate(gathered[0][1:]), column=1)]
    prefix, early, gathered[1] = tied((prefix, early, gathered[1]))
    across.append(places.swapped(jnp.concatenate(gathered[1][1:]), column=1))
    mine = [jnp.concatenate(rows + [one]) for rows, one in zip(gathered, early)]
    other = [places.swapped(one, core=1) for one in mine]
    prefix = jnp.concatenate(prefix)
    prefix = jnp.concatenate([prefix, places.swapped(prefix, core=1)])
    prefix = prefix.reshape(devices, 2, -1, prefix.shape[-1])
    own = (new_keys, new_values) + tuple(prefix[:, i].reshape(-1, prefix.shape[-1]) for i in range(2))
    half = pieces[0].shape[0] // 2

    def arrived(at):
        rows = (mine[at], other[at], across[at], places.swapped(across[at], core=1))
        return [(one, half) for one in rows]

    first = arrived(0)
    out = attend(queries, own, first, length, (0, count - 1), 0, kv_heads)
    across[1], out = tied((across[1], out))
    last = arrived(1)
    out = attend(queries, own, first, length, (count - 1, 1), 0, kv_heads, begun=out)
    return attend(queries, own, last, length, (count, kv_heads - count), count, kv_heads, begun=out)


def solution(mesh):
    both = ("groups", "ctx")
    placed = (P(both, None),) * 5 + (P(both, None, None, None),) * 2 + (P("groups"), P(both))
    return jax.shard_map(
        functools.partial(body, devices=mesh.shape["ctx"]),
        mesh=mesh,
        in_specs=placed,
        out_specs=P(both, None),
        check_vma=False,
    )
```

```python
import functools

import jax
import jax.numpy as jnp
from jax import lax
from jax.experimental import pallas as pl
from jax.experimental.pallas import tpu as pltpu
from jax.sharding import PartitionSpec as P

HD = 128
CORES = 2
COLUMNS = 2
PARTS = 3
LOG2_E = 1.4426950408889634
VMEM_LIMIT = 24 * 1024 * 1024


def attend_kernel(scale, halves, heads, first_column, length_ref, queries_ref, *rest):
    own_refs, piece_refs = rest[:4], rest[4 : 4 + len(halves)]
    out_ref, blocks_ref, sent_sems = rest[-3:]
    first, count = heads
    rows = queries_ref.shape[0]
    width = blocks_ref.shape[2]
    group = width // HD
    length = length_ref[...]
    query_at = lax.broadcasted_iota(jnp.int32, (rows, rows), 0)
    key_at = lax.broadcasted_iota(jnp.int32, (rows, rows), 1)
    seen = (key_at <= query_at) & (key_at < length)
    live = lax.broadcasted_iota(jnp.int32, (rows, HD), 0) < length

    def copied(h):
        target = out_ref.at[:, pl.ds(pl.multiple_of((first + h) * width, width), width)]
        return pltpu.make_async_copy(blocks_ref.at[h], target, sent_sems.at[h])

    def one_head(h, _):
        column = pl.ds(pl.multiple_of((first + h) * HD, HD), HD)
        local = pl.ds(pl.multiple_of((first + h) * HD - first_column, HD), HD)
        shared = [ref[:, local].reshape(-1, 2, half, HD) for ref, half in zip(piece_refs, halves)]
        keys = jnp.concatenate([ref[:, column] for ref in own_refs[::2]] + [one[:, 0].reshape(-1, HD) for one in shared])
        values = [ref[:, column] for ref in own_refs[1::2]] + [one[:, 1].reshape(-1, HD) for one in shared]
        values = jnp.concatenate(values)
        turned = keys.T

        def scored(g):
            asked = queries_ref[:, pl.ds(pl.multiple_of((first + h) * width + g * HD, HD), HD)]
            return jnp.dot(asked, turned, preferred_element_type=jnp.float32)

        def weighed(scores):
            scores = jnp.concatenate([jnp.where(seen, scores[:, :rows], -1e30), scores[:, rows:]], axis=1)
            top = jnp.max(scores, axis=1, keepdims=True)
            weights = jnp.exp2((scores - top) * scale)
            return weights.astype(jnp.bfloat16), jnp.sum(weights, axis=1, keepdims=True)

        def stored(g, weights, total):
            summed = jnp.dot(weights, values, preferred_element_type=jnp.float32)
            inverse = pl.reciprocal(total, approx=True)
            inverse *= 2.0 - total * inverse
            kept = jnp.where(live, summed * inverse, 0.0)
            blocks_ref[h, :, g * HD : (g + 1) * HD] = kept.astype(jnp.bfloat16)

        scores, weights = scored(0), None
        for g in range(group):
            ahead = scored(g + 1) if g + 1 < group else None
            if weights is not None:
                stored(g - 1, *weights)
            weights = weighed(scores)
            scores = ahead
        stored(group - 1, *weights)
        copied(h).start()
        return _

    lax.fori_loop(0, count, one_head, 0)
    for h in range(count):
        copied(h).wait()


def attend(queries, own, pieces, length, heads, first_column, kv_heads, begun=None):
    rows = queries.shape[0]
    width = queries.shape[1] // kv_heads
    count = heads[1]
    halves = [half for _, half in pieces]
    arrays = [array for array, _ in pieces]
    keys = sum(array.shape[0] for array in own[::2]) + sum(array.shape[0] for array in arrays) // 2
    operands = [length, queries, *own, *arrays]
    in_specs = [pl.BlockSpec(memory_space=pltpu.VMEM) for _ in operands]
    aliases = {}
    if begun is not None:
        aliases = {len(operands): 0}
        operands.append(begun)
        in_specs.append(pl.BlockSpec(memory_space=pl.ANY))
    return pl.pallas_call(
        functools.partial(attend_kernel, LOG2_E / HD**0.5, halves, heads, first_column * HD),
        in_specs=in_specs,
        out_specs=pl.BlockSpec(memory_space=pl.ANY),
        out_shape=jax.ShapeDtypeStruct(queries.shape, queries.dtype),
        scratch_shapes=[pltpu.VMEM((count, rows, width), queries.dtype), pltpu.SemaphoreType.DMA((count,))],
        input_output_aliases=aliases,
        compiler_params=pltpu.CompilerParams(vmem_limit_bytes=VMEM_LIMIT),
        cost_estimate=pl.CostEstimate(
            flops=4 * keys * rows * width * count,
            bytes_accessed=4 * rows * width * count,
            transcendentals=keys * rows * width // HD * count,
        ),
        name="attend_heads",
    )(*operands)


class Places:
    def __init__(self, devices):
        self.devices = devices
        self.levels = devices // (CORES * COLUMNS)

    def split(self, index):
        if isinstance(index, int):
            return index // (CORES * COLUMNS), index // CORES % COLUMNS, index % CORES
        chip = lax.div(index, CORES)
        return lax.div(chip, COLUMNS), lax.rem(chip, COLUMNS), lax.rem(index, CORES)

    def swapped(self, array, level=0, column=0, core=0):
        pairs = []
        for index in range(self.devices):
            z, y, c = self.split(index)
            z, y, c = z ^ level, y ^ column, c ^ core
            pairs.append((index, (z * COLUMNS + y) * CORES + c))
        return lax.ppermute(array, "ctx", pairs)

    def over_levels(self, array):
        return [array] + [self.swapped(array, level=s) for s in range(1, self.levels)]


def over_chips(places, rows):
    chips = [rows, places.swapped(rows, column=1)]
    return chips + [places.swapped(one, core=1) for one in chips]


def chosen(flag, mine, got, starts, sizes):
    return jnp.where(flag, lax.dynamic_slice(mine, starts, sizes), lax.dynamic_slice(got, starts, sizes))


def halved(part, at):
    rows = part.shape[1] // 2
    return lax.dynamic_slice_in_dim(part, at * rows, rows, 1)


def along_levels(places, parts, owner):
    z, _, _ = places.split(lax.axis_index("ctx"))
    owner_z, _, _ = places.split(owner)
    *low, high = [1 << k for k in range(places.levels.bit_length() - 1)]

    def in_turn(arrays, distance, sent):
        got = []
        for at in range(len(arrays)):
            got.append(places.swapped(sent(arrays[at]), level=distance))
            if at + 1 < len(arrays):
                arrays[at], arrays[at + 1] = lax.optimization_barrier((arrays[at], arrays[at + 1]))
        return got

    for distance in low:
        bit = (z // distance) & 1
        got = in_turn(parts, distance, lambda part: halved(part, 1 - bit))
        here = (owner_z ^ z) & distance == 0
        parts = [jnp.where(here, halved(part, bit), one) for part, one in zip(parts, got)]
    got = in_turn(parts, high, lambda part: part)
    parts = [jnp.where((owner_z ^ z) & high == 0, part, one) for part, one in zip(parts, got)]
    rows = [part.reshape(-1, part.shape[-1]) for part in parts]
    for distance in reversed(low):
        got = in_turn(rows, distance, lambda part: part)
        rows = [jnp.concatenate(both) for both in zip(rows, got)]
    return [(one, part.shape[1]) for one, part in zip(rows, parts)]


def owned_rows(pool, owners):
    owned = (owners == lax.axis_index("ctx"))[:, None, None]
    return lax.psum(jnp.where(owned, pool[0], 0), "ctx").reshape(-1, pool.shape[-1])


def body(queries, new_keys, new_values, prefix_keys, prefix_values, pool_keys, pool_values, owners, lengths, devices):
    kv_heads = new_keys.shape[1] // HD
    blocks, block_rows = pool_keys.shape[1:3]
    length = jnp.broadcast_to(lengths[:, None], (1, HD))
    chips = devices // CORES
    levels = chips // COLUMNS
    by_permutes = (
        blocks == CORES
        and chips % COLUMNS == 0
        and levels > 1
        and levels & (levels - 1) == 0
        and block_rows % (16 * chips) == 0
        and kv_heads >= PARTS
    )
    if not by_permutes:
        pre_k, pre_v = (lax.all_gather(rows, "ctx", axis=0, tiled=True) for rows in (prefix_keys, prefix_values))
        shared = jnp.concatenate([owned_rows(pool_keys, owners), owned_rows(pool_values, owners)])
        pieces = [(shared, shared.shape[0] // 2)]
        own = (new_keys, new_values, pre_k, pre_v)
        return attend(queries, own, pieces, length, (0, kv_heads), 0, kv_heads)
    places = Places(devices)
    z, y, c = places.split(lax.axis_index("ctx"))
    owner = jnp.where(c == 0, owners[0], owners[1])
    owner_z, owner_y, owner_c = places.split(owner)
    pools = [(pool[0], places.swapped(pool[0], core=1)) for pool in (pool_keys, pool_values)]
    counts = [(kv_heads + at) // PARTS for at in reversed(range(PARTS))]
    firsts = [sum(counts[:at]) for at in range(PARTS)]
    part_rows = block_rows // COLUMNS
    tied = lax.optimization_barrier

    def cut(pools, column, at):
        sizes = (1, part_rows, counts[at] * HD)
        rows = [chosen(owner_c == c, *pool, (c, column * part_rows, firsts[at] * HD), sizes) for pool in pools]
        return jnp.concatenate(rows)

    sent = [cut(pools, 1 - y, 0)]
    prefix = jnp.concatenate([prefix_keys, prefix_values])
    for at in range(1, PARTS):
        sent[-1], pools = tied((sent[-1], pools))
        sent.append(cut(pools, 1 - y, at))
    prefix, sent[1] = tied((prefix, sent[1]))
    for at in range(levels.bit_length() - 1):
        prefix = [prefix, places.swapped(prefix, level=1 << at)]
        later = min(at + 1, PARTS - 1)
        prefix, sent[later] = tied((prefix, sent[later]))
        prefix = jnp.concatenate(prefix)
    got = [places.swapped(one, column=1) for one in sent]
    parts = [jnp.where(owner_y == y, cut(pools, y, at), one) for at, one in enumerate(got)]
    prefix, parts[-1] = tied((prefix, parts[-1]))
    prefix = jnp.concatenate([prefix, places.swapped(prefix, column=1)])
    joined = along_levels(places, parts, owner)
    prefix = jnp.concatenate([prefix, places.swapped(prefix, core=1)])
    prefix = prefix.reshape(devices, 2, -1, prefix.shape[-1])
    own = (new_keys, new_values) + tuple(prefix[:, i].reshape(-1, prefix.shape[-1]) for i in range(2))
    across = [places.swapped(rows, column=1) for rows, _ in joined]
    other = [places.swapped(rows, core=1) for rows, _ in joined]
    out = None
    for at, (rows, half) in enumerate(joined):
        pieces = [rows, other[at], across[at], places.swapped(across[at], core=1)]
        pieces = [(one, half) for one in pieces]
        out = attend(queries, own, pieces, length, (firsts[at], counts[at]), firsts[at], kv_heads, begun=out)
        if at + 2 < PARTS:
            across[at + 2], out = tied((across[at + 2], out))
    return out


def solution(mesh):
    both = ("groups", "ctx")
    placed = (P(both, None),) * 5 + (P(both, None, None, None),) * 2 + (P("groups"), P(both))
    return jax.shard_map(
        functools.partial(body, devices=mesh.shape["ctx"]),
        mesh=mesh,
        in_specs=placed,
        out_specs=P(both, None),
        check_vma=False,
    )
```

```python
import functools

import jax
import jax.numpy as jnp
from jax import lax
from jax.experimental import pallas as pl
from jax.experimental.pallas import tpu as pltpu
from jax.sharding import PartitionSpec as P

HD = 128
CORES = 2
COLUMNS = 2
LOG2_E = 1.4426950408889634
VMEM_LIMIT = 24 * 1024 * 1024


def attend_kernel(scale, halves, heads, first_column, length_ref, queries_ref, *rest):
    own_refs, piece_refs = rest[:4], rest[4 : 4 + len(halves)]
    out_ref, blocks_ref, sent_sems = rest[-3:]
    first, count = heads
    rows = queries_ref.shape[0]
    width = blocks_ref.shape[2]
    group = width // HD
    length = length_ref[...]
    query_at = lax.broadcasted_iota(jnp.int32, (rows, rows), 0)
    key_at = lax.broadcasted_iota(jnp.int32, (rows, rows), 1)
    seen = (key_at <= query_at) & (key_at < length)
    live = lax.broadcasted_iota(jnp.int32, (rows, HD), 0) < length

    def copied(h):
        target = out_ref.at[:, pl.ds(pl.multiple_of((first + h) * width, width), width)]
        return pltpu.make_async_copy(blocks_ref.at[h], target, sent_sems.at[h])

    def one_head(h, _):
        column = pl.ds(pl.multiple_of((first + h) * HD, HD), HD)
        local = pl.ds(pl.multiple_of((first + h) * HD - first_column, HD), HD)
        shared = [ref[:, local].reshape(-1, 2, half, HD) for ref, half in zip(piece_refs, halves)]
        keys = jnp.concatenate([ref[:, column] for ref in own_refs[::2]] + [one[:, 0].reshape(-1, HD) for one in shared])
        values = [ref[:, column] for ref in own_refs[1::2]] + [one[:, 1].reshape(-1, HD) for one in shared]
        values = jnp.concatenate(values)
        turned = keys.T

        def scored(g):
            asked = queries_ref[:, pl.ds(pl.multiple_of((first + h) * width + g * HD, HD), HD)]
            return jnp.dot(asked, turned, preferred_element_type=jnp.float32)

        def weighed(scores):
            scores = jnp.concatenate([jnp.where(seen, scores[:, :rows], -1e30), scores[:, rows:]], axis=1)
            top = jnp.max(scores, axis=1, keepdims=True)
            weights = jnp.exp2((scores - top) * scale)
            return weights.astype(jnp.bfloat16), jnp.sum(weights, axis=1, keepdims=True)

        def stored(g, weights, total):
            summed = jnp.dot(weights, values, preferred_element_type=jnp.float32)
            inverse = pl.reciprocal(total, approx=True)
            inverse *= 2.0 - total * inverse
            kept = jnp.where(live, summed * inverse, 0.0)
            blocks_ref[h, :, g * HD : (g + 1) * HD] = kept.astype(jnp.bfloat16)

        scores, weights = scored(0), None
        for g in range(group):
            ahead = scored(g + 1) if g + 1 < group else None
            if weights is not None:
                stored(g - 1, *weights)
            weights = weighed(scores)
            scores = ahead
        stored(group - 1, *weights)
        copied(h).start()
        return _

    lax.fori_loop(0, count, one_head, 0)
    for h in range(count):
        copied(h).wait()


def attend(queries, own, pieces, length, heads, first_column, kv_heads, begun=None):
    rows = queries.shape[0]
    width = queries.shape[1] // kv_heads
    count = heads[1]
    halves = [half for _, half in pieces]
    arrays = [array for array, _ in pieces]
    keys = sum(array.shape[0] for array in own[::2]) + sum(array.shape[0] for array in arrays) // 2
    operands = [length, queries, *own, *arrays]
    in_specs = [pl.BlockSpec(memory_space=pltpu.VMEM) for _ in operands]
    aliases = {}
    if begun is not None:
        aliases = {len(operands): 0}
        operands.append(begun)
        in_specs.append(pl.BlockSpec(memory_space=pl.ANY))
    return pl.pallas_call(
        functools.partial(attend_kernel, LOG2_E / HD**0.5, halves, heads, first_column * HD),
        in_specs=in_specs,
        out_specs=pl.BlockSpec(memory_space=pl.ANY),
        out_shape=jax.ShapeDtypeStruct(queries.shape, queries.dtype),
        scratch_shapes=[pltpu.VMEM((count, rows, width), queries.dtype), pltpu.SemaphoreType.DMA((count,))],
        input_output_aliases=aliases,
        compiler_params=pltpu.CompilerParams(vmem_limit_bytes=VMEM_LIMIT),
        cost_estimate=pl.CostEstimate(
            flops=4 * keys * rows * width * count,
            bytes_accessed=4 * rows * width * count,
            transcendentals=keys * rows * width // HD * count,
        ),
        name="attend_heads",
    )(*operands)


class Places:
    def __init__(self, devices):
        self.devices = devices
        self.levels = devices // (CORES * COLUMNS)

    def split(self, index):
        if isinstance(index, int):
            return index // (CORES * COLUMNS), index // CORES % COLUMNS, index % CORES
        chip = lax.div(index, CORES)
        return lax.div(chip, COLUMNS), lax.rem(chip, COLUMNS), lax.rem(index, CORES)

    def swapped(self, array, level=0, column=0, core=0):
        pairs = []
        for index in range(self.devices):
            z, y, c = self.split(index)
            z, y, c = z ^ level, y ^ column, c ^ core
            pairs.append((index, (z * COLUMNS + y) * CORES + c))
        return lax.ppermute(array, "ctx", pairs)

    def over_levels(self, array):
        return [array] + [self.swapped(array, level=s) for s in range(1, self.levels)]


def over_chips(places, rows):
    chips = [rows, places.swapped(rows, column=1)]
    return chips + [places.swapped(one, core=1) for one in chips]


def chosen(flag, mine, got, starts, sizes):
    return jnp.where(flag, lax.dynamic_slice(mine, starts, sizes), lax.dynamic_slice(got, starts, sizes))


def halved(part, at):
    rows = part.shape[1] // 2
    return lax.dynamic_slice_in_dim(part, at * rows, rows, 1)


def for_levels(places, part):
    z, _, _ = places.split(lax.axis_index("ctx"))
    rows = part.shape[1] // places.levels
    return [
        lax.dynamic_slice_in_dim(part, (z ^ s) * rows, rows, 1).reshape(2 * rows, -1) for s in range(places.levels)
    ]


def from_owner(distance, mine, got):
    piece = mine
    for s, one in enumerate(got, 1):
        piece = jnp.where(distance == s, one, piece)
    return piece


def owned_rows(pool, owners):
    owned = (owners == lax.axis_index("ctx"))[:, None, None]
    return lax.psum(jnp.where(owned, pool[0], 0), "ctx").reshape(-1, pool.shape[-1])


def body(queries, new_keys, new_values, prefix_keys, prefix_values, pool_keys, pool_values, owners, lengths, devices):
    kv_heads = new_keys.shape[1] // HD
    blocks, block_rows = pool_keys.shape[1:3]
    length = jnp.broadcast_to(lengths[:, None], (1, HD))
    chips = devices // CORES
    levels = chips // COLUMNS
    by_permutes = (
        blocks == CORES
        and chips % COLUMNS == 0
        and levels > 1
        and levels & (levels - 1) == 0
        and block_rows % (16 * chips) == 0
        and kv_heads % 2 == 0
    )
    if not by_permutes:
        pre_k, pre_v = (lax.all_gather(rows, "ctx", axis=0, tiled=True) for rows in (prefix_keys, prefix_values))
        shared = jnp.concatenate([owned_rows(pool_keys, owners), owned_rows(pool_values, owners)])
        pieces = [(shared, shared.shape[0] // 2)]
        own = (new_keys, new_values, pre_k, pre_v)
        return attend(queries, own, pieces, length, (0, kv_heads), 0, kv_heads)
    places = Places(devices)
    z, y, c = places.split(lax.axis_index("ctx"))
    owner = jnp.where(c == 0, owners[0], owners[1])
    owner_z, owner_y, owner_c = places.split(owner)
    pools = [(pool[0], places.swapped(pool[0], core=1)) for pool in (pool_keys, pool_values)]
    count = kv_heads // 2
    part = block_rows // COLUMNS
    tied = lax.optimization_barrier

    def cut(pools, column, first):
        sizes = (1, part, count * HD)
        rows = [chosen(owner_c == c, *pool, (c, column * part, first * HD), sizes) for pool in pools]
        return jnp.concatenate(rows)

    sent = [cut(pools, 1 - y, 0)]
    sent[0], pools = tied((sent[0], pools))
    sent.append(cut(pools, 1 - y, count))
    prefix, sent[1] = tied((jnp.concatenate([prefix_keys, prefix_values]), sent[1]))
    got = [places.swapped(one, column=1) for one in sent]
    step = 1
    while step < levels:
        prefix = [prefix, places.swapped(prefix, level=step)]
        step *= 2
        prefix = jnp.concatenate(prefix) if step < levels else prefix

    def over_z(cuts):
        return [places.swapped(one, level=s) for s, one in enumerate(cuts) if s]

    first_cuts = for_levels(places, jnp.where(owner_y == y, cut(pools, y, 0), got[0]))
    first_got = over_z(first_cuts)
    *low, high = [1 << k for k in range(levels.bit_length() - 1)]
    last = jnp.where(owner_y == y, cut(pools, y, count), got[1])
    for distance in low:
        bit = (z // distance) & 1
        swap = places.swapped(halved(last, 1 - bit), level=distance)
        last = jnp.where((owner_z ^ z) & distance == 0, halved(last, bit), swap)
    prefix, first_cuts[0] = tied((prefix, first_cuts[0]))
    prefix = jnp.concatenate(prefix)
    prefix = [prefix, places.swapped(prefix, column=1)]
    prefix, last = tied((prefix, last))
    piece = from_owner(z ^ owner_z, first_cuts[0], first_got)
    early = places.swapped(piece, column=1)
    last = jnp.where((owner_z ^ z) & high == 0, last, places.swapped(last, level=high))
    early, last = tied((early, last))
    gathered = places.over_levels(piece)
    last_half = last.shape[1]
    last_rows = [last.reshape(-1, last.shape[-1])]
    last_early = places.swapped(last_rows[0], column=1)
    for distance in reversed(low):
        last_rows.append(places.swapped(jnp.concatenate(last_rows), level=distance))
    across = places.swapped(jnp.concatenate(gathered[1:]), column=1)
    prefix, early, last_rows[1] = tied((prefix, early, last_rows[1]))
    last_across = places.swapped(jnp.concatenate(last_rows[1:]), column=1)
    mine = jnp.concatenate(gathered + [early])
    last_mine = jnp.concatenate(last_rows + [last_early])
    prefix = jnp.concatenate(prefix)
    prefix = jnp.concatenate([prefix, places.swapped(prefix, core=1)])
    prefix = prefix.reshape(devices, 2, -1, prefix.shape[-1])
    own = (new_keys, new_values) + tuple(prefix[:, i].reshape(-1, prefix.shape[-1]) for i in range(2))

    def arrived(half, *rows):
        return [(one, half) for one in rows + tuple(places.swapped(one, core=1) for one in rows)]

    first = arrived(piece.shape[0] // 2, mine, across)
    out = attend(queries, own, first, length, (0, count - 1), 0, kv_heads)
    last_across, out = tied((last_across, out))
    last = arrived(last_half, last_mine, last_across)
    out = attend(queries, own, first, length, (count - 1, 1), 0, kv_heads, begun=out)
    return attend(queries, own, last, length, (count, kv_heads - count), count, kv_heads, begun=out)


def solution(mesh):
    both = ("groups", "ctx")
    placed = (P(both, None),) * 5 + (P(both, None, None, None),) * 2 + (P("groups"), P(both))
    return jax.shard_map(
        functools.partial(body, devices=mesh.shape["ctx"]),
        mesh=mesh,
        in_specs=placed,
        out_specs=P(both, None),
        check_vma=False,
    )
```

```python
import functools

import jax
import jax.numpy as jnp
from jax import lax
from jax.experimental import pallas as pl
from jax.experimental.pallas import tpu as pltpu
from jax.sharding import PartitionSpec as P

HD = 128
CORES = 2
COLUMNS = 2
LOG2_E = 1.4426950408889634
VMEM_LIMIT = 24 * 1024 * 1024


def attend_kernel(scale, halves, heads, first_column, width, earlier, length_ref, queries_ref, *rest):
    own_refs, piece_refs = rest[:4], rest[4 : 4 + len(halves)]
    first, count = heads
    rows = queries_ref.shape[0]
    if earlier is None:
        blocks_ref = rest[-1]
    else:
        earlier_refs = rest[4 + len(halves) : 4 + len(halves) + len(earlier)]
        out_ref, blocks_ref, sent_sems = rest[-3:]
    group = width // HD
    length = length_ref[...]
    query_at = lax.broadcasted_iota(jnp.int32, (rows, rows), 0)
    key_at = lax.broadcasted_iota(jnp.int32, (rows, rows), 1)
    seen = (key_at <= query_at) & (key_at < length)
    live = lax.broadcasted_iota(jnp.int32, (rows, HD), 0) < length

    def copied(source, head, sem):
        target = out_ref.at[:, pl.ds(pl.multiple_of(head * width, width), width)]
        return pltpu.make_async_copy(source, target, sent_sems.at[sem])

    kept = []
    if earlier is not None:
        for ref, (at, number) in zip(earlier_refs, earlier):
            kept += [copied(ref.at[h], at + h, count + len(kept) + h) for h in range(number)]
    for copy in kept:
        copy.start()

    def one_head(h, _):
        column = pl.ds(pl.multiple_of((first + h) * HD, HD), HD)
        local = pl.ds(pl.multiple_of((first + h) * HD - first_column, HD), HD)
        shared = [ref[:, local].reshape(-1, 2, half, HD) for ref, half in zip(piece_refs, halves)]
        keys = jnp.concatenate([ref[:, column] for ref in own_refs[::2]] + [one[:, 0].reshape(-1, HD) for one in shared])
        values = [ref[:, column] for ref in own_refs[1::2]] + [one[:, 1].reshape(-1, HD) for one in shared]
        values = jnp.concatenate(values)
        turned = keys.T

        def scored(g):
            asked = queries_ref[:, pl.ds(pl.multiple_of((first + h) * width + g * HD, HD), HD)]
            return jnp.dot(asked, turned, preferred_element_type=jnp.float32)

        def weighed(scores):
            scores = jnp.concatenate([jnp.where(seen, scores[:, :rows], -1e30), scores[:, rows:]], axis=1)
            top = jnp.max(scores, axis=1, keepdims=True)
            weights = jnp.exp2((scores - top) * scale)
            return weights.astype(jnp.bfloat16), jnp.sum(weights, axis=1, keepdims=True)

        def stored(g, weights, total):
            summed = jnp.dot(weights, values, preferred_element_type=jnp.float32)
            inverse = pl.reciprocal(total, approx=True)
            inverse *= 2.0 - total * inverse
            shown = jnp.where(live, summed * inverse, 0.0)
            blocks_ref[h, :, g * HD : (g + 1) * HD] = shown.astype(jnp.bfloat16)

        scores, weights = scored(0), None
        for g in range(group):
            ahead = scored(g + 1) if g + 1 < group else None
            if weights is not None:
                stored(g - 1, *weights)
            weights = weighed(scores)
            scores = ahead
        stored(group - 1, *weights)
        if earlier is not None:
            copied(blocks_ref.at[h], first + h, h).start()
        return _

    lax.fori_loop(0, count, one_head, 0)
    if earlier is not None:
        kept += [copied(blocks_ref.at[h], first + h, h) for h in range(count)]
    for copy in kept:
        copy.wait()


def attend(queries, own, pieces, length, heads, first_column, kv_heads, earlier=()):
    rows = queries.shape[0]
    width = queries.shape[1] // kv_heads
    count = heads[1]
    halves = [half for _, half in pieces]
    arrays = [array for array, _ in pieces]
    keys = sum(array.shape[0] for array in own[::2]) + sum(array.shape[0] for array in arrays) // 2
    operands = [length, queries, *own, *arrays]
    blocks = (count, rows, width)
    if earlier is None:
        ranges, scratch = None, []
        out_specs = pl.BlockSpec(memory_space=pltpu.VMEM)
        out_shape = jax.ShapeDtypeStruct(blocks, queries.dtype)
    else:
        ranges = [one[:2] for one in earlier]
        operands += [one[2] for one in earlier]
        copies = count + sum(number for _, number in ranges)
        scratch = [pltpu.VMEM(blocks, queries.dtype), pltpu.SemaphoreType.DMA((copies,))]
        out_specs = pl.BlockSpec(memory_space=pl.ANY)
        out_shape = jax.ShapeDtypeStruct(queries.shape, queries.dtype)
    return pl.pallas_call(
        functools.partial(attend_kernel, LOG2_E / HD**0.5, halves, heads, first_column * HD, width, ranges),
        in_specs=[pl.BlockSpec(memory_space=pltpu.VMEM) for _ in operands],
        out_specs=out_specs,
        out_shape=out_shape,
        scratch_shapes=scratch,
        compiler_params=pltpu.CompilerParams(vmem_limit_bytes=VMEM_LIMIT),
        cost_estimate=pl.CostEstimate(
            flops=4 * keys * rows * width * count,
            bytes_accessed=4 * rows * width * count,
            transcendentals=keys * rows * width // HD * count,
        ),
        name="attend_heads",
    )(*operands)


class Places:
    def __init__(self, devices):
        self.devices = devices
        self.levels = devices // (CORES * COLUMNS)

    def split(self, index):
        if isinstance(index, int):
            return index // (CORES * COLUMNS), index // CORES % COLUMNS, index % CORES
        chip = lax.div(index, CORES)
        return lax.div(chip, COLUMNS), lax.rem(chip, COLUMNS), lax.rem(index, CORES)

    def swapped(self, array, level=0, column=0, core=0):
        pairs = []
        for index in range(self.devices):
            z, y, c = self.split(index)
            z, y, c = z ^ level, y ^ column, c ^ core
            pairs.append((index, (z * COLUMNS + y) * CORES + c))
        return lax.ppermute(array, "ctx", pairs)

    def over_levels(self, array):
        return [array] + [self.swapped(array, level=s) for s in range(1, self.levels)]


def over_chips(places, rows):
    chips = [rows, places.swapped(rows, column=1)]
    return chips + [places.swapped(one, core=1) for one in chips]


def halved(part, at):
    rows = part.shape[1] // 2
    return lax.dynamic_slice_in_dim(part, at * rows, rows, 1)


def for_levels(places, part):
    z, _, _ = places.split(lax.axis_index("ctx"))
    rows = part.shape[1] // places.levels
    return [
        lax.dynamic_slice_in_dim(part, (z ^ s) * rows, rows, 1).reshape(2 * rows, -1) for s in range(places.levels)
    ]


def from_owner(distance, mine, got):
    piece = mine
    for s, one in enumerate(got, 1):
        piece = jnp.where(distance == s, one, piece)
    return piece


def owned_rows(pool, owners):
    owned = (owners == lax.axis_index("ctx"))[:, None, None]
    return lax.psum(jnp.where(owned, pool[0], 0), "ctx").reshape(-1, pool.shape[-1])


def body(queries, new_keys, new_values, prefix_keys, prefix_values, pool_keys, pool_values, owners, lengths, devices):
    kv_heads = new_keys.shape[1] // HD
    blocks, block_rows = pool_keys.shape[1:3]
    length = jnp.broadcast_to(lengths[:, None], (1, HD))
    chips = devices // CORES
    levels = chips // COLUMNS
    by_permutes = (
        blocks == CORES
        and chips % COLUMNS == 0
        and levels > 1
        and levels & (levels - 1) == 0
        and block_rows % (16 * chips) == 0
        and kv_heads % 2 == 0
    )
    if not by_permutes:
        pre_k, pre_v = (lax.all_gather(rows, "ctx", axis=0, tiled=True) for rows in (prefix_keys, prefix_values))
        shared = jnp.concatenate([owned_rows(pool_keys, owners), owned_rows(pool_values, owners)])
        pieces = [(shared, shared.shape[0] // 2)]
        own = (new_keys, new_values, pre_k, pre_v)
        return attend(queries, own, pieces, length, (0, kv_heads), 0, kv_heads)
    places = Places(devices)
    z, y, c = places.split(lax.axis_index("ctx"))
    owner = jnp.where(c == 0, owners[0], owners[1])
    owner_z, owner_y, owner_c = places.split(owner)
    pools = (pool_keys[0], pool_values[0])
    count = kv_heads // 2
    part = block_rows // COLUMNS
    tied = lax.optimization_barrier

    def cut(pools, column, first):
        at, sizes = (c, column * part, first * HD), (1, part, count * HD)
        return jnp.concatenate([lax.dynamic_slice(pool, at, sizes) for pool in pools])

    mine = [[cut(pools, column, first) for column in (1 - y, y)] for first in (0, count)]
    mine, pools = tied((mine, [places.swapped(pool, core=1) for pool in pools]))

    def chosen(which, column, first):
        return jnp.where(owner_c == c, mine[first // count][which], cut(pools, column, first))

    sent = [chosen(0, 1 - y, 0)]
    sent[0], pools = tied((sent[0], pools))
    sent.append(chosen(0, 1 - y, count))
    prefix, sent[1] = tied(((prefix_keys, prefix_values), sent[1]))
    prefix = jnp.concatenate(prefix)
    step = 1
    while step < levels:
        prefix = [prefix, places.swapped(prefix, level=step)]
        if step == 1:
            prefix, sent[1] = tied((prefix, sent[1]))
        step *= 2
        prefix = jnp.concatenate(prefix) if step < levels else prefix

    got = [places.swapped(one, column=1) for one in sent]

    def over_z(cuts):
        return [places.swapped(one, level=s) for s, one in enumerate(cuts) if s]

    first_cuts = for_levels(places, jnp.where(owner_y == y, chosen(1, y, 0), got[0]))
    first_got = over_z(first_cuts)
    *low, high = [1 << k for k in range(levels.bit_length() - 1)]
    last = jnp.where(owner_y == y, chosen(1, y, count), got[1])
    for distance in low:
        bit = (z // distance) & 1
        swap = places.swapped(halved(last, 1 - bit), level=distance)
        last = jnp.where((owner_z ^ z) & distance == 0, halved(last, bit), swap)
    prefix, first_got[0] = tied((prefix, first_got[0]))
    prefix = jnp.concatenate(prefix)
    prefix = [prefix, places.swapped(prefix, column=1)]
    prefix, last = tied((prefix, last))
    piece = from_owner(z ^ owner_z, first_cuts[0], first_got)
    early = places.swapped(piece, column=1)
    last = jnp.where((owner_z ^ z) & high == 0, last, places.swapped(last, level=high))
    early, last = tied((early, last))
    gathered = places.over_levels(piece)
    last_half = last.shape[1]
    last_rows = [last.reshape(-1, last.shape[-1])]
    last_early = places.swapped(last_rows[0], column=1)
    for distance in reversed(low):
        last_rows.append(places.swapped(jnp.concatenate(last_rows), level=distance))
    across = places.swapped(jnp.concatenate(gathered[1:]), column=1)
    prefix, early, last_rows[1] = tied((prefix, early, last_rows[1]))
    last_across = places.swapped(jnp.concatenate(last_rows[1:]), column=1)
    first_mine = jnp.concatenate(gathered + [early])
    last_mine = jnp.concatenate(last_rows + [last_early])
    prefix = jnp.concatenate(prefix)
    prefix = jnp.concatenate([prefix, places.swapped(prefix, core=1)])
    prefix = prefix.reshape(devices, 2, -1, prefix.shape[-1])
    own = (new_keys, new_values) + tuple(prefix[:, i].reshape(-1, prefix.shape[-1]) for i in range(2))

    def arrived(half, *rows):
        return [(one, half) for one in rows + tuple(places.swapped(one, core=1) for one in rows)]

    first = arrived(piece.shape[0] // 2, first_mine, across)
    blocks = attend(queries, own, first, length, (0, count - 1), 0, kv_heads, None)
    last_across, blocks = tied((last_across, blocks))
    last = arrived(last_half, last_mine, last_across)
    earlier = [(0, count - 1, blocks)]
    earlier.append((count - 1, 1, attend(queries, own, first, length, (count - 1, 1), 0, kv_heads, None)))
    return attend(queries, own, last, length, (count, kv_heads - count), count, kv_heads, earlier)


def solution(mesh):
    both = ("groups", "ctx")
    placed = (P(both, None),) * 5 + (P(both, None, None, None),) * 2 + (P("groups"), P(both))
    return jax.shard_map(
        functools.partial(body, devices=mesh.shape["ctx"]),
        mesh=mesh,
        in_specs=placed,
        out_specs=P(both, None),
        check_vma=False,
    )
```

```python
import functools

import jax
import jax.numpy as jnp
from jax import lax
from jax.experimental import pallas as pl
from jax.experimental.pallas import tpu as pltpu
from jax.sharding import PartitionSpec as P

HD = 128
CORES = 2
COLUMNS = 2
LOG2_E = 1.4426950408889634
VMEM_LIMIT = 24 * 1024 * 1024


def attend_kernel(scale, halves, heads, first_column, width, earlier, length_ref, queries_ref, *rest):
    own_refs, piece_refs = rest[:4], rest[4 : 4 + len(halves)]
    first, count = heads
    rows = queries_ref.shape[0]
    if earlier is None:
        blocks_ref = rest[-1]
    else:
        earlier_refs = rest[4 + len(halves) : 4 + len(halves) + len(earlier)]
        out_ref, blocks_ref, sent_sems = rest[-3:]
    group = width // HD
    length = length_ref[...]
    query_at = lax.broadcasted_iota(jnp.int32, (rows, rows), 0)
    key_at = lax.broadcasted_iota(jnp.int32, (rows, rows), 1)
    seen = (key_at <= query_at) & (key_at < length)
    live = lax.broadcasted_iota(jnp.int32, (rows, HD), 0) < length

    def copied(source, head, sem):
        target = out_ref.at[:, pl.ds(pl.multiple_of(head * width, width), width)]
        return pltpu.make_async_copy(source, target, sent_sems.at[sem])

    kept = []
    if earlier is not None:
        for ref, (at, number) in zip(earlier_refs, earlier):
            kept += [copied(ref.at[h], at + h, count + len(kept) + h) for h in range(number)]
    for copy in kept:
        copy.start()

    def one_head(h, _):
        column = pl.ds(pl.multiple_of((first + h) * HD, HD), HD)
        local = pl.ds(pl.multiple_of((first + h) * HD - first_column, HD), HD)
        shared = [ref[:, local].reshape(-1, 2, half, HD) for ref, half in zip(piece_refs, halves)]
        keys = jnp.concatenate([ref[:, column] for ref in own_refs[::2]] + [one[:, 0].reshape(-1, HD) for one in shared])
        values = [ref[:, column] for ref in own_refs[1::2]] + [one[:, 1].reshape(-1, HD) for one in shared]
        values = jnp.concatenate(values)
        turned = keys.T

        def scored(g):
            asked = queries_ref[:, pl.ds(pl.multiple_of((first + h) * width + g * HD, HD), HD)]
            return jnp.dot(asked, turned, preferred_element_type=jnp.float32)

        def weighed(scores):
            scores = jnp.concatenate([jnp.where(seen, scores[:, :rows], -1e30), scores[:, rows:]], axis=1)
            top = jnp.max(scores, axis=1, keepdims=True)
            weights = jnp.exp2((scores - top) * scale)
            return weights.astype(jnp.bfloat16), jnp.sum(weights, axis=1, keepdims=True)

        def stored(g, weights, total):
            summed = jnp.dot(weights, values, preferred_element_type=jnp.float32)
            inverse = pl.reciprocal(total, approx=True)
            inverse *= 2.0 - total * inverse
            shown = jnp.where(live, summed * inverse, 0.0)
            blocks_ref[h, :, g * HD : (g + 1) * HD] = shown.astype(jnp.bfloat16)

        scores, weights = scored(0), None
        for g in range(group):
            ahead = scored(g + 1) if g + 1 < group else None
            if weights is not None:
                stored(g - 1, *weights)
            weights = weighed(scores)
            scores = ahead
        stored(group - 1, *weights)
        if earlier is not None:
            copied(blocks_ref.at[h], first + h, h).start()
        return _

    lax.fori_loop(0, count, one_head, 0)
    if earlier is not None:
        kept += [copied(blocks_ref.at[h], first + h, h) for h in range(count)]
    for copy in kept:
        copy.wait()


def attend(queries, own, pieces, length, heads, first_column, kv_heads, earlier=()):
    rows = queries.shape[0]
    width = queries.shape[1] // kv_heads
    count = heads[1]
    halves = [half for _, half in pieces]
    arrays = [array for array, _ in pieces]
    keys = sum(array.shape[0] for array in own[::2]) + sum(array.shape[0] for array in arrays) // 2
    operands = [length, queries, *own, *arrays]
    blocks = (count, rows, width)
    if earlier is None:
        ranges, scratch = None, []
        out_specs = pl.BlockSpec(memory_space=pltpu.VMEM)
        out_shape = jax.ShapeDtypeStruct(blocks, queries.dtype)
    else:
        ranges = [one[:2] for one in earlier]
        operands += [one[2] for one in earlier]
        copies = count + sum(number for _, number in ranges)
        scratch = [pltpu.VMEM(blocks, queries.dtype), pltpu.SemaphoreType.DMA((copies,))]
        out_specs = pl.BlockSpec(memory_space=pl.ANY)
        out_shape = jax.ShapeDtypeStruct(queries.shape, queries.dtype)
    return pl.pallas_call(
        functools.partial(attend_kernel, LOG2_E / HD**0.5, halves, heads, first_column * HD, width, ranges),
        in_specs=[pl.BlockSpec(memory_space=pltpu.VMEM) for _ in operands],
        out_specs=out_specs,
        out_shape=out_shape,
        scratch_shapes=scratch,
        compiler_params=pltpu.CompilerParams(vmem_limit_bytes=VMEM_LIMIT),
        cost_estimate=pl.CostEstimate(
            flops=4 * keys * rows * width * count,
            bytes_accessed=4 * rows * width * count,
            transcendentals=keys * rows * width // HD * count,
        ),
        name="attend_heads",
    )(*operands)


class Places:
    def __init__(self, devices):
        self.devices = devices
        self.levels = devices // (CORES * COLUMNS)

    def split(self, index):
        if isinstance(index, int):
            return index // (CORES * COLUMNS), index // CORES % COLUMNS, index % CORES
        chip = lax.div(index, CORES)
        return lax.div(chip, COLUMNS), lax.rem(chip, COLUMNS), lax.rem(index, CORES)

    def swapped(self, array, level=0, column=0, core=0):
        pairs = []
        for index in range(self.devices):
            z, y, c = self.split(index)
            z, y, c = z ^ level, y ^ column, c ^ core
            pairs.append((index, (z * COLUMNS + y) * CORES + c))
        return lax.ppermute(array, "ctx", pairs)

    def over_levels(self, array):
        return [array] + [self.swapped(array, level=s) for s in range(1, self.levels)]


def over_chips(places, rows):
    chips = [rows, places.swapped(rows, column=1)]
    return chips + [places.swapped(one, core=1) for one in chips]


def chosen(flag, mine, got, starts, sizes):
    return jnp.where(flag, lax.dynamic_slice(mine, starts, sizes), lax.dynamic_slice(got, starts, sizes))


def halved(part, at):
    rows = part.shape[1] // 2
    return lax.dynamic_slice_in_dim(part, at * rows, rows, 1)


def for_levels(places, part):
    z, _, _ = places.split(lax.axis_index("ctx"))
    rows = part.shape[1] // places.levels
    return [
        lax.dynamic_slice_in_dim(part, (z ^ s) * rows, rows, 1).reshape(2 * rows, -1) for s in range(places.levels)
    ]


def from_owner(distance, mine, got):
    piece = mine
    for s, one in enumerate(got, 1):
        piece = jnp.where(distance == s, one, piece)
    return piece


def owned_rows(pool, owners):
    owned = (owners == lax.axis_index("ctx"))[:, None, None]
    return lax.psum(jnp.where(owned, pool[0], 0), "ctx").reshape(-1, pool.shape[-1])


def body(queries, new_keys, new_values, prefix_keys, prefix_values, pool_keys, pool_values, owners, lengths, devices):
    kv_heads = new_keys.shape[1] // HD
    blocks, block_rows = pool_keys.shape[1:3]
    length = jnp.broadcast_to(lengths[:, None], (1, HD))
    chips = devices // CORES
    levels = chips // COLUMNS
    by_permutes = (
        blocks == CORES
        and chips % COLUMNS == 0
        and levels > 1
        and levels & (levels - 1) == 0
        and block_rows % (16 * chips) == 0
        and kv_heads % 2 == 0
    )
    if not by_permutes:
        pre_k, pre_v = (lax.all_gather(rows, "ctx", axis=0, tiled=True) for rows in (prefix_keys, prefix_values))
        shared = jnp.concatenate([owned_rows(pool_keys, owners), owned_rows(pool_values, owners)])
        pieces = [(shared, shared.shape[0] // 2)]
        own = (new_keys, new_values, pre_k, pre_v)
        return attend(queries, own, pieces, length, (0, kv_heads), 0, kv_heads)
    places = Places(devices)
    z, y, c = places.split(lax.axis_index("ctx"))
    owner = jnp.where(c == 0, owners[0], owners[1])
    owner_z, owner_y, owner_c = places.split(owner)
    pools = [(pool[0], places.swapped(pool[0], core=1)) for pool in (pool_keys, pool_values)]
    count = kv_heads // 2
    part = block_rows // COLUMNS
    tied = lax.optimization_barrier

    def cut(pools, column, first):
        sizes = (1, part, count * HD)
        rows = [chosen(owner_c == c, *pool, (c, column * part, first * HD), sizes) for pool in pools]
        return jnp.concatenate(rows)

    sent = [cut(pools, 1 - y, 0)]
    sent[0], pools = tied((sent[0], pools))
    sent.append(cut(pools, 1 - y, count))
    prefix, sent[1] = tied((jnp.concatenate([prefix_keys, prefix_values]), sent[1]))
    got = [places.swapped(one, column=1) for one in sent]
    step = 1
    while step < levels:
        prefix = [prefix, places.swapped(prefix, level=step)]
        step *= 2
        prefix = jnp.concatenate(prefix) if step < levels else prefix

    def over_z(cuts):
        return [places.swapped(one, level=s) for s, one in enumerate(cuts) if s]

    first_cuts = for_levels(places, jnp.where(owner_y == y, cut(pools, y, 0), got[0]))
    first_got = over_z(first_cuts)
    *low, high = [1 << k for k in range(levels.bit_length() - 1)]
    last = jnp.where(owner_y == y, cut(pools, y, count), got[1])
    for distance in low:
        bit = (z // distance) & 1
        swap = places.swapped(halved(last, 1 - bit), level=distance)
        last = jnp.where((owner_z ^ z) & distance == 0, halved(last, bit), swap)
    prefix, first_got[-1] = tied((prefix, first_got[-1]))
    prefix = jnp.concatenate(prefix)
    prefix = [prefix, places.swapped(prefix, column=1)]
    piece = from_owner(z ^ owner_z, first_cuts[0], first_got)
    early = places.swapped(piece, column=1)
    prefix, early = tied((prefix, early))
    last = jnp.where((owner_z ^ z) & high == 0, last, places.swapped(last, level=high))
    early, last = tied((early, last))
    gathered = places.over_levels(piece)
    last_half = last.shape[1]
    last_rows = [last.reshape(-1, last.shape[-1])]
    last_early = places.swapped(last_rows[0], column=1)
    for distance in reversed(low):
        last_rows.append(places.swapped(jnp.concatenate(last_rows), level=distance))
    across = places.swapped(jnp.concatenate(gathered[1:]), column=1)
    prefix, early, gathered[0] = tied((prefix, early, gathered[0]))
    last_across = places.swapped(jnp.concatenate(last_rows[1:]), column=1)
    mine = jnp.concatenate(gathered + [early])
    last_mine = jnp.concatenate(last_rows + [last_early])
    prefix = jnp.concatenate(prefix)
    prefix = jnp.concatenate([prefix, places.swapped(prefix, core=1)])
    prefix = prefix.reshape(devices, 2, -1, prefix.shape[-1])
    own = (new_keys, new_values) + tuple(prefix[:, i].reshape(-1, prefix.shape[-1]) for i in range(2))

    def arrived(half, *rows):
        return [(one, half) for one in rows + tuple(places.swapped(one, core=1) for one in rows)]

    first = arrived(piece.shape[0] // 2, mine, across)
    blocks = attend(queries, own, first, length, (0, count - 1), 0, kv_heads, None)
    last_across, blocks, turn = tied((last_across, blocks, length))
    last = arrived(last_half, last_mine, last_across)
    earlier = [(0, count - 1, blocks)]
    earlier.append((count - 1, 1, attend(queries, own, first, turn, (count - 1, 1), 0, kv_heads, None)))
    return attend(queries, own, last, length, (count, kv_heads - count), count, kv_heads, earlier)


def solution(mesh):
    both = ("groups", "ctx")
    placed = (P(both, None),) * 5 + (P(both, None, None, None),) * 2 + (P("groups"), P(both))
    return jax.shard_map(
        functools.partial(body, devices=mesh.shape["ctx"]),
        mesh=mesh,
        in_specs=placed,
        out_specs=P(both, None),
        check_vma=False,
    )
```

```python
import functools

import jax
import jax.numpy as jnp
from jax import lax
from jax.experimental import pallas as pl
from jax.experimental.pallas import tpu as pltpu
from jax.sharding import PartitionSpec as P

HD = 128
CORES = 2
COLUMNS = 2
COPIES = 4
LOG2_E = 1.4426950408889634
VMEM_LIMIT = 24 * 1024 * 1024


def attend_kernel(scale, halves, heads, first_column, width, earlier, length_ref, queries_ref, *rest):
    own_refs, piece_refs = rest[:4], rest[4 : 4 + len(halves)]
    first, count = heads
    rows = queries_ref.shape[0]
    if earlier is None:
        blocks_ref = rest[-1]
    else:
        earlier_refs = rest[4 + len(halves) : 4 + len(halves) + len(earlier)]
        out_ref, blocks_ref, sent_sems = rest[-3:]
    group = width // HD
    length = length_ref[...]
    query_at = lax.broadcasted_iota(jnp.int32, (rows, rows), 0)
    key_at = lax.broadcasted_iota(jnp.int32, (rows, rows), 1)
    seen = (key_at <= query_at) & (key_at < length)
    live = lax.broadcasted_iota(jnp.int32, (rows, HD), 0) < length

    def copied(source, head, sem):
        target = out_ref.at[:, pl.ds(pl.multiple_of(head * width, width), width)]
        return pltpu.make_async_copy(source, target, sent_sems.at[sem])

    def copied_part(h, part):
        size = width // COPIES
        target = out_ref.at[:, pl.ds(pl.multiple_of((first + h) * width + part * size, size), size)]
        source = blocks_ref.at[h, :, part * size : (part + 1) * size]
        return pltpu.make_async_copy(source, target, sent_sems.at[h * COPIES + part])

    kept = []
    if earlier is not None:
        for ref, (at, number) in zip(earlier_refs, earlier):
            kept += [copied(ref.at[h], at + h, count * COPIES + len(kept) + h) for h in range(number)]
    for copy in kept:
        copy.start()

    def one_head(h, _):
        column = pl.ds(pl.multiple_of((first + h) * HD, HD), HD)
        local = pl.ds(pl.multiple_of((first + h) * HD - first_column, HD), HD)
        shared = [ref[:, local].reshape(-1, 2, half, HD) for ref, half in zip(piece_refs, halves)]
        keys = jnp.concatenate([ref[:, column] for ref in own_refs[::2]] + [one[:, 0].reshape(-1, HD) for one in shared])
        values = [ref[:, column] for ref in own_refs[1::2]] + [one[:, 1].reshape(-1, HD) for one in shared]
        values = jnp.concatenate(values)
        turned = keys.T

        def scored(g):
            asked = queries_ref[:, pl.ds(pl.multiple_of((first + h) * width + g * HD, HD), HD)]
            return jnp.dot(asked, turned, preferred_element_type=jnp.float32)

        def weighed(scores):
            scores = jnp.concatenate([jnp.where(seen, scores[:, :rows], -1e30), scores[:, rows:]], axis=1)
            top = jnp.max(scores, axis=1, keepdims=True)
            weights = jnp.exp2((scores - top) * scale)
            return weights.astype(jnp.bfloat16), jnp.sum(weights, axis=1, keepdims=True)

        def stored(g, weights, total):
            summed = jnp.dot(weights, values, preferred_element_type=jnp.float32)
            inverse = pl.reciprocal(total, approx=True)
            inverse *= 2.0 - total * inverse
            shown = jnp.where(live, summed * inverse, 0.0)
            blocks_ref[h, :, g * HD : (g + 1) * HD] = shown.astype(jnp.bfloat16)
            if earlier is not None and (g + 1) * COPIES % group == 0:
                copied_part(h, (g + 1) * COPIES // group - 1).start()

        scores, weights = scored(0), None
        for g in range(group):
            ahead = scored(g + 1) if g + 1 < group else None
            if weights is not None:
                stored(g - 1, *weights)
            weights = weighed(scores)
            scores = ahead
        stored(group - 1, *weights)
        return _

    lax.fori_loop(0, count, one_head, 0)
    if earlier is not None:
        kept += [copied_part(h, part) for h in range(count) for part in range(COPIES)]
    for copy in kept:
        copy.wait()


def attend(queries, own, pieces, length, heads, first_column, kv_heads, earlier=()):
    rows = queries.shape[0]
    width = queries.shape[1] // kv_heads
    count = heads[1]
    halves = [half for _, half in pieces]
    arrays = [array for array, _ in pieces]
    keys = sum(array.shape[0] for array in own[::2]) + sum(array.shape[0] for array in arrays) // 2
    operands = [length, queries, *own, *arrays]
    blocks = (count, rows, width)
    if earlier is None:
        ranges, scratch = None, []
        out_specs = pl.BlockSpec(memory_space=pltpu.VMEM)
        out_shape = jax.ShapeDtypeStruct(blocks, queries.dtype)
    else:
        ranges = [one[:2] for one in earlier]
        operands += [one[2] for one in earlier]
        copies = count * COPIES + sum(number for _, number in ranges)
        scratch = [pltpu.VMEM(blocks, queries.dtype), pltpu.SemaphoreType.DMA((copies,))]
        out_specs = pl.BlockSpec(memory_space=pl.ANY)
        out_shape = jax.ShapeDtypeStruct(queries.shape, queries.dtype)
    return pl.pallas_call(
        functools.partial(attend_kernel, LOG2_E / HD**0.5, halves, heads, first_column * HD, width, ranges),
        in_specs=[pl.BlockSpec(memory_space=pltpu.VMEM) for _ in operands],
        out_specs=out_specs,
        out_shape=out_shape,
        scratch_shapes=scratch,
        compiler_params=pltpu.CompilerParams(vmem_limit_bytes=VMEM_LIMIT),
        cost_estimate=pl.CostEstimate(
            flops=4 * keys * rows * width * count,
            bytes_accessed=4 * rows * width * count,
            transcendentals=keys * rows * width // HD * count,
        ),
        name="attend_heads",
    )(*operands)


class Places:
    def __init__(self, devices):
        self.devices = devices
        self.levels = devices // (CORES * COLUMNS)

    def split(self, index):
        if isinstance(index, int):
            return index // (CORES * COLUMNS), index // CORES % COLUMNS, index % CORES
        chip = lax.div(index, CORES)
        return lax.div(chip, COLUMNS), lax.rem(chip, COLUMNS), lax.rem(index, CORES)

    def swapped(self, array, level=0, column=0, core=0):
        pairs = []
        for index in range(self.devices):
            z, y, c = self.split(index)
            z, y, c = z ^ level, y ^ column, c ^ core
            pairs.append((index, (z * COLUMNS + y) * CORES + c))
        return lax.ppermute(array, "ctx", pairs)

    def over_levels(self, array):
        return [array] + [self.swapped(array, level=s) for s in range(1, self.levels)]


def over_chips(places, rows):
    chips = [rows, places.swapped(rows, column=1)]
    return chips + [places.swapped(one, core=1) for one in chips]


def chosen(flag, mine, got, starts, sizes):
    return jnp.where(flag, lax.dynamic_slice(mine, starts, sizes), lax.dynamic_slice(got, starts, sizes))


def halved(part, at):
    rows = part.shape[1] // 2
    return lax.dynamic_slice_in_dim(part, at * rows, rows, 1)


def for_levels(places, part):
    z, _, _ = places.split(lax.axis_index("ctx"))
    rows = part.shape[1] // places.levels
    return [
        lax.dynamic_slice_in_dim(part, (z ^ s) * rows, rows, 1).reshape(2 * rows, -1) for s in range(places.levels)
    ]


def from_owner(distance, mine, got):
    piece = mine
    for s, one in enumerate(got, 1):
        piece = jnp.where(distance == s, one, piece)
    return piece


def owned_rows(pool, owners):
    owned = (owners == lax.axis_index("ctx"))[:, None, None]
    return lax.psum(jnp.where(owned, pool[0], 0), "ctx").reshape(-1, pool.shape[-1])


def body(queries, new_keys, new_values, prefix_keys, prefix_values, pool_keys, pool_values, owners, lengths, devices):
    kv_heads = new_keys.shape[1] // HD
    blocks, block_rows = pool_keys.shape[1:3]
    length = jnp.broadcast_to(lengths[:, None], (1, HD))
    chips = devices // CORES
    levels = chips // COLUMNS
    by_permutes = (
        blocks == CORES
        and chips % COLUMNS == 0
        and levels > 1
        and levels & (levels - 1) == 0
        and block_rows % (16 * chips) == 0
        and kv_heads % 2 == 0
    )
    if not by_permutes:
        pre_k, pre_v = (lax.all_gather(rows, "ctx", axis=0, tiled=True) for rows in (prefix_keys, prefix_values))
        shared = jnp.concatenate([owned_rows(pool_keys, owners), owned_rows(pool_values, owners)])
        pieces = [(shared, shared.shape[0] // 2)]
        own = (new_keys, new_values, pre_k, pre_v)
        return attend(queries, own, pieces, length, (0, kv_heads), 0, kv_heads)
    places = Places(devices)
    z, y, c = places.split(lax.axis_index("ctx"))
    owner = jnp.where(c == 0, owners[0], owners[1])
    owner_z, owner_y, owner_c = places.split(owner)
    pools = [(pool[0], places.swapped(pool[0], core=1)) for pool in (pool_keys, pool_values)]
    count = kv_heads // 2
    part = block_rows // COLUMNS
    tied = lax.optimization_barrier

    def cut(pools, column, first):
        sizes = (1, part, count * HD)
        rows = [chosen(owner_c == c, *pool, (c, column * part, first * HD), sizes) for pool in pools]
        return jnp.concatenate(rows)

    sent = [cut(pools, 1 - y, 0)]
    sent[0], pools = tied((sent[0], pools))
    sent.append(cut(pools, 1 - y, count))
    prefix, sent[1] = tied(((prefix_keys, prefix_values), sent[1]))
    prefix = jnp.concatenate(prefix)
    got = [places.swapped(one, column=1) for one in sent]
    step = 1
    while step < levels:
        prefix = [prefix, places.swapped(prefix, level=step)]
        step *= 2
        prefix = jnp.concatenate(prefix) if step < levels else prefix

    def over_z(cuts):
        return [places.swapped(one, level=s) for s, one in enumerate(cuts) if s]

    first_cuts = for_levels(places, jnp.where(owner_y == y, cut(pools, y, 0), got[0]))
    first_got = over_z(first_cuts)
    *low, high = [1 << k for k in range(levels.bit_length() - 1)]
    last = jnp.where(owner_y == y, cut(pools, y, count), got[1])
    for distance in low:
        bit = (z // distance) & 1
        swap = places.swapped(halved(last, 1 - bit), level=distance)
        last = jnp.where((owner_z ^ z) & distance == 0, halved(last, bit), swap)
    prefix, first_got[-1] = tied((prefix, first_got[-1]))
    prefix = jnp.concatenate(prefix)
    prefix = [prefix, places.swapped(prefix, column=1)]
    piece = from_owner(z ^ owner_z, first_cuts[0], first_got)
    early = places.swapped(piece, column=1)
    prefix, early = tied((prefix, early))
    last = jnp.where((owner_z ^ z) & high == 0, last, places.swapped(last, level=high))
    early, last = tied((early, last))
    gathered = places.over_levels(piece)
    last_half = last.shape[1]
    last_rows = [last.reshape(-1, last.shape[-1])]
    last_early = places.swapped(last_rows[0], column=1)
    last_across = []
    for distance in reversed(low):
        rows = jnp.concatenate(last_rows)
        last_rows.append(places.swapped(rows, level=distance))
        last_across.append(places.swapped(rows, level=distance, column=1))
    last_across = jnp.concatenate(last_across)
    across = places.swapped(jnp.concatenate(gathered[1:]), column=1)
    prefix, early, gathered[0] = tied((prefix, early, gathered[0]))
    mine = jnp.concatenate(gathered + [early])
    last_mine = jnp.concatenate(last_rows + [last_early])
    prefix = jnp.concatenate(prefix)
    prefix = jnp.concatenate([prefix, places.swapped(prefix, core=1)])
    prefix = prefix.reshape(devices, 2, -1, prefix.shape[-1])
    own = (new_keys, new_values) + tuple(prefix[:, i].reshape(-1, prefix.shape[-1]) for i in range(2))

    def arrived(half, *rows):
        return [(one, half) for one in rows + tuple(places.swapped(one, core=1) for one in rows)]

    first = arrived(piece.shape[0] // 2, mine, across)
    blocks = attend(queries, own, first, length, (0, count - 1), 0, kv_heads, None)
    last_across, blocks, turn = tied((last_across, blocks, length))
    last = arrived(last_half, last_mine, last_across)
    earlier = [(0, count - 1, blocks)]
    earlier.append((count - 1, 1, attend(queries, own, first, turn, (count - 1, 1), 0, kv_heads, None)))
    return attend(queries, own, last, length, (count, kv_heads - count), count, kv_heads, earlier)


def solution(mesh):
    both = ("groups", "ctx")
    placed = (P(both, None),) * 5 + (P(both, None, None, None),) * 2 + (P("groups"), P(both))
    return jax.shard_map(
        functools.partial(body, devices=mesh.shape["ctx"]),
        mesh=mesh,
        in_specs=placed,
        out_specs=P(both, None),
        check_vma=False,
    )
```

```python
import functools

import jax
import jax.numpy as jnp
from jax import lax
from jax.experimental import pallas as pl
from jax.experimental.pallas import tpu as pltpu
from jax.sharding import PartitionSpec as P

HD = 128
CORES = 2
COLUMNS = 2
LOG2_E = 1.4426950408889634
VMEM_LIMIT = 24 * 1024 * 1024


def attend_kernel(scale, halves, heads, first_column, width, earlier, length_ref, queries_ref, *rest):
    own_refs, piece_refs = rest[:4], rest[4 : 4 + len(halves)]
    first, count = heads
    rows = queries_ref.shape[0]
    if earlier is None:
        blocks_ref = rest[-1]
    else:
        earlier_refs = rest[4 + len(halves) : 4 + len(halves) + len(earlier)]
        out_ref, blocks_ref, sent_sems = rest[-3:]
    group = width // HD
    length = length_ref[...]
    query_at = lax.broadcasted_iota(jnp.int32, (rows, rows), 0)
    key_at = lax.broadcasted_iota(jnp.int32, (rows, rows), 1)
    seen = (key_at <= query_at) & (key_at < length)
    live = lax.broadcasted_iota(jnp.int32, (rows, HD), 0) < length

    def copied(source, head, sem):
        target = out_ref.at[:, pl.ds(pl.multiple_of(head * width, width), width)]
        return pltpu.make_async_copy(source, target, sent_sems.at[sem])

    kept = []
    if earlier is not None:
        for ref, (at, number) in zip(earlier_refs, earlier):
            kept += [copied(ref.at[h], at + h, count + len(kept) + h) for h in range(number)]
    for copy in kept:
        copy.start()

    def one_head(h, _):
        column = pl.ds(pl.multiple_of((first + h) * HD, HD), HD)
        local = pl.ds(pl.multiple_of((first + h) * HD - first_column, HD), HD)
        shared = [ref[:, local].reshape(-1, 2, half, HD) for ref, half in zip(piece_refs, halves)]
        keys = jnp.concatenate([ref[:, column] for ref in own_refs[::2]] + [one[:, 0].reshape(-1, HD) for one in shared])
        values = [ref[:, column] for ref in own_refs[1::2]] + [one[:, 1].reshape(-1, HD) for one in shared]
        values = jnp.concatenate(values)
        turned = keys.T

        def scored(g):
            asked = queries_ref[:, pl.ds(pl.multiple_of((first + h) * width + g * HD, HD), HD)]
            return jnp.dot(asked, turned, preferred_element_type=jnp.float32)

        def weighed(scores):
            scores = jnp.concatenate([jnp.where(seen, scores[:, :rows], -1e30), scores[:, rows:]], axis=1)
            top = jnp.max(scores, axis=1, keepdims=True)
            weights = jnp.exp2((scores - top) * scale)
            return weights.astype(jnp.bfloat16), jnp.sum(weights, axis=1, keepdims=True)

        def stored(g, weights, total):
            summed = jnp.dot(weights, values, preferred_element_type=jnp.float32)
            inverse = pl.reciprocal(total, approx=True)
            inverse *= 2.0 - total * inverse
            shown = jnp.where(live, summed * inverse, 0.0)
            blocks_ref[h, :, g * HD : (g + 1) * HD] = shown.astype(jnp.bfloat16)

        scores, weights = scored(0), None
        for g in range(group):
            ahead = scored(g + 1) if g + 1 < group else None
            if weights is not None:
                stored(g - 1, *weights)
            weights = weighed(scores)
            scores = ahead
        stored(group - 1, *weights)
        if earlier is not None:
            copied(blocks_ref.at[h], first + h, h).start()
        return _

    lax.fori_loop(0, count, one_head, 0)
    if earlier is not None:
        kept += [copied(blocks_ref.at[h], first + h, h) for h in range(count)]
    for copy in kept:
        copy.wait()


def attend(queries, own, pieces, length, heads, first_column, kv_heads, earlier=()):
    rows = queries.shape[0]
    width = queries.shape[1] // kv_heads
    count = heads[1]
    halves = [half for _, half in pieces]
    arrays = [array for array, _ in pieces]
    keys = sum(array.shape[0] for array in own[::2]) + sum(array.shape[0] for array in arrays) // 2
    operands = [length, queries, *own, *arrays]
    blocks = (count, rows, width)
    if earlier is None:
        ranges, scratch = None, []
        out_specs = pl.BlockSpec(memory_space=pltpu.VMEM)
        out_shape = jax.ShapeDtypeStruct(blocks, queries.dtype)
    else:
        ranges = [one[:2] for one in earlier]
        operands += [one[2] for one in earlier]
        copies = count + sum(number for _, number in ranges)
        scratch = [pltpu.VMEM(blocks, queries.dtype), pltpu.SemaphoreType.DMA((copies,))]
        out_specs = pl.BlockSpec(memory_space=pl.ANY)
        out_shape = jax.ShapeDtypeStruct(queries.shape, queries.dtype)
    return pl.pallas_call(
        functools.partial(attend_kernel, LOG2_E / HD**0.5, halves, heads, first_column * HD, width, ranges),
        in_specs=[pl.BlockSpec(memory_space=pltpu.VMEM) for _ in operands],
        out_specs=out_specs,
        out_shape=out_shape,
        scratch_shapes=scratch,
        compiler_params=pltpu.CompilerParams(vmem_limit_bytes=VMEM_LIMIT),
        cost_estimate=pl.CostEstimate(
            flops=4 * keys * rows * width * count,
            bytes_accessed=4 * rows * width * count,
            transcendentals=keys * rows * width // HD * count,
        ),
        name="attend_heads",
    )(*operands)


class Places:
    def __init__(self, devices):
        self.devices = devices
        self.levels = devices // (CORES * COLUMNS)

    def split(self, index):
        if isinstance(index, int):
            return index // (CORES * COLUMNS), index // CORES % COLUMNS, index % CORES
        chip = lax.div(index, CORES)
        return lax.div(chip, COLUMNS), lax.rem(chip, COLUMNS), lax.rem(index, CORES)

    def swapped(self, array, level=0, column=0, core=0):
        pairs = []
        for index in range(self.devices):
            z, y, c = self.split(index)
            z, y, c = z ^ level, y ^ column, c ^ core
            pairs.append((index, (z * COLUMNS + y) * CORES + c))
        return lax.ppermute(array, "ctx", pairs)

    def over_levels(self, array):
        return [array] + [self.swapped(array, level=s) for s in range(1, self.levels)]


def over_chips(places, rows):
    chips = [rows, places.swapped(rows, column=1)]
    return chips + [places.swapped(one, core=1) for one in chips]


def chosen(flag, mine, got, starts, sizes):
    return jnp.where(flag, lax.dynamic_slice(mine, starts, sizes), lax.dynamic_slice(got, starts, sizes))


def halved(part, at):
    rows = part.shape[1] // 2
    return lax.dynamic_slice_in_dim(part, at * rows, rows, 1)


def for_levels(places, part):
    z, _, _ = places.split(lax.axis_index("ctx"))
    rows = part.shape[1] // places.levels
    return [
        lax.dynamic_slice_in_dim(part, (z ^ s) * rows, rows, 1).reshape(2 * rows, -1) for s in range(places.levels)
    ]


def from_owner(distance, mine, got):
    piece = mine
    for s, one in enumerate(got, 1):
        piece = jnp.where(distance == s, one, piece)
    return piece


def owned_rows(pool, owners):
    owned = (owners == lax.axis_index("ctx"))[:, None, None]
    return lax.psum(jnp.where(owned, pool[0], 0), "ctx").reshape(-1, pool.shape[-1])


def body(queries, new_keys, new_values, prefix_keys, prefix_values, pool_keys, pool_values, owners, lengths, devices):
    kv_heads = new_keys.shape[1] // HD
    blocks, block_rows = pool_keys.shape[1:3]
    length = jnp.broadcast_to(lengths[:, None], (1, HD))
    chips = devices // CORES
    levels = chips // COLUMNS
    by_permutes = (
        blocks == CORES
        and chips % COLUMNS == 0
        and levels > 1
        and levels & (levels - 1) == 0
        and block_rows % (16 * chips) == 0
        and kv_heads % 2 == 0
    )
    if not by_permutes:
        pre_k, pre_v = (lax.all_gather(rows, "ctx", axis=0, tiled=True) for rows in (prefix_keys, prefix_values))
        shared = jnp.concatenate([owned_rows(pool_keys, owners), owned_rows(pool_values, owners)])
        pieces = [(shared, shared.shape[0] // 2)]
        own = (new_keys, new_values, pre_k, pre_v)
        return attend(queries, own, pieces, length, (0, kv_heads), 0, kv_heads)
    places = Places(devices)
    z, y, c = places.split(lax.axis_index("ctx"))
    owner = jnp.where(c == 0, owners[0], owners[1])
    owner_z, owner_y, owner_c = places.split(owner)
    pools = [(pool[0], places.swapped(pool[0], core=1)) for pool in (pool_keys, pool_values)]
    count = kv_heads // 2
    part = block_rows // COLUMNS
    tied = lax.optimization_barrier

    def cut(pools, column, first):
        sizes = (1, part, count * HD)
        rows = [chosen(owner_c == c, *pool, (c, column * part, first * HD), sizes) for pool in pools]
        return jnp.concatenate(rows)

    at, sizes = (c, (1 - y) * part, 0), (1, part, count * HD)
    mine = [lax.dynamic_slice(pool, at, sizes) for pool, _ in pools]
    mine, pools = tied((mine, pools))
    rows = [jnp.where(owner_c == c, one, lax.dynamic_slice(got, at, sizes)) for one, (_, got) in zip(mine, pools)]
    sent = [jnp.concatenate(rows)]
    sent[0], pools, prefix = tied((sent[0], pools, (prefix_keys, prefix_values)))
    prefix = jnp.concatenate(prefix)
    sent.append(cut(pools, 1 - y, count))
    prefix, sent[1] = tied((prefix, sent[1]))
    got = [places.swapped(one, column=1) for one in sent]
    step = 1
    while step < levels:
        prefix = [prefix, places.swapped(prefix, level=step)]
        step *= 2
        prefix = jnp.concatenate(prefix) if step < levels else prefix

    def over_z(cuts):
        return [places.swapped(one, level=s) for s, one in enumerate(cuts) if s]

    first_cuts = for_levels(places, jnp.where(owner_y == y, cut(pools, y, 0), got[0]))
    first_got = over_z(first_cuts)
    *low, high = [1 << k for k in range(levels.bit_length() - 1)]
    last = jnp.where(owner_y == y, cut(pools, y, count), got[1])
    for distance in low:
        bit = (z // distance) & 1
        swap = places.swapped(halved(last, 1 - bit), level=distance)
        last = jnp.where((owner_z ^ z) & distance == 0, halved(last, bit), swap)
    prefix, first_got[-1] = tied((prefix, first_got[-1]))
    prefix = jnp.concatenate(prefix)
    prefix = [prefix, places.swapped(prefix, column=1)]
    piece = from_owner(z ^ owner_z, first_cuts[0], first_got)
    early = places.swapped(piece, column=1)
    prefix, early = tied((prefix, early))
    last = jnp.where((owner_z ^ z) & high == 0, last, places.swapped(last, level=high))
    early, last = tied((early, last))
    gathered = places.over_levels(piece)
    last_half = last.shape[1]
    last_rows = [last.reshape(-1, last.shape[-1])]
    last_early = places.swapped(last_rows[0], column=1)
    for distance in reversed(low):
        last_rows.append(places.swapped(jnp.concatenate(last_rows), level=distance))
    across = places.swapped(jnp.concatenate(gathered[1:]), column=1)
    prefix, early, gathered[0] = tied((prefix, early, gathered[0]))
    last_across = places.swapped(jnp.concatenate(last_rows[1:]), column=1)
    mine = jnp.concatenate(gathered + [early])
    last_mine = jnp.concatenate(last_rows + [last_early])
    prefix = jnp.concatenate(prefix)
    prefix = jnp.concatenate([prefix, places.swapped(prefix, core=1)])
    prefix = prefix.reshape(devices, 2, -1, prefix.shape[-1])
    own = (new_keys, new_values) + tuple(prefix[:, i].reshape(-1, prefix.shape[-1]) for i in range(2))

    def arrived(half, *rows):
        return [(one, half) for one in rows + tuple(places.swapped(one, core=1) for one in rows)]

    first = arrived(piece.shape[0] // 2, mine, across)
    blocks = attend(queries, own, first, length, (0, count - 1), 0, kv_heads, None)
    last_across, blocks, turn = tied((last_across, blocks, length))
    last = arrived(last_half, last_mine, last_across)
    earlier = [(0, count - 1, blocks)]
    earlier.append((count - 1, 1, attend(queries, own, first, turn, (count - 1, 1), 0, kv_heads, None)))
    return attend(queries, own, last, length, (count, kv_heads - count), count, kv_heads, earlier)


def solution(mesh):
    both = ("groups", "ctx")
    placed = (P(both, None),) * 5 + (P(both, None, None, None),) * 2 + (P("groups"), P(both))
    return jax.shard_map(
        functools.partial(body, devices=mesh.shape["ctx"]),
        mesh=mesh,
        in_specs=placed,
        out_specs=P(both, None),
        check_vma=False,
    )
```

```python
import functools

import jax
import jax.numpy as jnp
from jax import lax
from jax.experimental import pallas as pl
from jax.experimental.pallas import tpu as pltpu
from jax.sharding import PartitionSpec as P

HD = 128
CORES = 2
COLUMNS = 2
LOG2_E = 1.4426950408889634
VMEM_LIMIT = 24 * 1024 * 1024


def attend_kernel(scale, halves, heads, first_column, width, earlier, length_ref, queries_ref, *rest):
    own_refs, piece_refs = rest[:4], rest[4 : 4 + len(halves)]
    first, count = heads
    rows = queries_ref.shape[0]
    if earlier is None:
        blocks_ref = rest[-1]
    else:
        earlier_refs = rest[4 + len(halves) : 4 + len(halves) + len(earlier)]
        out_ref, blocks_ref, sent_sems = rest[-3:]
    group = width // HD
    length = length_ref[...]
    query_at = lax.broadcasted_iota(jnp.int32, (rows, rows), 0)
    key_at = lax.broadcasted_iota(jnp.int32, (rows, rows), 1)
    seen = (key_at <= query_at) & (key_at < length)
    live = lax.broadcasted_iota(jnp.int32, (rows, HD), 0) < length

    def copied(source, head, sem):
        target = out_ref.at[:, pl.ds(pl.multiple_of(head * width, width), width)]
        return pltpu.make_async_copy(source, target, sent_sems.at[sem])

    kept = []
    if earlier is not None:
        for ref, (at, number) in zip(earlier_refs, earlier):
            kept += [copied(ref.at[h], at + h, count + len(kept) + h) for h in range(number)]
    for copy in kept:
        copy.start()

    def one_head(h, _):
        column = pl.ds(pl.multiple_of((first + h) * HD, HD), HD)
        local = pl.ds(pl.multiple_of((first + h) * HD - first_column, HD), HD)
        shared = [ref[:, local].reshape(-1, 2, half, HD) for ref, half in zip(piece_refs, halves)]
        keys = jnp.concatenate([ref[:, column] for ref in own_refs[::2]] + [one[:, 0].reshape(-1, HD) for one in shared])
        values = [ref[:, column] for ref in own_refs[1::2]] + [one[:, 1].reshape(-1, HD) for one in shared]
        values = jnp.concatenate(values)
        turned = keys.T

        def scored(g):
            asked = queries_ref[:, pl.ds(pl.multiple_of((first + h) * width + g * HD, HD), HD)]
            return jnp.dot(asked, turned, preferred_element_type=jnp.float32)

        def weighed(scores):
            scores = jnp.concatenate([jnp.where(seen, scores[:, :rows], -1e30), scores[:, rows:]], axis=1)
            top = jnp.max(scores, axis=1, keepdims=True)
            weights = jnp.exp2((scores - top) * scale)
            return weights.astype(jnp.bfloat16), jnp.sum(weights, axis=1, keepdims=True)

        def stored(g, weights, total):
            summed = jnp.dot(weights, values, preferred_element_type=jnp.float32)
            inverse = pl.reciprocal(total, approx=True)
            inverse *= 2.0 - total * inverse
            shown = jnp.where(live, summed * inverse, 0.0)
            blocks_ref[h, :, g * HD : (g + 1) * HD] = shown.astype(jnp.bfloat16)

        scores, weights = scored(0), None
        for g in range(group):
            ahead = scored(g + 1) if g + 1 < group else None
            if weights is not None:
                stored(g - 1, *weights)
            weights = weighed(scores)
            scores = ahead
        stored(group - 1, *weights)
        if earlier is not None:
            copied(blocks_ref.at[h], first + h, h).start()
        return _

    lax.fori_loop(0, count, one_head, 0)
    if earlier is not None:
        kept += [copied(blocks_ref.at[h], first + h, h) for h in range(count)]
    for copy in kept:
        copy.wait()


def attend(queries, own, pieces, length, heads, first_column, kv_heads, earlier=()):
    rows = queries.shape[0]
    width = queries.shape[1] // kv_heads
    count = heads[1]
    halves = [half for _, half in pieces]
    arrays = [array for array, _ in pieces]
    keys = sum(array.shape[0] for array in own[::2]) + sum(array.shape[0] for array in arrays) // 2
    operands = [length, queries, *own, *arrays]
    blocks = (count, rows, width)
    if earlier is None:
        ranges, scratch = None, []
        out_specs = pl.BlockSpec(memory_space=pltpu.VMEM)
        out_shape = jax.ShapeDtypeStruct(blocks, queries.dtype)
    else:
        ranges = [one[:2] for one in earlier]
        operands += [one[2] for one in earlier]
        copies = count + sum(number for _, number in ranges)
        scratch = [pltpu.VMEM(blocks, queries.dtype), pltpu.SemaphoreType.DMA((copies,))]
        out_specs = pl.BlockSpec(memory_space=pl.ANY)
        out_shape = jax.ShapeDtypeStruct(queries.shape, queries.dtype)
    return pl.pallas_call(
        functools.partial(attend_kernel, LOG2_E / HD**0.5, halves, heads, first_column * HD, width, ranges),
        in_specs=[pl.BlockSpec(memory_space=pltpu.VMEM) for _ in operands],
        out_specs=out_specs,
        out_shape=out_shape,
        scratch_shapes=scratch,
        compiler_params=pltpu.CompilerParams(vmem_limit_bytes=VMEM_LIMIT),
        cost_estimate=pl.CostEstimate(
            flops=4 * keys * rows * width * count,
            bytes_accessed=4 * rows * width * count,
            transcendentals=keys * rows * width // HD * count,
        ),
        name="attend_heads",
    )(*operands)


class Places:
    def __init__(self, devices):
        self.devices = devices
        self.levels = devices // (CORES * COLUMNS)

    def split(self, index):
        if isinstance(index, int):
            return index // (CORES * COLUMNS), index // CORES % COLUMNS, index % CORES
        chip = lax.div(index, CORES)
        return lax.div(chip, COLUMNS), lax.rem(chip, COLUMNS), lax.rem(index, CORES)

    def swapped(self, array, level=0, column=0, core=0):
        pairs = []
        for index in range(self.devices):
            z, y, c = self.split(index)
            z, y, c = z ^ level, y ^ column, c ^ core
            pairs.append((index, (z * COLUMNS + y) * CORES + c))
        return lax.ppermute(array, "ctx", pairs)

    def over_levels(self, array):
        return [array] + [self.swapped(array, level=s) for s in range(1, self.levels)]


def over_chips(places, rows):
    chips = [rows, places.swapped(rows, column=1)]
    return chips + [places.swapped(one, core=1) for one in chips]


def chosen(flag, mine, got, starts, sizes):
    return jnp.where(flag, lax.dynamic_slice(mine, starts, sizes), lax.dynamic_slice(got, starts, sizes))


def halved(part, at):
    rows = part.shape[1] // 2
    return lax.dynamic_slice_in_dim(part, at * rows, rows, 1)


def for_levels(places, part):
    z, _, _ = places.split(lax.axis_index("ctx"))
    rows = part.shape[1] // places.levels
    return [
        lax.dynamic_slice_in_dim(part, (z ^ s) * rows, rows, 1).reshape(2 * rows, -1) for s in range(places.levels)
    ]


def from_owner(distance, mine, got):
    piece = mine
    for s, one in enumerate(got, 1):
        piece = jnp.where(distance == s, one, piece)
    return piece


def owned_rows(pool, owners):
    owned = (owners == lax.axis_index("ctx"))[:, None, None]
    return lax.psum(jnp.where(owned, pool[0], 0), "ctx").reshape(-1, pool.shape[-1])


def body(queries, new_keys, new_values, prefix_keys, prefix_values, pool_keys, pool_values, owners, lengths, devices):
    kv_heads = new_keys.shape[1] // HD
    blocks, block_rows = pool_keys.shape[1:3]
    length = jnp.broadcast_to(lengths[:, None], (1, HD))
    chips = devices // CORES
    levels = chips // COLUMNS
    by_permutes = (
        blocks == CORES
        and chips % COLUMNS == 0
        and levels > 1
        and levels & (levels - 1) == 0
        and block_rows % (16 * chips) == 0
        and kv_heads % 2 == 0
    )
    if not by_permutes:
        pre_k, pre_v = (lax.all_gather(rows, "ctx", axis=0, tiled=True) for rows in (prefix_keys, prefix_values))
        shared = jnp.concatenate([owned_rows(pool_keys, owners), owned_rows(pool_values, owners)])
        pieces = [(shared, shared.shape[0] // 2)]
        own = (new_keys, new_values, pre_k, pre_v)
        return attend(queries, own, pieces, length, (0, kv_heads), 0, kv_heads)
    places = Places(devices)
    z, y, c = places.split(lax.axis_index("ctx"))
    owner = jnp.where(c == 0, owners[0], owners[1])
    owner_z, owner_y, owner_c = places.split(owner)
    pools = [(pool[0], places.swapped(pool[0], core=1)) for pool in (pool_keys, pool_values)]
    count = kv_heads // 2
    part = block_rows // COLUMNS
    tied = lax.optimization_barrier

    def cut(pools, column, first):
        sizes = (1, part, count * HD)
        rows = [chosen(owner_c == c, *pool, (c, column * part, first * HD), sizes) for pool in pools]
        return jnp.concatenate(rows)

    at, sizes = (c, (1 - y) * part, 0), (1, part, count * HD)
    mine = [lax.dynamic_slice(pool, at, sizes) for pool, _ in pools]
    mine, pools = tied((mine, pools))
    rows = [jnp.where(owner_c == c, one, lax.dynamic_slice(got, at, sizes)) for one, (_, got) in zip(mine, pools)]
    sent = [jnp.concatenate(rows)]
    sent[0], pools, prefix = tied((sent[0], pools, (prefix_keys, prefix_values)))
    prefix = jnp.concatenate(prefix)
    sent.append(cut(pools, 1 - y, count))
    prefix, sent[1] = tied((prefix, sent[1]))
    got = [places.swapped(one, column=1) for one in sent]
    step = 1
    while step < levels:
        prefix = [prefix, places.swapped(prefix, level=step)]
        step *= 2
        prefix = jnp.concatenate(prefix) if step < levels else prefix

    def over_z(cuts):
        return [places.swapped(one, level=s) for s, one in enumerate(cuts) if s]

    first_cuts = for_levels(places, jnp.where(owner_y == y, cut(pools, y, 0), got[0]))
    first_got = over_z(first_cuts)
    *low, high = [1 << k for k in range(levels.bit_length() - 1)]
    last = jnp.where(owner_y == y, cut(pools, y, count), got[1])
    for distance in low:
        bit = (z // distance) & 1
        swap = places.swapped(halved(last, 1 - bit), level=distance)
        last = jnp.where((owner_z ^ z) & distance == 0, halved(last, bit), swap)
    prefix, first_got[0] = tied((prefix, first_got[0]))
    prefix = jnp.concatenate(prefix)
    prefix = [prefix, places.swapped(prefix, column=1)]
    piece = from_owner(z ^ owner_z, first_cuts[0], first_got)
    early = places.swapped(piece, column=1)
    prefix, early = tied((prefix, early))
    last = jnp.where((owner_z ^ z) & high == 0, last, places.swapped(last, level=high))
    early, last = tied((early, last))
    gathered = places.over_levels(piece)
    last_half = last.shape[1]
    last_rows = [last.reshape(-1, last.shape[-1])]
    last_early = places.swapped(last_rows[0], column=1)
    for distance in reversed(low):
        last_rows.append(places.swapped(jnp.concatenate(last_rows), level=distance))
    across = places.swapped(jnp.concatenate(gathered[1:]), column=1)
    prefix, early, gathered[0] = tied((prefix, early, gathered[0]))
    last_across = places.swapped(jnp.concatenate(last_rows[1:]), column=1)
    mine = jnp.concatenate(gathered + [early])
    last_mine = jnp.concatenate(last_rows + [last_early])
    prefix = jnp.concatenate(prefix)
    prefix = jnp.concatenate([prefix, places.swapped(prefix, core=1)])
    prefix = prefix.reshape(devices, 2, -1, prefix.shape[-1])
    own = (new_keys, new_values) + tuple(prefix[:, i].reshape(-1, prefix.shape[-1]) for i in range(2))

    def arrived(half, *rows):
        return [(one, half) for one in rows + tuple(places.swapped(one, core=1) for one in rows)]

    first = arrived(piece.shape[0] // 2, mine, across)
    blocks = attend(queries, own, first, length, (0, count - 1), 0, kv_heads, None)
    last_across, blocks, turn = tied((last_across, blocks, length))
    last = arrived(last_half, last_mine, last_across)
    earlier = [(0, count - 1, blocks)]
    earlier.append((count - 1, 1, attend(queries, own, first, turn, (count - 1, 1), 0, kv_heads, None)))
    return attend(queries, own, last, length, (count, kv_heads - count), count, kv_heads, earlier)


def solution(mesh):
    both = ("groups", "ctx")
    placed = (P(both, None),) * 5 + (P(both, None, None, None),) * 2 + (P("groups"), P(both))
    return jax.shard_map(
        functools.partial(body, devices=mesh.shape["ctx"]),
        mesh=mesh,
        in_specs=placed,
        out_specs=P(both, None),
        check_vma=False,
    )
```

```python
import functools

import jax
import jax.numpy as jnp
from jax import lax
from jax.experimental import pallas as pl
from jax.experimental.pallas import tpu as pltpu
from jax.sharding import PartitionSpec as P

HD = 128
CORES = 2
COLUMNS = 2
LOG2_E = 1.4426950408889634
VMEM_LIMIT = 24 * 1024 * 1024


def attend_kernel(scale, halves, heads, first_column, width, earlier, length_ref, queries_ref, *rest):
    own_refs, piece_refs = rest[:4], rest[4 : 4 + len(halves)]
    first, count = heads
    rows = queries_ref.shape[0]
    if earlier is None:
        blocks_ref = rest[-1]
    else:
        earlier_refs = rest[4 + len(halves) : 4 + len(halves) + len(earlier)]
        out_ref, blocks_ref, sent_sems = rest[-3:]
    group = width // HD
    length = length_ref[...]
    query_at = lax.broadcasted_iota(jnp.int32, (rows, rows), 0)
    key_at = lax.broadcasted_iota(jnp.int32, (rows, rows), 1)
    seen = (key_at <= query_at) & (key_at < length)
    live = lax.broadcasted_iota(jnp.int32, (rows, HD), 0) < length

    def copied(source, head, sem):
        target = out_ref.at[:, pl.ds(pl.multiple_of(head * width, width), width)]
        return pltpu.make_async_copy(source, target, sent_sems.at[sem])

    kept = []
    if earlier is not None:
        for ref, (at, number) in zip(earlier_refs, earlier):
            kept += [copied(ref.at[h], at + h, count + len(kept) + h) for h in range(number)]
    for copy in kept:
        copy.start()

    def one_head(h, _):
        column = pl.ds(pl.multiple_of((first + h) * HD, HD), HD)
        local = pl.ds(pl.multiple_of((first + h) * HD - first_column, HD), HD)
        shared = [ref[:, local].reshape(-1, 2, half, HD) for ref, half in zip(piece_refs, halves)]
        keys = jnp.concatenate([ref[:, column] for ref in own_refs[::2]] + [one[:, 0].reshape(-1, HD) for one in shared])
        values = [ref[:, column] for ref in own_refs[1::2]] + [one[:, 1].reshape(-1, HD) for one in shared]
        values = jnp.concatenate(values)
        turned = keys.T

        def scored(g):
            asked = queries_ref[:, pl.ds(pl.multiple_of((first + h) * width + g * HD, HD), HD)]
            return jnp.dot(asked, turned, preferred_element_type=jnp.float32)

        def weighed(scores):
            scores = jnp.concatenate([jnp.where(seen, scores[:, :rows], -1e30), scores[:, rows:]], axis=1)
            top = jnp.max(scores, axis=1, keepdims=True)
            weights = jnp.exp2((scores - top) * scale)
            return weights.astype(jnp.bfloat16), jnp.sum(weights, axis=1, keepdims=True)

        def stored(g, weights, total):
            summed = jnp.dot(weights, values, preferred_element_type=jnp.float32)
            inverse = pl.reciprocal(total, approx=True)
            inverse *= 2.0 - total * inverse
            shown = jnp.where(live, summed * inverse, 0.0)
            blocks_ref[h, :, g * HD : (g + 1) * HD] = shown.astype(jnp.bfloat16)

        scores, weights = scored(0), None
        for g in range(group):
            ahead = scored(g + 1) if g + 1 < group else None
            if weights is not None:
                stored(g - 1, *weights)
            weights = weighed(scores)
            scores = ahead
        stored(group - 1, *weights)
        if earlier is not None:
            copied(blocks_ref.at[h], first + h, h).start()
        return _

    lax.fori_loop(0, count, one_head, 0)
    if earlier is not None:
        kept += [copied(blocks_ref.at[h], first + h, h) for h in range(count)]
    for copy in kept:
        copy.wait()


def attend(queries, own, pieces, length, heads, first_column, kv_heads, earlier=()):
    rows = queries.shape[0]
    width = queries.shape[1] // kv_heads
    count = heads[1]
    halves = [half for _, half in pieces]
    arrays = [array for array, _ in pieces]
    keys = sum(array.shape[0] for array in own[::2]) + sum(array.shape[0] for array in arrays) // 2
    operands = [length, queries, *own, *arrays]
    blocks = (count, rows, width)
    if earlier is None:
        ranges, scratch = None, []
        out_specs = pl.BlockSpec(memory_space=pltpu.VMEM)
        out_shape = jax.ShapeDtypeStruct(blocks, queries.dtype)
    else:
        ranges = [one[:2] for one in earlier]
        operands += [one[2] for one in earlier]
        copies = count + sum(number for _, number in ranges)
        scratch = [pltpu.VMEM(blocks, queries.dtype), pltpu.SemaphoreType.DMA((copies,))]
        out_specs = pl.BlockSpec(memory_space=pl.ANY)
        out_shape = jax.ShapeDtypeStruct(queries.shape, queries.dtype)
    return pl.pallas_call(
        functools.partial(attend_kernel, LOG2_E / HD**0.5, halves, heads, first_column * HD, width, ranges),
        in_specs=[pl.BlockSpec(memory_space=pltpu.VMEM) for _ in operands],
        out_specs=out_specs,
        out_shape=out_shape,
        scratch_shapes=scratch,
        compiler_params=pltpu.CompilerParams(vmem_limit_bytes=VMEM_LIMIT),
        cost_estimate=pl.CostEstimate(
            flops=4 * keys * rows * width * count,
            bytes_accessed=4 * rows * width * count,
            transcendentals=keys * rows * width // HD * count,
        ),
        name="attend_heads",
    )(*operands)


class Places:
    def __init__(self, devices):
        self.devices = devices
        self.levels = devices // (CORES * COLUMNS)

    def split(self, index):
        if isinstance(index, int):
            return index // (CORES * COLUMNS), index // CORES % COLUMNS, index % CORES
        chip = lax.div(index, CORES)
        return lax.div(chip, COLUMNS), lax.rem(chip, COLUMNS), lax.rem(index, CORES)

    def swapped(self, array, level=0, column=0, core=0):
        pairs = []
        for index in range(self.devices):
            z, y, c = self.split(index)
            z, y, c = z ^ level, y ^ column, c ^ core
            pairs.append((index, (z * COLUMNS + y) * CORES + c))
        return lax.ppermute(array, "ctx", pairs)

    def over_levels(self, array):
        return [array] + [self.swapped(array, level=s) for s in range(1, self.levels)]


def over_chips(places, rows):
    chips = [rows, places.swapped(rows, column=1)]
    return chips + [places.swapped(one, core=1) for one in chips]


def chosen(flag, mine, got, starts, sizes):
    return jnp.where(flag, lax.dynamic_slice(mine, starts, sizes), lax.dynamic_slice(got, starts, sizes))


def halved(part, at):
    rows = part.shape[1] // 2
    return lax.dynamic_slice_in_dim(part, at * rows, rows, 1)


def for_levels(places, part):
    z, _, _ = places.split(lax.axis_index("ctx"))
    rows = part.shape[1] // places.levels
    return [
        lax.dynamic_slice_in_dim(part, (z ^ s) * rows, rows, 1).reshape(2 * rows, -1) for s in range(places.levels)
    ]


def from_owner(distance, mine, got):
    piece = mine
    for s, one in enumerate(got, 1):
        piece = jnp.where(distance == s, one, piece)
    return piece


def owned_rows(pool, owners):
    owned = (owners == lax.axis_index("ctx"))[:, None, None]
    return lax.psum(jnp.where(owned, pool[0], 0), "ctx").reshape(-1, pool.shape[-1])


def body(queries, new_keys, new_values, prefix_keys, prefix_values, pool_keys, pool_values, owners, lengths, devices):
    kv_heads = new_keys.shape[1] // HD
    blocks, block_rows = pool_keys.shape[1:3]
    length = jnp.broadcast_to(lengths[:, None], (1, HD))
    chips = devices // CORES
    levels = chips // COLUMNS
    by_permutes = (
        blocks == CORES
        and chips % COLUMNS == 0
        and levels > 1
        and levels & (levels - 1) == 0
        and block_rows % (16 * chips) == 0
        and kv_heads % 2 == 0
    )
    if not by_permutes:
        pre_k, pre_v = (lax.all_gather(rows, "ctx", axis=0, tiled=True) for rows in (prefix_keys, prefix_values))
        shared = jnp.concatenate([owned_rows(pool_keys, owners), owned_rows(pool_values, owners)])
        pieces = [(shared, shared.shape[0] // 2)]
        own = (new_keys, new_values, pre_k, pre_v)
        return attend(queries, own, pieces, length, (0, kv_heads), 0, kv_heads)
    places = Places(devices)
    z, y, c = places.split(lax.axis_index("ctx"))
    owner = jnp.where(c == 0, owners[0], owners[1])
    owner_z, owner_y, owner_c = places.split(owner)
    pools = [(pool[0], places.swapped(pool[0], core=1)) for pool in (pool_keys, pool_values)]
    count = kv_heads // 2
    part = block_rows // COLUMNS
    tied = lax.optimization_barrier

    def cut(pools, column, first):
        sizes = (1, part, count * HD)
        rows = [chosen(owner_c == c, *pool, (c, column * part, first * HD), sizes) for pool in pools]
        return jnp.concatenate(rows)

    at, sizes = (c, (1 - y) * part, 0), (1, part, count * HD)
    mine = [lax.dynamic_slice(pool, at, sizes) for pool, _ in pools]
    mine, pools = tied((mine, pools))
    rows = [jnp.where(owner_c == c, one, lax.dynamic_slice(got, at, sizes)) for one, (_, got) in zip(mine, pools)]
    sent = [jnp.concatenate(rows)]
    sent[0], pools, prefix = tied((sent[0], pools, (prefix_keys, prefix_values)))
    prefix = jnp.concatenate(prefix)
    sent.append(cut(pools, 1 - y, count))
    prefix, sent[1] = tied((prefix, sent[1]))
    got = [places.swapped(one, column=1) for one in sent]
    step = 1
    while step < levels:
        prefix = [prefix, places.swapped(prefix, level=step)]
        step *= 2
        prefix = jnp.concatenate(prefix) if step < levels else prefix

    def over_z(cuts):
        return [places.swapped(one, level=s) for s, one in enumerate(cuts) if s]

    first_cuts = for_levels(places, jnp.where(owner_y == y, cut(pools, y, 0), got[0]))
    first_got = over_z(first_cuts)
    *low, high = [1 << k for k in range(levels.bit_length() - 1)]
    last = jnp.where(owner_y == y, cut(pools, y, count), got[1])
    for distance in low:
        bit = (z // distance) & 1
        swap = places.swapped(halved(last, 1 - bit), level=distance)
        last = jnp.where((owner_z ^ z) & distance == 0, halved(last, bit), swap)
    prefix, first_got[0] = tied((prefix, first_got[0]))
    prefix = jnp.concatenate(prefix)
    prefix = [prefix, places.swapped(prefix, column=1)]
    piece = from_owner(z ^ owner_z, first_cuts[0], first_got)
    early = places.swapped(piece, column=1)
    prefix, early = tied((prefix, early))
    last = jnp.where((owner_z ^ z) & high == 0, last, places.swapped(last, level=high))
    early, last = tied((early, last))
    gathered = places.over_levels(piece)
    last_half = last.shape[1]
    last_rows = [last.reshape(-1, last.shape[-1])]
    for distance in reversed(low):
        last_rows.append(places.swapped(jnp.concatenate(last_rows), level=distance))
    last_rows[0], gathered[0] = tied((last_rows[0], gathered[0]))
    last_early = places.swapped(last_rows[0], column=1)
    across = places.swapped(jnp.concatenate(gathered[1:]), column=1)
    prefix, early, gathered[0] = tied((prefix, early, gathered[0]))
    prefix = jnp.concatenate(prefix)
    prefix = jnp.concatenate([prefix, places.swapped(prefix, core=1)])
    prefix, last_rows[1] = tied((prefix, last_rows[1]))
    last_across = places.swapped(jnp.concatenate(last_rows[1:]), column=1)
    mine = jnp.concatenate(gathered + [early])
    last_mine = jnp.concatenate(last_rows)
    prefix = prefix.reshape(devices, 2, -1, prefix.shape[-1])
    own = (new_keys, new_values) + tuple(prefix[:, i].reshape(-1, prefix.shape[-1]) for i in range(2))

    def arrived(half, *rows):
        return [(one, half) for one in rows + tuple(places.swapped(one, core=1) for one in rows)]

    first = arrived(piece.shape[0] // 2, mine, across)
    blocks = attend(queries, own, first, length, (0, count - 1), 0, kv_heads, None)
    last_across, blocks, turn = tied((last_across, blocks, length))
    last = arrived(last_half, last_mine, jnp.concatenate([last_early, last_across]))
    earlier = [(0, count - 1, blocks)]
    earlier.append((count - 1, 1, attend(queries, own, first, turn, (count - 1, 1), 0, kv_heads, None)))
    return attend(queries, own, last, length, (count, kv_heads - count), count, kv_heads, earlier)


def solution(mesh):
    both = ("groups", "ctx")
    placed = (P(both, None),) * 5 + (P(both, None, None, None),) * 2 + (P("groups"), P(both))
    return jax.shard_map(
        functools.partial(body, devices=mesh.shape["ctx"]),
        mesh=mesh,
        in_specs=placed,
        out_specs=P(both, None),
        check_vma=False,
    )
```

```python
import functools

import jax
import jax.numpy as jnp
from jax import lax
from jax.experimental import pallas as pl
from jax.experimental.pallas import tpu as pltpu
from jax.sharding import PartitionSpec as P

HD = 128
CORES = 2
COLUMNS = 2
LOG2_E = 1.4426950408889634
VMEM_LIMIT = 24 * 1024 * 1024


def attend_kernel(scale, halves, heads, first_column, width, earlier, length_ref, queries_ref, *rest):
    own_refs, piece_refs = rest[:4], rest[4 : 4 + len(halves)]
    first, count = heads
    rows = queries_ref.shape[0]
    if earlier is None:
        blocks_ref = rest[-1]
    else:
        earlier_refs = rest[4 + len(halves) : 4 + len(halves) + len(earlier)]
        out_ref, blocks_ref, sent_sems = rest[-3:]
    group = width // HD
    length = length_ref[...]
    query_at = lax.broadcasted_iota(jnp.int32, (rows, rows), 0)
    key_at = lax.broadcasted_iota(jnp.int32, (rows, rows), 1)
    seen = (key_at <= query_at) & (key_at < length)
    live = lax.broadcasted_iota(jnp.int32, (rows, HD), 0) < length

    def copied(source, head, sem):
        target = out_ref.at[:, pl.ds(pl.multiple_of(head * width, width), width)]
        return pltpu.make_async_copy(source, target, sent_sems.at[sem])

    kept = []
    if earlier is not None:
        for ref, (at, number) in zip(earlier_refs, earlier):
            kept += [copied(ref.at[h], at + h, count + len(kept) + h) for h in range(number)]
    for copy in kept:
        copy.start()

    def one_head(h, _):
        column = pl.ds(pl.multiple_of((first + h) * HD, HD), HD)
        local = pl.ds(pl.multiple_of((first + h) * HD - first_column, HD), HD)
        shared = [ref[:, local].reshape(-1, 2, half, HD) for ref, half in zip(piece_refs, halves)]
        keys = jnp.concatenate([ref[:, column] for ref in own_refs[::2]] + [one[:, 0].reshape(-1, HD) for one in shared])
        values = [ref[:, column] for ref in own_refs[1::2]] + [one[:, 1].reshape(-1, HD) for one in shared]
        values = jnp.concatenate(values)
        turned = keys.T

        def scored(g):
            asked = queries_ref[:, pl.ds(pl.multiple_of((first + h) * width + g * HD, HD), HD)]
            return jnp.dot(asked, turned, preferred_element_type=jnp.float32)

        def weighed(scores):
            scores = jnp.concatenate([jnp.where(seen, scores[:, :rows], -1e30), scores[:, rows:]], axis=1)
            top = jnp.max(scores, axis=1, keepdims=True)
            weights = jnp.exp2((scores - top) * scale)
            return weights.astype(jnp.bfloat16), jnp.sum(weights, axis=1, keepdims=True)

        def stored(g, weights, total):
            summed = jnp.dot(weights, values, preferred_element_type=jnp.float32)
            inverse = pl.reciprocal(total, approx=True)
            inverse *= 2.0 - total * inverse
            shown = jnp.where(live, summed * inverse, 0.0)
            blocks_ref[h, :, g * HD : (g + 1) * HD] = shown.astype(jnp.bfloat16)

        scores, weights = scored(0), None
        for g in range(group):
            ahead = scored(g + 1) if g + 1 < group else None
            if weights is not None:
                stored(g - 1, *weights)
            weights = weighed(scores)
            scores = ahead
        stored(group - 1, *weights)
        if earlier is not None:
            copied(blocks_ref.at[h], first + h, h).start()
        return _

    lax.fori_loop(0, count, one_head, 0)
    if earlier is not None:
        kept += [copied(blocks_ref.at[h], first + h, h) for h in range(count)]
    for copy in kept:
        copy.wait()


def attend(queries, own, pieces, length, heads, first_column, kv_heads, earlier=()):
    rows = queries.shape[0]
    width = queries.shape[1] // kv_heads
    count = heads[1]
    halves = [half for _, half in pieces]
    arrays = [array for array, _ in pieces]
    keys = sum(array.shape[0] for array in own[::2]) + sum(array.shape[0] for array in arrays) // 2
    operands = [length, queries, *own, *arrays]
    blocks = (count, rows, width)
    if earlier is None:
        ranges, scratch = None, []
        out_specs = pl.BlockSpec(memory_space=pltpu.VMEM)
        out_shape = jax.ShapeDtypeStruct(blocks, queries.dtype)
    else:
        ranges = [one[:2] for one in earlier]
        operands += [one[2] for one in earlier]
        copies = count + sum(number for _, number in ranges)
        scratch = [pltpu.VMEM(blocks, queries.dtype), pltpu.SemaphoreType.DMA((copies,))]
        out_specs = pl.BlockSpec(memory_space=pl.ANY)
        out_shape = jax.ShapeDtypeStruct(queries.shape, queries.dtype)
    return pl.pallas_call(
        functools.partial(attend_kernel, LOG2_E / HD**0.5, halves, heads, first_column * HD, width, ranges),
        in_specs=[pl.BlockSpec(memory_space=pltpu.VMEM) for _ in operands],
        out_specs=out_specs,
        out_shape=out_shape,
        scratch_shapes=scratch,
        compiler_params=pltpu.CompilerParams(vmem_limit_bytes=VMEM_LIMIT),
        cost_estimate=pl.CostEstimate(
            flops=4 * keys * rows * width * count,
            bytes_accessed=4 * rows * width * count,
            transcendentals=keys * rows * width // HD * count,
        ),
        name="attend_heads",
    )(*operands)


class Places:
    def __init__(self, devices):
        self.devices = devices
        self.levels = devices // (CORES * COLUMNS)

    def split(self, index):
        if isinstance(index, int):
            return index // (CORES * COLUMNS), index // CORES % COLUMNS, index % CORES
        chip = lax.div(index, CORES)
        return lax.div(chip, COLUMNS), lax.rem(chip, COLUMNS), lax.rem(index, CORES)

    def swapped(self, array, level=0, column=0, core=0):
        pairs = []
        for index in range(self.devices):
            z, y, c = self.split(index)
            z, y, c = z ^ level, y ^ column, c ^ core
            pairs.append((index, (z * COLUMNS + y) * CORES + c))
        return lax.ppermute(array, "ctx", pairs)

    def over_levels(self, array):
        return [array] + [self.swapped(array, level=s) for s in range(1, self.levels)]


def over_chips(places, rows):
    chips = [rows, places.swapped(rows, column=1)]
    return chips + [places.swapped(one, core=1) for one in chips]


def chosen(flag, mine, got, starts, sizes):
    return jnp.where(flag, lax.dynamic_slice(mine, starts, sizes), lax.dynamic_slice(got, starts, sizes))


def halved(part, at):
    rows = part.shape[1] // 2
    return lax.dynamic_slice_in_dim(part, at * rows, rows, 1)


def for_levels(places, part):
    z, _, _ = places.split(lax.axis_index("ctx"))
    rows = part.shape[1] // places.levels
    return [
        lax.dynamic_slice_in_dim(part, (z ^ s) * rows, rows, 1).reshape(2 * rows, -1) for s in range(places.levels)
    ]


def from_owner(distance, mine, got):
    piece = mine
    for s, one in enumerate(got, 1):
        piece = jnp.where(distance == s, one, piece)
    return piece


def owned_rows(pool, owners):
    owned = (owners == lax.axis_index("ctx"))[:, None, None]
    return lax.psum(jnp.where(owned, pool[0], 0), "ctx").reshape(-1, pool.shape[-1])


def body(queries, new_keys, new_values, prefix_keys, prefix_values, pool_keys, pool_values, owners, lengths, devices):
    kv_heads = new_keys.shape[1] // HD
    blocks, block_rows = pool_keys.shape[1:3]
    length = jnp.broadcast_to(lengths[:, None], (1, HD))
    chips = devices // CORES
    levels = chips // COLUMNS
    by_permutes = (
        blocks == CORES
        and chips % COLUMNS == 0
        and levels > 1
        and levels & (levels - 1) == 0
        and block_rows % (16 * chips) == 0
        and kv_heads % 2 == 0
    )
    if not by_permutes:
        pre_k, pre_v = (lax.all_gather(rows, "ctx", axis=0, tiled=True) for rows in (prefix_keys, prefix_values))
        shared = jnp.concatenate([owned_rows(pool_keys, owners), owned_rows(pool_values, owners)])
        pieces = [(shared, shared.shape[0] // 2)]
        own = (new_keys, new_values, pre_k, pre_v)
        return attend(queries, own, pieces, length, (0, kv_heads), 0, kv_heads)
    places = Places(devices)
    z, y, c = places.split(lax.axis_index("ctx"))
    owner = jnp.where(c == 0, owners[0], owners[1])
    owner_z, owner_y, owner_c = places.split(owner)
    pools = [(pool[0], places.swapped(pool[0], core=1)) for pool in (pool_keys, pool_values)]
    count = kv_heads // 2
    part = block_rows // COLUMNS
    tied = lax.optimization_barrier

    def cut(pools, column, first):
        sizes = (1, part, count * HD)
        rows = [chosen(owner_c == c, *pool, (c, column * part, first * HD), sizes) for pool in pools]
        return jnp.concatenate(rows)

    at, sizes = (c, (1 - y) * part, 0), (1, part, count * HD)
    mine = [lax.dynamic_slice(pool, at, sizes) for pool, _ in pools]
    mine, pools = tied((mine, pools))
    rows = [jnp.where(owner_c == c, one, lax.dynamic_slice(got, at, sizes)) for one, (_, got) in zip(mine, pools)]
    sent = [jnp.concatenate(rows)]
    sent[0], pools, prefix = tied((sent[0], pools, (prefix_keys, prefix_values)))
    prefix = jnp.concatenate(prefix)
    sent.append(cut(pools, 1 - y, count))
    prefix, sent[1] = tied((prefix, sent[1]))
    got = [places.swapped(one, column=1) for one in sent]
    step = 1
    while step < levels:
        prefix = [prefix, places.swapped(prefix, level=step)]
        step *= 2
        prefix = jnp.concatenate(prefix) if step < levels else prefix

    def over_z(cuts):
        return [places.swapped(one, level=s) for s, one in enumerate(cuts) if s]

    first_cuts = for_levels(places, jnp.where(owner_y == y, cut(pools, y, 0), got[0]))
    first_got = over_z(first_cuts)
    *low, high = [1 << k for k in range(levels.bit_length() - 1)]
    last = jnp.where(owner_y == y, cut(pools, y, count), got[1])
    for distance in low:
        bit = (z // distance) & 1
        swap = places.swapped(halved(last, 1 - bit), level=distance)
        last = jnp.where((owner_z ^ z) & distance == 0, halved(last, bit), swap)
    prefix, first_got[0] = tied((prefix, first_got[0]))
    piece = from_owner(z ^ owner_z, first_cuts[0], first_got)
    early = places.swapped(piece, column=1)
    last = jnp.where((owner_z ^ z) & high == 0, last, places.swapped(last, level=high))
    early, last = tied((early, last))
    gathered = places.over_levels(piece)
    prefix, gathered[-1] = tied((prefix, gathered[-1]))
    prefix = jnp.concatenate(prefix)
    prefix = [prefix, places.swapped(prefix, column=1)]
    last_half = last.shape[1]
    last_rows = [last.reshape(-1, last.shape[-1])]
    for distance in reversed(low):
        last_rows.append(places.swapped(jnp.concatenate(last_rows), level=distance))
    last_rows[0], gathered[0] = tied((last_rows[0], gathered[0]))
    last_early = places.swapped(last_rows[0], column=1)
    across = places.swapped(jnp.concatenate(gathered[1:]), column=1)
    prefix, early, gathered[0] = tied((prefix, early, gathered[0]))
    prefix = jnp.concatenate(prefix)
    prefix = jnp.concatenate([prefix, places.swapped(prefix, core=1)])
    prefix, last_rows[1] = tied((prefix, last_rows[1]))
    last_across = places.swapped(jnp.concatenate(last_rows[1:]), column=1)
    mine = jnp.concatenate(gathered + [early])
    last_mine = jnp.concatenate(last_rows)
    prefix = prefix.reshape(devices, 2, -1, prefix.shape[-1])
    own = (new_keys, new_values) + tuple(prefix[:, i].reshape(-1, prefix.shape[-1]) for i in range(2))

    def arrived(half, *rows):
        return [(one, half) for one in rows + tuple(places.swapped(one, core=1) for one in rows)]

    first = arrived(piece.shape[0] // 2, mine, across)
    blocks = attend(queries, own, first, length, (0, count - 1), 0, kv_heads, None)
    last_across, blocks, turn = tied((last_across, blocks, length))
    last = arrived(last_half, last_mine, jnp.concatenate([last_early, last_across]))
    earlier = [(0, count - 1, blocks)]
    earlier.append((count - 1, 1, attend(queries, own, first, turn, (count - 1, 1), 0, kv_heads, None)))
    return attend(queries, own, last, length, (count, kv_heads - count), count, kv_heads, earlier)


def solution(mesh):
    both = ("groups", "ctx")
    placed = (P(both, None),) * 5 + (P(both, None, None, None),) * 2 + (P("groups"), P(both))
    return jax.shard_map(
        functools.partial(body, devices=mesh.shape["ctx"]),
        mesh=mesh,
        in_specs=placed,
        out_specs=P(both, None),
        check_vma=False,
    )
```

```python
import functools

import jax
import jax.numpy as jnp
from jax import lax
from jax.experimental import pallas as pl
from jax.experimental.pallas import tpu as pltpu
from jax.sharding import PartitionSpec as P

HD = 128
CORES = 2
COLUMNS = 2
LOG2_E = 1.4426950408889634
VMEM_LIMIT = 24 * 1024 * 1024


def attend_kernel(scale, halves, heads, first_column, width, earlier, length_ref, queries_ref, *rest):
    own_refs, piece_refs = rest[:4], rest[4 : 4 + len(halves)]
    first, count = heads
    rows = queries_ref.shape[0]
    if earlier is None:
        blocks_ref = rest[-1]
    else:
        earlier_refs = rest[4 + len(halves) : 4 + len(halves) + len(earlier)]
        out_ref, blocks_ref, sent_sems = rest[-3:]
    group = width // HD
    length = length_ref[...]
    query_at = lax.broadcasted_iota(jnp.int32, (rows, rows), 0)
    key_at = lax.broadcasted_iota(jnp.int32, (rows, rows), 1)
    seen = (key_at <= query_at) & (key_at < length)
    live = lax.broadcasted_iota(jnp.int32, (rows, HD), 0) < length

    def copied(source, head, sem):
        target = out_ref.at[:, pl.ds(pl.multiple_of(head * width, width), width)]
        return pltpu.make_async_copy(source, target, sent_sems.at[sem])

    kept = []
    if earlier is not None:
        for ref, (at, number) in zip(earlier_refs, earlier):
            kept += [copied(ref.at[h], at + h, count + len(kept) + h) for h in range(number)]
    for copy in kept:
        copy.start()

    def one_head(h, _):
        column = pl.ds(pl.multiple_of((first + h) * HD, HD), HD)
        local = pl.ds(pl.multiple_of((first + h) * HD - first_column, HD), HD)
        shared = [ref[:, local].reshape(-1, 2, half, HD) for ref, half in zip(piece_refs, halves)]
        keys = jnp.concatenate([ref[:, column] for ref in own_refs[::2]] + [one[:, 0].reshape(-1, HD) for one in shared])
        values = [ref[:, column] for ref in own_refs[1::2]] + [one[:, 1].reshape(-1, HD) for one in shared]
        values = jnp.concatenate(values)
        turned = keys.T

        def scored(g):
            asked = queries_ref[:, pl.ds(pl.multiple_of((first + h) * width + g * HD, HD), HD)]
            return jnp.dot(asked, turned, preferred_element_type=jnp.float32)

        def weighed(scores):
            scores = jnp.concatenate([jnp.where(seen, scores[:, :rows], -1e30), scores[:, rows:]], axis=1)
            top = jnp.max(scores, axis=1, keepdims=True)
            weights = jnp.exp2((scores - top) * scale)
            return weights.astype(jnp.bfloat16), jnp.sum(weights, axis=1, keepdims=True)

        def stored(g, weights, total):
            summed = jnp.dot(weights, values, preferred_element_type=jnp.float32)
            inverse = pl.reciprocal(total, approx=True)
            inverse *= 2.0 - total * inverse
            shown = jnp.where(live, summed * inverse, 0.0)
            blocks_ref[h, :, g * HD : (g + 1) * HD] = shown.astype(jnp.bfloat16)

        scores, weights = scored(0), None
        for g in range(group):
            ahead = scored(g + 1) if g + 1 < group else None
            if weights is not None:
                stored(g - 1, *weights)
            weights = weighed(scores)
            scores = ahead
        stored(group - 1, *weights)
        if earlier is not None:
            copied(blocks_ref.at[h], first + h, h).start()
        return _

    lax.fori_loop(0, count, one_head, 0, unroll=True)
    if earlier is not None:
        kept += [copied(blocks_ref.at[h], first + h, h) for h in range(count)]
    for copy in kept:
        copy.wait()


def attend(queries, own, pieces, length, heads, first_column, kv_heads, earlier=()):
    rows = queries.shape[0]
    width = queries.shape[1] // kv_heads
    count = heads[1]
    halves = [half for _, half in pieces]
    arrays = [array for array, _ in pieces]
    keys = sum(array.shape[0] for array in own[::2]) + sum(array.shape[0] for array in arrays) // 2
    operands = [length, queries, *own, *arrays]
    blocks = (count, rows, width)
    if earlier is None:
        ranges, scratch = None, []
        out_specs = pl.BlockSpec(memory_space=pltpu.VMEM)
        out_shape = jax.ShapeDtypeStruct(blocks, queries.dtype)
    else:
        ranges = [one[:2] for one in earlier]
        operands += [one[2] for one in earlier]
        copies = count + sum(number for _, number in ranges)
        scratch = [pltpu.VMEM(blocks, queries.dtype), pltpu.SemaphoreType.DMA((copies,))]
        out_specs = pl.BlockSpec(memory_space=pl.ANY)
        out_shape = jax.ShapeDtypeStruct(queries.shape, queries.dtype)
    return pl.pallas_call(
        functools.partial(attend_kernel, LOG2_E / HD**0.5, halves, heads, first_column * HD, width, ranges),
        in_specs=[pl.BlockSpec(memory_space=pltpu.VMEM) for _ in operands],
        out_specs=out_specs,
        out_shape=out_shape,
        scratch_shapes=scratch,
        compiler_params=pltpu.CompilerParams(vmem_limit_bytes=VMEM_LIMIT),
        cost_estimate=pl.CostEstimate(
            flops=4 * keys * rows * width * count,
            bytes_accessed=4 * rows * width * count,
            transcendentals=keys * rows * width // HD * count,
        ),
        name="attend_heads",
    )(*operands)


class Places:
    def __init__(self, devices):
        self.devices = devices
        self.levels = devices // (CORES * COLUMNS)

    def split(self, index):
        if isinstance(index, int):
            return index // (CORES * COLUMNS), index // CORES % COLUMNS, index % CORES
        chip = lax.div(index, CORES)
        return lax.div(chip, COLUMNS), lax.rem(chip, COLUMNS), lax.rem(index, CORES)

    def swapped(self, array, level=0, column=0, core=0):
        pairs = []
        for index in range(self.devices):
            z, y, c = self.split(index)
            z, y, c = z ^ level, y ^ column, c ^ core
            pairs.append((index, (z * COLUMNS + y) * CORES + c))
        return lax.ppermute(array, "ctx", pairs)

    def over_levels(self, array):
        return [array] + [self.swapped(array, level=s) for s in range(1, self.levels)]


def over_chips(places, rows):
    chips = [rows, places.swapped(rows, column=1)]
    return chips + [places.swapped(one, core=1) for one in chips]


def chosen(flag, mine, got, starts, sizes):
    return jnp.where(flag, lax.dynamic_slice(mine, starts, sizes), lax.dynamic_slice(got, starts, sizes))


def halved(part, at):
    rows = part.shape[1] // 2
    return lax.dynamic_slice_in_dim(part, at * rows, rows, 1)


def for_levels(places, part):
    z, _, _ = places.split(lax.axis_index("ctx"))
    rows = part.shape[1] // places.levels
    return [
        lax.dynamic_slice_in_dim(part, (z ^ s) * rows, rows, 1).reshape(2 * rows, -1) for s in range(places.levels)
    ]


def from_owner(distance, mine, got):
    piece = mine
    for s, one in enumerate(got, 1):
        piece = jnp.where(distance == s, one, piece)
    return piece


def owned_rows(pool, owners):
    owned = (owners == lax.axis_index("ctx"))[:, None, None]
    return lax.psum(jnp.where(owned, pool[0], 0), "ctx").reshape(-1, pool.shape[-1])


def body(queries, new_keys, new_values, prefix_keys, prefix_values, pool_keys, pool_values, owners, lengths, devices):
    kv_heads = new_keys.shape[1] // HD
    blocks, block_rows = pool_keys.shape[1:3]
    length = jnp.broadcast_to(lengths[:, None], (1, HD))
    chips = devices // CORES
    levels = chips // COLUMNS
    by_permutes = (
        blocks == CORES
        and chips % COLUMNS == 0
        and levels > 1
        and levels & (levels - 1) == 0
        and block_rows % (16 * chips) == 0
        and kv_heads % 2 == 0
    )
    if not by_permutes:
        pre_k, pre_v = (lax.all_gather(rows, "ctx", axis=0, tiled=True) for rows in (prefix_keys, prefix_values))
        shared = jnp.concatenate([owned_rows(pool_keys, owners), owned_rows(pool_values, owners)])
        pieces = [(shared, shared.shape[0] // 2)]
        own = (new_keys, new_values, pre_k, pre_v)
        return attend(queries, own, pieces, length, (0, kv_heads), 0, kv_heads)
    places = Places(devices)
    z, y, c = places.split(lax.axis_index("ctx"))
    owner = jnp.where(c == 0, owners[0], owners[1])
    owner_z, owner_y, owner_c = places.split(owner)
    pools = [(pool[0], places.swapped(pool[0], core=1)) for pool in (pool_keys, pool_values)]
    count = kv_heads // 2
    part = block_rows // COLUMNS
    tied = lax.optimization_barrier

    def cut(pools, column, first):
        sizes = (1, part, count * HD)
        rows = [chosen(owner_c == c, *pool, (c, column * part, first * HD), sizes) for pool in pools]
        return jnp.concatenate(rows)

    at, sizes = (c, (1 - y) * part, 0), (1, part, count * HD)
    mine = [lax.dynamic_slice(pool, at, sizes) for pool, _ in pools]
    mine, pools = tied((mine, pools))
    rows = [jnp.where(owner_c == c, one, lax.dynamic_slice(got, at, sizes)) for one, (_, got) in zip(mine, pools)]
    sent = [jnp.concatenate(rows)]
    sent[0], pools, prefix = tied((sent[0], pools, (prefix_keys, prefix_values)))
    prefix = jnp.concatenate(prefix)
    sent.append(cut(pools, 1 - y, count))
    prefix, sent[1] = tied((prefix, sent[1]))
    got = [places.swapped(one, column=1) for one in sent]
    step = 1
    while step < levels:
        prefix = [prefix, places.swapped(prefix, level=step)]
        step *= 2
        prefix = jnp.concatenate(prefix) if step < levels else prefix

    def over_z(cuts):
        return [places.swapped(one, level=s) for s, one in enumerate(cuts) if s]

    first_cuts = for_levels(places, jnp.where(owner_y == y, cut(pools, y, 0), got[0]))
    first_got = over_z(first_cuts)
    *low, high = [1 << k for k in range(levels.bit_length() - 1)]
    last = jnp.where(owner_y == y, cut(pools, y, count), got[1])
    for distance in low:
        bit = (z // distance) & 1
        swap = places.swapped(halved(last, 1 - bit), level=distance)
        last = jnp.where((owner_z ^ z) & distance == 0, halved(last, bit), swap)
    prefix, first_got[0] = tied((prefix, first_got[0]))
    prefix = jnp.concatenate(prefix)
    prefix = [prefix, places.swapped(prefix, column=1)]
    piece = from_owner(z ^ owner_z, first_cuts[0], first_got)
    early = places.swapped(piece, column=1)
    prefix, early = tied((prefix, early))
    last = jnp.where((owner_z ^ z) & high == 0, last, places.swapped(last, level=high))
    early, last = tied((early, last))
    gathered = places.over_levels(piece)
    last_half = last.shape[1]
    last_rows = [last.reshape(-1, last.shape[-1])]
    for distance in reversed(low):
        last_rows.append(places.swapped(jnp.concatenate(last_rows), level=distance))
    last_rows[0], gathered[0] = tied((last_rows[0], gathered[0]))
    last_early = places.swapped(last_rows[0], column=1)
    across = places.swapped(jnp.concatenate(gathered[1:]), column=1)
    prefix, early, gathered[0] = tied((prefix, early, gathered[0]))
    prefix = jnp.concatenate(prefix)
    prefix = jnp.concatenate([prefix, places.swapped(prefix, core=1)])
    prefix, last_rows[1] = tied((prefix, last_rows[1]))
    last_across = places.swapped(jnp.concatenate(last_rows[1:]), column=1)
    mine = jnp.concatenate(gathered + [early])
    last_mine = jnp.concatenate(last_rows)
    prefix = prefix.reshape(devices, 2, -1, prefix.shape[-1])
    own = (new_keys, new_values) + tuple(prefix[:, i].reshape(-1, prefix.shape[-1]) for i in range(2))

    def arrived(half, *rows):
        return [(one, half) for one in rows + tuple(places.swapped(one, core=1) for one in rows)]

    first = arrived(piece.shape[0] // 2, mine, across)
    blocks = attend(queries, own, first, length, (0, count - 1), 0, kv_heads, None)
    last_across, blocks, turn = tied((last_across, blocks, length))
    last = arrived(last_half, last_mine, jnp.concatenate([last_early, last_across]))
    earlier = [(0, count - 1, blocks)]
    earlier.append((count - 1, 1, attend(queries, own, first, turn, (count - 1, 1), 0, kv_heads, None)))
    return attend(queries, own, last, length, (count, kv_heads - count), count, kv_heads, earlier)


def solution(mesh):
    both = ("groups", "ctx")
    placed = (P(both, None),) * 5 + (P(both, None, None, None),) * 2 + (P("groups"), P(both))
    return jax.shard_map(
        functools.partial(body, devices=mesh.shape["ctx"]),
        mesh=mesh,
        in_specs=placed,
        out_specs=P(both, None),
        check_vma=False,
    )
```
